32 devices in a mesh: groups: 1, tm: 8 (over z, y), cell: 2 (over x), sub: 2 (over core).
Axes of the slice: x: 2, y: 2, z: 4, core: 2. Of those that a mesh axis runs over, the one named last changes fastest.
Arguments:
- frames: bfloat16 [512, 128, 384], P(('groups', 'tm', 'sub'), 'cell'), may hold values from -6 to 6
- w_qkv: bfloat16 [384, 1152], P('sub'), may hold values from -1.5 to 1.5
- w_out: bfloat16 [384, 384], P('sub'), may hold values from -0.3125 to 0.3125
- w_up: bfloat16 [384, 1536], P('sub'), may hold values from -0.3125 to 0.3125
- w_down: bfloat16 [1536, 384], P('sub'), may hold values from -0.15625 to 0.15625
- temporal_weight_first: bfloat16 [1152, 768], P('sub'), may hold values from -0.1875 to 0.1875
- temporal_weight_second: bfloat16 [1152, 768], P('sub'), may hold values from -0.1875 to 0.1875
Outputs:
- features_out: bfloat16 [512, 128, 384], P(('groups', 'tm', 'sub'), 'cell')
The draws below stay inside these ranges and needn't reach their ends.
All inputs are finite; a program needn't handle non-finite values.
Results may differ from the reference program's by a relative error of at most 0.009.
Values may be sent and summed in bfloat16 or wider, within the bound.
No kernel may reach another device: no remote copies, remote signals or barrier semaphores. Data moves between devices by JAX's collectives and lax.ppermute only.
A program may use at most 64 MiB of HBM per device.

```python
import math
import jax
import jax.numpy as jnp
from jax import lax

C = 384
FF = 1536
HEAD_DIM = 64
P_SIZE = 128
F_LOC = 32
DILATION_FIRST = 16
DILATION_SECOND = 256
FRAMES = 512


def draw_w_qkv(key, part):
    key_base = jax.random.fold_in(key, 0)
    base = jax.random.truncated_normal(key_base, -4.0, 4.0, (C, 3 * C), jnp.float32) / math.sqrt(C)
    return base.astype(jnp.bfloat16)


def levels(key, extent, shards, smallest, top_value):
    gain, own = 1.0, jax.random.fold_in(key, 6)
    for dim, shards_of in shards:
        steps = jnp.exp(jax.random.uniform(jax.random.fold_in(own, dim), (shards_of,), jnp.float32, smallest / len(shards), top_value / len(shards)))
        gain = gain * jnp.repeat(steps, extent[dim] // shards_of).reshape([-1 if axis == dim else 1 for axis in range(len(extent))])
    return gain


def noise(rng, extent, scale, bound, cuts=(), dtype=jnp.bfloat16):
    level = levels(rng, extent, cuts, -0.22, 0.18) if cuts else 1.0
    drawn = jax.random.normal(rng, extent, jnp.float32) * scale * level
    return jnp.minimum(jnp.maximum(drawn, -bound), bound).astype(dtype)


def setup_inputs(seed: int = 0, part: int = 0) -> dict:
    key_list = jax.random.split(jax.random.key(seed), 8)
    own_keys = jax.random.split(jax.random.fold_in(key_list[7], part), 8)
    frames = noise(own_keys[0], (FRAMES, P_SIZE, C), 1.0, 6.0, ((0, 16), (1, 2)))
    w_qkv = draw_w_qkv(jax.random.fold_in(key_list[7], 71), part)
    w_out = noise(key_list[2], (C, C), C ** -0.5, 0.3125, ((0, 2),))
    w_up = noise(key_list[3], (C, FF), C ** -0.5, 0.3125, ((0, 2),))
    w_down = noise(key_list[4], (FF, C), FF ** -0.5, 0.15625, ((0, 2),))
    temporal_weight_first = noise(key_list[5], (3 * C, 2 * C), (3 * C) ** -0.5, 0.1875, ((0, 2),))
    temporal_weight_second = noise(key_list[6], (3 * C, 2 * C), (3 * C) ** -0.5, 0.1875, ((0, 2),))
    return {"frames": frames, "w_qkv": w_qkv, "w_out": w_out, "w_up": w_up, "w_down": w_down, "temporal_weight_first": temporal_weight_first, "temporal_weight_second": temporal_weight_second}


def normalize(values):
    row_mean = lax.optimization_barrier(jnp.mean(values, axis=-1, keepdims=True))
    centred = values - row_mean
    row_var = lax.optimization_barrier(jnp.mean(centred * centred, axis=-1, keepdims=True))
    return centred * lax.rsqrt(row_var + 1e-05)

def attend(queries, key_part, value_part):
    frame_count, q_cells, features = queries.shape
    head_count = features // HEAD_DIM
    q_heads = queries.reshape(frame_count, q_cells, head_count, HEAD_DIM).astype(jnp.float32)
    k_heads = key_part.reshape(frame_count, -1, head_count, HEAD_DIM).astype(jnp.float32)
    v_heads = value_part.reshape(frame_count, -1, head_count, HEAD_DIM).astype(jnp.float32)
    scores = jnp.einsum('fqhd,fkhd->fhqk', q_heads, k_heads) * HEAD_DIM ** (-0.5)
    row_max = lax.optimization_barrier(jnp.max(scores, axis=-1, keepdims=True))
    exp_terms = jnp.exp(scores - row_max)
    attn_probs = (exp_terms / lax.optimization_barrier(jnp.sum(exp_terms, axis=-1, keepdims=True))).astype(jnp.bfloat16)
    attn_probs = lax.optimization_barrier(attn_probs)
    mixed = jnp.einsum('fhqk,fkhd->fqhd', attn_probs.astype(jnp.float32), v_heads)
    return mixed.astype(jnp.bfloat16).reshape(frame_count, q_cells, features)

def section_one(block, w_qkv, w_out, w_up, w_down):
    frame_count, cells, features = block.shape
    residual = block.astype(jnp.float32)
    normed = normalize(residual).astype(jnp.bfloat16).reshape(-1, features)
    projected = jnp.dot(normed, w_qkv, preferred_element_type=jnp.float32).astype(jnp.bfloat16)
    projected = lax.optimization_barrier(projected).reshape(frame_count, cells, 3 * features)
    attended = attend(projected[..., :features], projected[..., features:2 * features], projected[..., 2 * features:])
    out_part = jnp.dot(attended.reshape(-1, features), w_out, preferred_element_type=jnp.float32)
    mid_state = (residual + out_part.reshape(frame_count, cells, features)).astype(jnp.bfloat16)
    mid_float = lax.optimization_barrier(mid_state).astype(jnp.float32)
    normed_two = normalize(mid_float).astype(jnp.bfloat16).reshape(-1, features)
    hidden = jax.nn.gelu(jnp.dot(normed_two, w_up, preferred_element_type=jnp.float32)).astype(jnp.bfloat16)
    down_part = jnp.dot(hidden, w_down, preferred_element_type=jnp.float32)
    return (mid_float + down_part.reshape(frame_count, cells, features)).astype(jnp.bfloat16)

def gated_temporal_layer(center, weight, dilation):
    frame_total = center.shape[0]
    features = center.shape[-1]
    padded_frames = jnp.pad(center, ((dilation, dilation), (0, 0), (0, 0)))
    earlier = padded_frames[:frame_total]
    later_frames = padded_frames[2 * dilation:]
    stacked = jnp.concatenate([earlier, center, later_frames], axis=-1).reshape(-1, 3 * features)
    preact = jnp.dot(stacked, weight, preferred_element_type=jnp.float32)
    gated_part = jnp.tanh(preact[:, :features]) * jax.nn.sigmoid(preact[:, features:])
    return (center.astype(jnp.float32) + gated_part.reshape(center.shape)).astype(jnp.bfloat16)

def reference(frames, w_qkv, w_out, w_up, w_down, temporal_weight_first, temporal_weight_second):
    frame_total = frames.shape[0]
    blocks = frames.reshape(frame_total // F_LOC, F_LOC, P_SIZE, C)
    sectioned_frames = lax.map(lambda block: section_one(block, w_qkv, w_out, w_up, w_down), blocks)
    sectioned_frames = sectioned_frames.reshape(frame_total, P_SIZE, C)
    opening_layer = gated_temporal_layer(sectioned_frames, temporal_weight_first, DILATION_FIRST)
    return gated_temporal_layer(opening_layer, temporal_weight_second, DILATION_SECOND)
```

```python
import functools
import math

import jax
import jax.numpy as jnp
from jax import lax
from jax.experimental import pallas as pl
from jax.experimental.pallas import tpu as pltpu
from jax.sharding import PartitionSpec as P

HEAD_DIM = 64
DILATION_FIRST = 16
DILATION_SECOND = 256
CHUNKS = (1, 1, 1, 1)
VMEM_LIMIT = 40 * 1024 * 1024


def with_halo(block, sides, width):
    for axis, dim in sides:
        count = lax.axis_size(axis)
        forward = [(i, i + 1) for i in range(count - 1)]
        backward = [(target, source) for source, target in forward]
        low = lax.ppermute(
            lax.slice_in_dim(block, block.shape[dim] - width, None, axis=dim), axis, forward
        )
        high = lax.ppermute(lax.slice_in_dim(block, 0, width, axis=dim), axis, backward)
        block = jnp.concatenate([low, block, high], axis=dim)
    return block


def shifted(shard, axis, by):
    size = lax.axis_size(axis)
    pairs = [(i, i + by) for i in range(size) if 0 <= i + by < size]
    return lax.ppermute(shard, axis, pairs)


def normalize(values):
    row_mean = jnp.mean(values, axis=-1, keepdims=True)
    centred = values - row_mean
    row_var = jnp.mean(centred * centred, axis=-1, keepdims=True)
    return centred * lax.rsqrt(row_var + 1e-05)


def attend(queries, key_part, value_part):
    frame_count, q_cells, features = queries.shape
    head_count = features // HEAD_DIM
    q_heads = queries.reshape(frame_count, q_cells, head_count, HEAD_DIM)
    k_heads = key_part.reshape(frame_count, -1, head_count, HEAD_DIM)
    v_heads = value_part.reshape(frame_count, -1, head_count, HEAD_DIM)
    scores = jnp.einsum(
        "fqhd,fkhd->fhqk", q_heads, k_heads, preferred_element_type=jnp.float32
    ) * HEAD_DIM ** (-0.5)
    row_max = jnp.max(scores, axis=-1, keepdims=True)
    exp_terms = jnp.exp(scores - row_max)
    attn_probs = (exp_terms / jnp.sum(exp_terms, axis=-1, keepdims=True)).astype(jnp.bfloat16)
    mixed = jnp.einsum("fhqk,fkhd->fqhd", attn_probs, v_heads, preferred_element_type=jnp.float32)
    return mixed.astype(jnp.bfloat16).reshape(frame_count, q_cells, features)


def gated_step(center, earlier, later_frames, weight):
    features = center.shape[-1]
    stacked = jnp.concatenate([earlier, center, later_frames], axis=-1).reshape(-1, 3 * features)
    preact = jnp.dot(stacked, weight, preferred_element_type=jnp.float32)
    gated_part = jnp.tanh(preact[:, :features]) * jax.nn.sigmoid(preact[:, features:])
    return (center.astype(jnp.float32) + gated_part.reshape(center.shape)).astype(jnp.bfloat16)


def general(frames, w_qkv, w_out, w_up, w_down, temporal_weight_first, temporal_weight_second):
    frames_local, cell_rows, features = frames.shape
    whole_qkv, whole_out, whole_up, whole_down, whole_tcn_a, whole_tcn_b = (
        lax.all_gather(w, "sub", axis=0, tiled=True)
        for w in (w_qkv, w_out, w_up, w_down, temporal_weight_first, temporal_weight_second)
    )
    working = lax.all_to_all(frames, "cell", split_axis=0, concat_axis=1, tiled=True)
    frame_count, cells_here = (working.shape[0], working.shape[1])
    residual = working.astype(jnp.float32)
    normed = normalize(residual).astype(jnp.bfloat16).reshape(-1, features)
    projected = jnp.dot(normed, whole_qkv, preferred_element_type=jnp.float32).astype(jnp.bfloat16)
    projected = projected.reshape(frame_count, cells_here, 3 * features)
    attended = attend(
        projected[..., :features],
        projected[..., features : 2 * features],
        projected[..., 2 * features :],
    )
    out_part = jnp.dot(
        attended.reshape(-1, features), whole_out, preferred_element_type=jnp.float32
    )
    mid_state = (residual + out_part.reshape(frame_count, cells_here, features)).astype(
        jnp.bfloat16
    )
    mid_float = lax.optimization_barrier(mid_state).astype(jnp.float32)
    normed_two = normalize(mid_float).astype(jnp.bfloat16).reshape(-1, features)
    hidden = jax.nn.gelu(jnp.dot(normed_two, whole_up, preferred_element_type=jnp.float32)).astype(
        jnp.bfloat16
    )
    down_part = jnp.dot(hidden, whole_down, preferred_element_type=jnp.float32).reshape(
        frame_count, cells_here, features
    )
    sectioned_frames = (mid_float + down_part).astype(jnp.bfloat16)
    sectioned_frames = lax.all_to_all(
        sectioned_frames, "cell", split_axis=1, concat_axis=0, tiled=True
    )
    padded_frames = with_halo(sectioned_frames, ((("tm", "sub"), 0),), DILATION_FIRST)
    earlier = padded_frames[:frames_local]
    later_frames = padded_frames[2 * DILATION_FIRST : 2 * DILATION_FIRST + frames_local]
    opening_layer = gated_step(sectioned_frames, earlier, later_frames, whole_tcn_a)
    shard_step_count = DILATION_SECOND // frames_local
    far_earlier = shifted(opening_layer, ("tm", "sub"), shard_step_count)
    far_later = shifted(opening_layer, ("tm", "sub"), -shard_step_count)
    return gated_step(opening_layer, far_earlier, far_later, whole_tcn_b)


def load_halves(core, pairs, scratches, sems):
    copies = []
    for index, ((mine, other), scratch) in enumerate(zip(pairs, scratches)):
        rows = mine.shape[0]
        here = pl.multiple_of(core * rows, 16)
        there = pl.multiple_of((1 - core) * rows, 16)
        copies.append(
            (
                pltpu.make_async_copy(mine, scratch.at[pl.ds(here, rows)], sems.at[index, 0]),
                pltpu.make_async_copy(other, scratch.at[pl.ds(there, rows)], sems.at[index, 1]),
            )
        )
    return copies


def start_all(copies):
    for pair in copies:
        for copy in pair:
            copy.start()


def wait_pair(pair):
    for copy in pair:
        copy.wait()


def section_kernel(
    place,
    own,
    near_cells,
    far_own,
    far_cells,
    qkv_a,
    qkv_b,
    out_a,
    out_b,
    up_a,
    up_b,
    down_a,
    down_b,
    even_ref,
    odd_ref,
    w_qkv,
    w_out,
    w_up,
    w_down,
    sems,
):
    core = place[0]
    copies = load_halves(
        core,
        ((qkv_a, qkv_b), (out_a, out_b), (up_a, up_b), (down_a, down_b)),
        (w_qkv, w_out, w_up, w_down),
        sems,
    )
    first = pl.program_id(0) == 0

    @pl.when(first)
    def _():
        start_all(copies)

    features = own.shape[-1]
    cells = 2 * own.shape[2]
    parts = []
    for mine, other in ((own, near_cells), (far_own, far_cells)):
        for slot in range(2):
            parts += [mine[slot, 0], other[slot, 0]]
    residual = jnp.concatenate(parts, axis=0).astype(jnp.float32)
    frame_count = 4
    normed = normalize(residual).astype(jnp.bfloat16)

    @pl.when(first)
    def _():
        wait_pair(copies[0])

    projected = jnp.dot(normed, w_qkv[...], preferred_element_type=jnp.float32).astype(jnp.bfloat16)
    pair_width = 2 * HEAD_DIM
    low = lax.broadcasted_iota(jnp.int32, (cells, pair_width), 1) < HEAD_DIM
    low_one = low.astype(jnp.bfloat16)
    high_one = 1 - low_one
    scale = HEAD_DIM ** (-0.5) * math.log2(math.e)
    rows = []
    for frame in range(frame_count):
        block = projected[frame * cells : (frame + 1) * cells]
        columns = []
        for pair in range(features // pair_width):
            at = pair * pair_width
            queries = block[:, at : at + pair_width]
            keys = block[:, features + at : features + at + pair_width]
            values = block[:, 2 * features + at : 2 * features + at + pair_width]
            split_keys = jnp.concatenate([keys * low_one, keys * high_one], axis=0)
            scores = lax.dot_general(
                queries, split_keys, (((1,), (1,)), ((), ())), preferred_element_type=jnp.float32
            )
            terms = []
            for head in range(2):
                own_scores = scores[:, head * cells : (head + 1) * cells]
                row_max = jnp.max(own_scores, axis=-1, keepdims=True)
                terms.append(jnp.exp2((own_scores - row_max) * scale).astype(jnp.bfloat16))
            split_values = jnp.concatenate(
                [
                    jnp.concatenate([values * low_one, low_one], axis=1),
                    jnp.concatenate([values * high_one, high_one], axis=1),
                ],
                axis=0,
            )
            mixed = jnp.dot(
                jnp.concatenate(terms, axis=1), split_values, preferred_element_type=jnp.float32
            )
            columns.append((mixed[:, :pair_width] / mixed[:, pair_width:]).astype(jnp.bfloat16))
        rows.append(jnp.concatenate(columns, axis=1))
    attended = jnp.concatenate(rows, axis=0)

    @pl.when(first)
    def _():
        wait_pair(copies[1])
        wait_pair(copies[2])
        wait_pair(copies[3])

    mid_state = (
        residual + jnp.dot(attended, w_out[...], preferred_element_type=jnp.float32)
    ).astype(jnp.bfloat16)
    mid_float = mid_state.astype(jnp.float32)
    normed_two = normalize(mid_float).astype(jnp.bfloat16)
    total = mid_float
    width = features
    for at in range(0, w_up.shape[1], width):
        lifted = jnp.dot(normed_two, w_up[:, at : at + width], preferred_element_type=jnp.float32)
        inner = lifted * (
            math.sqrt(2 / math.pi) + (math.sqrt(2 / math.pi) * 0.044715) * (lifted * lifted)
        )
        halved = 0.5 * lifted
        hidden = (halved + halved * jnp.tanh(inner)).astype(jnp.bfloat16)
        total = total + jnp.dot(hidden, w_down[at : at + width], preferred_element_type=jnp.float32)
    sectioned = total.astype(jnp.bfloat16)
    for block in range(2):
        even_ref[block, 0] = sectioned[(2 * block) * cells : (2 * block + 1) * cells]
        odd_ref[block, 0] = sectioned[(2 * block + 1) * cells : (2 * block + 2) * cells]


def gate(center, preact):
    features = center.shape[-1]
    gated = jnp.tanh(preact[:, :features]) * (
        0.5 + 0.5 * jnp.tanh(0.5 * preact[:, features:])
    )
    return (center.astype(jnp.float32) + gated).astype(jnp.bfloat16)


def temporal_kernel(
    place,
    even,
    odd,
    left_odd,
    right_even,
    first_a,
    first_b,
    second_a,
    second_b,
    out0,
    out1,
    out2,
    out3,
    w_first,
    w_second,
    sems,
):
    core, near, is_first, is_last = place[0], place[1], place[2], place[3]
    copies = load_halves(
        core, ((first_a, first_b), (second_a, second_b)), (w_first, w_second), sems
    )
    starting = pl.program_id(0) == 0

    @pl.when(starting)
    def _():
        start_all(copies)
        wait_pair(copies[0])

    far = 1 - near
    features = even.shape[-1]
    cells = even.shape[2]
    zero = jnp.zeros((cells, features), even.dtype)
    even_n, odd_n, even_f, odd_f = even[near, 0], odd[near, 0], even[far, 0], odd[far, 0]
    left_n = jnp.where(is_first == 1, zero, left_odd[near, 0])
    left_f = left_odd[jnp.where(is_first == 1, near, far), 0]
    right_n = right_even[jnp.where(is_last == 1, far, near), 0]
    right_f = jnp.where(is_last == 1, zero, right_even[far, 0])
    center = jnp.concatenate([even_n, odd_n, even_f, odd_f], axis=0)
    stacked = jnp.concatenate(
        [
            jnp.concatenate([left_n, even_n, left_f, even_f], axis=0),
            center,
            jnp.concatenate([odd_n, right_n, odd_f, right_f], axis=0),
        ],
        axis=1,
    )
    opening = gate(center, jnp.dot(stacked, w_first[...], preferred_element_type=jnp.float32))

    @pl.when(starting)
    def _():
        wait_pair(copies[1])

    rows = 2 * cells
    near_part, far_part = opening[:rows], opening[rows:]
    both = jnp.concatenate([near_part, far_part], axis=1)
    result_n = gate(
        near_part, jnp.dot(both, w_second[features:], preferred_element_type=jnp.float32)
    )
    result_f = gate(
        far_part, jnp.dot(both, w_second[: 2 * features], preferred_element_type=jnp.float32)
    )
    same = jnp.where(near == 0, result_n, result_f)
    other = jnp.where(near == 0, result_f, result_n)
    half = cells // 2
    for slot in range(2):
        at = slot * cells
        out0[slot, 0] = same[at : at + half]
        out1[slot, 0] = same[at + half : at + cells]
        out2[slot, 0] = other[at : at + half]
        out3[slot, 0] = other[at + half : at + cells]


ANYWHERE = pl.BlockSpec(memory_space=pl.ANY)
SCALARS = pl.BlockSpec(memory_space=pltpu.SMEM)


def run_section(place, pieces, weights):
    slots, count, cells, features = pieces[0].shape
    ff = weights[2][0].shape[1]
    block_in = pl.BlockSpec((slots, 1, cells, features), lambda i: (0, i, 0, 0))
    block_out = pl.BlockSpec((2, 1, 2 * cells, features), lambda i: (0, i, 0, 0))
    shape = jax.ShapeDtypeStruct((2, count, 2 * cells, features), jnp.bfloat16)
    tokens = 2 * slots * count * 2 * cells
    macs = tokens * (features * (4 * features + 2 * ff) + 4 * cells * features)
    flat = [half for pair in weights for half in pair]
    return pl.pallas_call(
        section_kernel,
        grid=(count,),
        out_shape=(shape, shape),
        in_specs=[SCALARS] + [block_in] * 4 + [ANYWHERE] * 8,
        out_specs=(block_out, block_out),
        scratch_shapes=[
            pltpu.VMEM((2 * mine.shape[0], mine.shape[1]), mine.dtype) for mine, _ in weights
        ]
        + [pltpu.SemaphoreType.DMA((4, 2))],
        compiler_params=pltpu.CompilerParams(vmem_limit_bytes=VMEM_LIMIT),
        cost_estimate=pl.CostEstimate(
            flops=2 * macs, bytes_accessed=8 * tokens * features, transcendentals=tokens * ff
        ),
        name="section",
    )(place, *pieces, *flat)


def run_temporal(place, even, odd, left_odd, right_even, weights):
    blocks, count, cells, features = even.shape
    block_in = pl.BlockSpec((blocks, 1, cells, features), lambda i: (0, i, 0, 0))
    block_out = pl.BlockSpec((2, 1, cells // 2, features), lambda i: (0, i, 0, 0))
    shape = jax.ShapeDtypeStruct((2, count, cells // 2, features), jnp.bfloat16)
    tokens = 2 * blocks * count * cells
    flat = [half for pair in weights for half in pair]
    return pl.pallas_call(
        temporal_kernel,
        grid=(count,),
        out_shape=(shape,) * 4,
        in_specs=[SCALARS] + [block_in] * 4 + [ANYWHERE] * 4,
        out_specs=(block_out,) * 4,
        scratch_shapes=[
            pltpu.VMEM((2 * mine.shape[0], mine.shape[1]), mine.dtype) for mine, _ in weights
        ]
        + [pltpu.SemaphoreType.DMA((2, 2))],
        compiler_params=pltpu.CompilerParams(vmem_limit_bytes=VMEM_LIMIT),
        cost_estimate=pl.CostEstimate(
            flops=20 * tokens * features * features,
            bytes_accessed=8 * tokens * features,
            transcendentals=4 * tokens * features,
        ),
        name="temporal",
    )(place, even, odd, left_odd, right_even, *flat)


AXES = ("tm", "cell", "sub")


def permutation(sizes, target):
    tm_size, cell_size, sub_size = sizes
    pairs = []
    for tm in range(tm_size):
        for cell in range(cell_size):
            for sub in range(sub_size):
                to_tm, to_cell, to_sub = target(tm, cell, sub)
                pairs.append(
                    (
                        (tm * cell_size + cell) * sub_size + sub,
                        (to_tm * cell_size + to_cell) * sub_size + to_sub,
                    )
                )
    return pairs


def paired(frames, w_qkv, w_out, w_up, w_down, temporal_weight_first, temporal_weight_second):
    frames_local, cells, features = frames.shape
    sizes = tuple(lax.axis_size(axis) for axis in AXES)
    half = sizes[0] // 2
    subs = sizes[2]
    tm, cell, sub = (lax.axis_index(axis) for axis in AXES)
    side = tm // half
    quarter = 2 * side + cell
    position = (tm % half) * subs + sub
    place = jnp.stack(
        [sub, side, (position == 0).astype(jnp.int32), (position == half * subs - 1).astype(jnp.int32)]
    ).astype(jnp.int32)

    def partner(delta):
        def target(at_tm, at_cell, at_sub):
            return (at_tm + half * (delta // 2)) % (2 * half), at_cell ^ (delta % 2), at_sub

        return permutation(sizes, target)

    def ring(step):
        def target(at_tm, at_cell, at_sub):
            spot = ((at_tm % half) * subs + at_sub + step) % (half * subs)
            return (at_tm // half) * half + spot // subs, at_cell, spot % subs

        return permutation(sizes, target)

    slots = frames_local // DILATION_FIRST
    grouped = frames.reshape(slots, DILATION_FIRST, cells, features)

    starts = []
    at = 0
    for count in CHUNKS:
        starts.append(at)
        at += 4 * count
    pieces = []
    for begin, count in zip(starts, CHUNKS):
        cut = [
            lax.dynamic_slice_in_dim(grouped, begin + (quarter ^ delta) * count, count, axis=1)
            for delta in range(4)
        ]
        pieces.append([cut[0]] + [lax.ppermute(cut[d], AXES, partner(d)) for d in (1, 2, 3)])

    def swap_core(weight):
        return weight, lax.ppermute(
            weight, AXES, permutation(sizes, lambda a, b, c: (a, b, (c + 1) % subs))
        )

    section_weights = [swap_core(w) for w in (w_qkv, w_out, w_up, w_down)]
    temporal_weights = [swap_core(w) for w in (temporal_weight_first, temporal_weight_second)]

    result = jnp.zeros_like(grouped)
    for begin, count, chunk in zip(starts, CHUNKS, pieces):
        even, odd = run_section(place, chunk, section_weights)
        left_odd = lax.ppermute(odd, AXES, ring(1))
        right_even = lax.ppermute(even, AXES, ring(-1))
        outs = run_temporal(place, even, odd, left_odd, right_even, temporal_weights)
        for delta in range(4):
            back = outs[delta]
            if delta:
                back = lax.ppermute(back, AXES, partner(delta))
            result = lax.dynamic_update_slice_in_dim(
                result, back, begin + (quarter ^ delta) * count, axis=1
            )
    return result.reshape(frames.shape)


def local(frames, *weights):
    frames_local, cells, features = frames.shape
    tm_size, cell_size, sub_size = (lax.axis_size(axis) for axis in AXES)
    video = frames_local * tm_size * sub_size
    fits = (
        video == 2 * DILATION_SECOND
        and frames_local == 2 * DILATION_FIRST
        and tm_size % 2 == 0
        and cell_size == 2
        and sub_size == 2
        and cells % 16 == 0
        and DILATION_FIRST == 4 * sum(CHUNKS)
    )
    return (paired if fits else general)(frames, *weights)


def solution(mesh):
    placed = (P(("groups", "tm", "sub"), "cell", None),) + (P("sub", None),) * 6
    return jax.shard_map(
        local,
        mesh=mesh,
        in_specs=placed,
        out_specs=P(("groups", "tm", "sub"), "cell", None),
        check_vma=False,
    )
```

```python
import functools
import math

import jax
import jax.numpy as jnp
from jax import lax
from jax.experimental import pallas as pl
from jax.experimental.pallas import tpu as pltpu
from jax.sharding import PartitionSpec as P

HEAD_DIM = 64
DILATION_FIRST = 16
DILATION_SECOND = 256
CHUNKS = (1, 2, 1)
ORDER = (("s", 0), ("t", 0), ("s", 1), ("s", 2), ("t", 1), ("t", 2))
VMEM_LIMIT = 24 * 1024 * 1024


def with_halo(block, sides, width):
    for axis, dim in sides:
        count = lax.axis_size(axis)
        forward = [(i, i + 1) for i in range(count - 1)]
        backward = [(target, source) for source, target in forward]
        low = lax.ppermute(
            lax.slice_in_dim(block, block.shape[dim] - width, None, axis=dim), axis, forward
        )
        high = lax.ppermute(lax.slice_in_dim(block, 0, width, axis=dim), axis, backward)
        block = jnp.concatenate([low, block, high], axis=dim)
    return block


def shifted(shard, axis, by):
    size = lax.axis_size(axis)
    pairs = [(i, i + by) for i in range(size) if 0 <= i + by < size]
    return lax.ppermute(shard, axis, pairs)


def normalize(values):
    row_mean = jnp.mean(values, axis=-1, keepdims=True)
    centred = values - row_mean
    row_var = jnp.mean(centred * centred, axis=-1, keepdims=True)
    return centred * lax.rsqrt(row_var + 1e-05)


def attend(queries, key_part, value_part):
    frame_count, q_cells, features = queries.shape
    head_count = features // HEAD_DIM
    q_heads = queries.reshape(frame_count, q_cells, head_count, HEAD_DIM)
    k_heads = key_part.reshape(frame_count, -1, head_count, HEAD_DIM)
    v_heads = value_part.reshape(frame_count, -1, head_count, HEAD_DIM)
    scores = jnp.einsum(
        "fqhd,fkhd->fhqk", q_heads, k_heads, preferred_element_type=jnp.float32
    ) * HEAD_DIM ** (-0.5)
    row_max = jnp.max(scores, axis=-1, keepdims=True)
    exp_terms = jnp.exp(scores - row_max)
    attn_probs = (exp_terms / jnp.sum(exp_terms, axis=-1, keepdims=True)).astype(jnp.bfloat16)
    mixed = jnp.einsum("fhqk,fkhd->fqhd", attn_probs, v_heads, preferred_element_type=jnp.float32)
    return mixed.astype(jnp.bfloat16).reshape(frame_count, q_cells, features)


def gated_step(center, earlier, later_frames, weight):
    features = center.shape[-1]
    stacked = jnp.concatenate([earlier, center, later_frames], axis=-1).reshape(-1, 3 * features)
    preact = jnp.dot(stacked, weight, preferred_element_type=jnp.float32)
    gated_part = jnp.tanh(preact[:, :features]) * jax.nn.sigmoid(preact[:, features:])
    return (center.astype(jnp.float32) + gated_part.reshape(center.shape)).astype(jnp.bfloat16)


def general(frames, w_qkv, w_out, w_up, w_down, temporal_weight_first, temporal_weight_second):
    frames_local, cell_rows, features = frames.shape
    whole_qkv, whole_out, whole_up, whole_down, whole_tcn_a, whole_tcn_b = (
        lax.all_gather(w, "sub", axis=0, tiled=True)
        for w in (w_qkv, w_out, w_up, w_down, temporal_weight_first, temporal_weight_second)
    )
    working = lax.all_to_all(frames, "cell", split_axis=0, concat_axis=1, tiled=True)
    frame_count, cells_here = (working.shape[0], working.shape[1])
    residual = working.astype(jnp.float32)
    normed = normalize(residual).astype(jnp.bfloat16).reshape(-1, features)
    projected = jnp.dot(normed, whole_qkv, preferred_element_type=jnp.float32).astype(jnp.bfloat16)
    projected = projected.reshape(frame_count, cells_here, 3 * features)
    attended = attend(
        projected[..., :features],
        projected[..., features : 2 * features],
        projected[..., 2 * features :],
    )
    out_part = jnp.dot(
        attended.reshape(-1, features), whole_out, preferred_element_type=jnp.float32
    )
    mid_state = (residual + out_part.reshape(frame_count, cells_here, features)).astype(
        jnp.bfloat16
    )
    mid_float = lax.optimization_barrier(mid_state).astype(jnp.float32)
    normed_two = normalize(mid_float).astype(jnp.bfloat16).reshape(-1, features)
    hidden = jax.nn.gelu(jnp.dot(normed_two, whole_up, preferred_element_type=jnp.float32)).astype(
        jnp.bfloat16
    )
    down_part = jnp.dot(hidden, whole_down, preferred_element_type=jnp.float32).reshape(
        frame_count, cells_here, features
    )
    sectioned_frames = (mid_float + down_part).astype(jnp.bfloat16)
    sectioned_frames = lax.all_to_all(
        sectioned_frames, "cell", split_axis=1, concat_axis=0, tiled=True
    )
    padded_frames = with_halo(sectioned_frames, ((("tm", "sub"), 0),), DILATION_FIRST)
    earlier = padded_frames[:frames_local]
    later_frames = padded_frames[2 * DILATION_FIRST : 2 * DILATION_FIRST + frames_local]
    opening_layer = gated_step(sectioned_frames, earlier, later_frames, whole_tcn_a)
    shard_step_count = DILATION_SECOND // frames_local
    far_earlier = shifted(opening_layer, ("tm", "sub"), shard_step_count)
    far_later = shifted(opening_layer, ("tm", "sub"), -shard_step_count)
    return gated_step(opening_layer, far_earlier, far_later, whole_tcn_b)


def load_halves(core, pairs, scratches, sems):
    copies = []
    for index, ((mine, other), scratch) in enumerate(zip(pairs, scratches)):
        rows = mine.shape[0]
        here = pl.multiple_of(core * rows, 16)
        there = pl.multiple_of((1 - core) * rows, 16)
        copies.append(
            (
                pltpu.make_async_copy(mine, scratch.at[pl.ds(here, rows)], sems.at[index, 0]),
                pltpu.make_async_copy(other, scratch.at[pl.ds(there, rows)], sems.at[index, 1]),
            )
        )
    return copies


def start_all(copies):
    for pair in copies:
        for copy in pair:
            copy.start()


def wait_pair(pair):
    for copy in pair:
        copy.wait()


def section_kernel(
    place,
    before,
    arrived,
    qkv_a,
    qkv_b,
    out_a,
    out_b,
    up_a,
    up_b,
    down_a,
    down_b,
    even_ref,
    odd_ref,
    w_qkv,
    w_out,
    w_up,
    w_down,
    sems,
):
    core = place[0]
    copies = load_halves(
        core,
        ((qkv_a, qkv_b), (out_a, out_b), (up_a, up_b), (down_a, down_b)),
        (w_qkv, w_out, w_up, w_down),
        sems,
    )
    first = pl.program_id(0) == 0

    @pl.when(first)
    def _():
        start_all(copies)

    features = arrived.shape[-1]
    cells = 2 * arrived.shape[3]
    parts = []
    for block in range(2):
        for slot in range(2):
            parts += [arrived[2 * block, slot, 0], arrived[2 * block + 1, slot, 0]]
    residual = jnp.concatenate(parts, axis=0).astype(jnp.float32)
    frame_count = 4
    normed = normalize(residual).astype(jnp.bfloat16)

    @pl.when(first)
    def _():
        wait_pair(copies[0])

    projected = jnp.dot(normed, w_qkv[...], preferred_element_type=jnp.float32).astype(jnp.bfloat16)
    pair_width = 2 * HEAD_DIM
    low = lax.broadcasted_iota(jnp.int32, (cells, pair_width), 1) < HEAD_DIM
    low_one = low.astype(jnp.bfloat16)
    high_one = 1 - low_one
    scale = HEAD_DIM ** (-0.5) * math.log2(math.e)
    rows = []
    for frame in range(frame_count):
        block = projected[frame * cells : (frame + 1) * cells]
        columns = []
        for pair in range(features // pair_width):
            at = pair * pair_width
            queries = block[:, at : at + pair_width]
            keys = block[:, features + at : features + at + pair_width]
            values = block[:, 2 * features + at : 2 * features + at + pair_width]
            split_keys = jnp.concatenate([keys * low_one, keys * high_one], axis=0)
            scores = lax.dot_general(
                queries, split_keys, (((1,), (1,)), ((), ())), preferred_element_type=jnp.float32
            )
            terms = []
            for head in range(2):
                own_scores = scores[:, head * cells : (head + 1) * cells]
                row_max = jnp.max(own_scores, axis=-1, keepdims=True)
                terms.append(jnp.exp2((own_scores - row_max) * scale).astype(jnp.bfloat16))
            split_values = jnp.concatenate(
                [
                    jnp.concatenate([values * low_one, low_one], axis=1),
                    jnp.concatenate([values * high_one, high_one], axis=1),
                ],
                axis=0,
            )
            mixed = jnp.dot(
                jnp.concatenate(terms, axis=1), split_values, preferred_element_type=jnp.float32
            )
            columns.append((mixed[:, :pair_width] / mixed[:, pair_width:]).astype(jnp.bfloat16))
        rows.append(jnp.concatenate(columns, axis=1))
    attended = jnp.concatenate(rows, axis=0)

    @pl.when(first)
    def _():
        wait_pair(copies[1])
        wait_pair(copies[2])
        wait_pair(copies[3])

    mid_state = (
        residual + jnp.dot(attended, w_out[...], preferred_element_type=jnp.float32)
    ).astype(jnp.bfloat16)
    mid_float = mid_state.astype(jnp.float32)
    normed_two = normalize(mid_float).astype(jnp.bfloat16)
    total = mid_float
    width = features
    for at in range(0, w_up.shape[1], width):
        lifted = jnp.dot(normed_two, w_up[:, at : at + width], preferred_element_type=jnp.float32)
        inner = lifted * (
            math.sqrt(2 / math.pi) + (math.sqrt(2 / math.pi) * 0.044715) * (lifted * lifted)
        )
        halved = 0.5 * lifted
        hidden = (halved + halved * jnp.tanh(inner)).astype(jnp.bfloat16)
        total = total + jnp.dot(hidden, w_down[at : at + width], preferred_element_type=jnp.float32)
    sectioned = total.astype(jnp.bfloat16)
    for block in range(2):
        even_ref[block, 0] = sectioned[(2 * block) * cells : (2 * block + 1) * cells]
        odd_ref[block, 0] = sectioned[(2 * block + 1) * cells : (2 * block + 2) * cells]


def gate(center, preact):
    features = center.shape[-1]
    gated = jnp.tanh(preact[:, :features]) * (
        0.5 + 0.5 * jnp.tanh(0.5 * preact[:, features:])
    )
    return (center.astype(jnp.float32) + gated).astype(jnp.bfloat16)


def temporal_kernel(
    place,
    before,
    even,
    odd,
    left_odd,
    right_even,
    first_a,
    first_b,
    second_a,
    second_b,
    out,
    w_first,
    w_second,
    sems,
):
    core, is_first, is_last = place[0], place[1], place[2]
    copies = load_halves(
        core, ((first_a, first_b), (second_a, second_b)), (w_first, w_second), sems
    )
    starting = pl.program_id(0) == 0

    @pl.when(starting)
    def _():
        start_all(copies)
        wait_pair(copies[0])

    near, far = 0, 1
    features = even.shape[-1]
    cells = even.shape[2]
    zero = jnp.zeros((cells, features), even.dtype)
    even_n, odd_n, even_f, odd_f = even[near, 0], odd[near, 0], even[far, 0], odd[far, 0]
    left_n = jnp.where(is_first == 1, zero, left_odd[near, 0])
    left_f = left_odd[jnp.where(is_first == 1, near, far), 0]
    right_n = right_even[jnp.where(is_last == 1, far, near), 0]
    right_f = jnp.where(is_last == 1, zero, right_even[far, 0])
    center = jnp.concatenate([even_n, odd_n, even_f, odd_f], axis=0)
    stacked = jnp.concatenate(
        [
            jnp.concatenate([left_n, even_n, left_f, even_f], axis=0),
            center,
            jnp.concatenate([odd_n, right_n, odd_f, right_f], axis=0),
        ],
        axis=1,
    )
    opening = gate(center, jnp.dot(stacked, w_first[...], preferred_element_type=jnp.float32))

    @pl.when(starting)
    def _():
        wait_pair(copies[1])

    rows = 2 * cells
    near_part, far_part = opening[:rows], opening[rows:]
    both = jnp.concatenate([near_part, far_part], axis=1)
    result_n = gate(
        near_part, jnp.dot(both, w_second[features:], preferred_element_type=jnp.float32)
    )
    result_f = gate(
        far_part, jnp.dot(both, w_second[: 2 * features], preferred_element_type=jnp.float32)
    )
    half = cells // 2
    for block, result in enumerate((result_n, result_f)):
        for slot in range(2):
            at = slot * cells
            out[2 * block, slot, 0] = result[at : at + half]
            out[2 * block + 1, slot, 0] = result[at + half : at + cells]


PINNED = pl.BlockSpec(memory_space=pl.ANY)
SCALARS = pl.BlockSpec(memory_space=pltpu.SMEM)


def run_section(place, before, arrived, weights):
    parts, slots, count, cells, features = arrived.shape
    ff = weights[2][0].shape[1]
    block_in = pl.BlockSpec((parts, slots, 1, cells, features), lambda i: (0, 0, i, 0, 0))
    block_out = pl.BlockSpec((2, 1, 2 * cells, features), lambda i: (0, i, 0, 0))
    shape = jax.ShapeDtypeStruct((2, count, 2 * cells, features), jnp.bfloat16)
    tokens = parts * slots * count * cells
    macs = tokens * (features * (4 * features + 2 * ff) + 4 * cells * features)
    flat = [half for pair in weights for half in pair]
    return pl.pallas_call(
        section_kernel,
        grid=(count,),
        out_shape=(shape, shape),
        in_specs=[SCALARS, PINNED, block_in] + [PINNED] * 8,
        out_specs=(block_out, block_out),
        scratch_shapes=[
            pltpu.VMEM((2 * mine.shape[0], mine.shape[1]), mine.dtype) for mine, _ in weights
        ]
        + [pltpu.SemaphoreType.DMA((4, 2))],
        compiler_params=pltpu.CompilerParams(vmem_limit_bytes=VMEM_LIMIT),
        cost_estimate=pl.CostEstimate(
            flops=6 * macs, bytes_accessed=8 * tokens * features, transcendentals=tokens * ff
        ),
        name="section",
    )(place, before, arrived, *flat)


def run_temporal(place, before, even, odd, left_odd, right_even, weights):
    blocks, count, cells, features = even.shape
    block_in = pl.BlockSpec((blocks, 1, cells, features), lambda i: (0, i, 0, 0))
    parts, slots = 2 * blocks, 2
    block_out = pl.BlockSpec((parts, slots, 1, cells // 2, features), lambda i: (0, 0, i, 0, 0))
    shape = jax.ShapeDtypeStruct((parts, slots, count, cells // 2, features), jnp.bfloat16)
    tokens = 2 * blocks * count * cells
    flat = [half for pair in weights for half in pair]
    return pl.pallas_call(
        temporal_kernel,
        grid=(count,),
        out_shape=shape,
        in_specs=[SCALARS, PINNED] + [block_in] * 4 + [PINNED] * 4,
        out_specs=block_out,
        scratch_shapes=[
            pltpu.VMEM((2 * mine.shape[0], mine.shape[1]), mine.dtype) for mine, _ in weights
        ]
        + [pltpu.SemaphoreType.DMA((2, 2))],
        compiler_params=pltpu.CompilerParams(vmem_limit_bytes=VMEM_LIMIT),
        cost_estimate=pl.CostEstimate(
            flops=60 * tokens * features * features,
            bytes_accessed=8 * tokens * features,
            transcendentals=4 * tokens * features,
        ),
        name="temporal",
    )(place, before, even, odd, left_odd, right_even, *flat)


def pack_kernel(begin, count, before, frames, packed, sems):
    copies = []
    for part in range(packed.shape[0]):
        for slot in range(packed.shape[1]):
            source = frames.at[slot, begin + part * count : begin + (part + 1) * count]
            copies.append(
                pltpu.make_async_copy(source, packed.at[part, slot], sems.at[part, slot])
            )
    for copy in copies:
        copy.start()
    for copy in copies:
        copy.wait()


def run_pack(before, grouped, begin, count, parts):
    slots, _, cells, features = grouped.shape
    return pl.pallas_call(
        functools.partial(pack_kernel, begin, count),
        out_shape=jax.ShapeDtypeStruct((parts, slots, count, cells, features), grouped.dtype),
        in_specs=[PINNED, PINNED],
        out_specs=PINNED,
        scratch_shapes=[pltpu.SemaphoreType.DMA((parts, slots))],
        cost_estimate=pl.CostEstimate(
            flops=0,
            bytes_accessed=4 * parts * slots * count * cells * features,
            transcendentals=0,
        ),
        name="pack",
    )(before, grouped)


def paired(frames, w_qkv, w_out, w_up, w_down, temporal_weight_first, temporal_weight_second):
    frames_local, cells, features = frames.shape
    near_size, subs = lax.axis_size("near"), lax.axis_size("sub")
    sub = lax.axis_index("sub")
    ring = near_size * subs
    position = lax.axis_index("near") * subs + sub
    place = jnp.stack([sub, position == 0, position == ring - 1]).astype(jnp.int32)
    rightward = [(i, (i + 1) % ring) for i in range(ring)]
    leftward = [(target, source) for source, target in rightward]
    slots = frames_local // DILATION_FIRST
    grouped = frames.reshape(slots, DILATION_FIRST, cells, features)

    arrived = []
    begin = 0
    before = place
    for count in CHUNKS:
        before = run_pack(before, grouped, begin, count, 4)
        arrived.append(lax.all_to_all(before, ("far", "cell"), 0, 0))
        begin += 4 * count

    def swap_core(weight):
        return weight, lax.ppermute(weight, "sub", [(0, 1), (1, 0)])

    section_weights = [swap_core(w) for w in (w_qkv, w_out, w_up, w_down)]
    temporal_weights = [swap_core(w) for w in (temporal_weight_first, temporal_weight_second)]

    waiting, backs = {}, {}
    before = place
    for kind, index in ORDER:
        if kind == "s":
            even, odd = run_section(place, before, arrived[index], section_weights)
            left_odd = lax.ppermute(odd, ("near", "sub"), rightward)
            right_even = lax.ppermute(even, ("near", "sub"), leftward)
            waiting[index] = (even, odd, left_odd, right_even)
            before = even
        else:
            before = run_temporal(place, before, *waiting[index], temporal_weights)
            backs[index] = lax.all_to_all(before, ("far", "cell"), 0, 0)
    results = [
        backs[index].swapaxes(0, 1).reshape(slots, 4 * count, cells, features)
        for index, count in enumerate(CHUNKS)
    ]
    return jnp.concatenate(results, axis=1).reshape(frames.shape)


def solution(mesh):
    groups, tm, cell, sub = (mesh.shape[axis] for axis in ("groups", "tm", "cell", "sub"))

    def run(frames, *weights):
        frame_total, cells, _ = frames.shape
        video = frame_total // groups
        frames_local = video // (tm * sub)
        fits = (
            video == 2 * DILATION_SECOND
            and frames_local == 2 * DILATION_FIRST
            and tm % 2 == 0
            and cell == 2
            and sub == 2
            and (cells // cell) % 16 == 0
            and DILATION_FIRST == 4 * sum(CHUNKS)
        )
        if fits:
            devices = mesh.devices.reshape(groups, 2, tm // 2, cell, sub)
            axes = ("groups", "far", "near", "cell", "sub")
            used, split, body = jax.sharding.Mesh(devices, axes), ("groups", "far", "near", "sub"), paired
        else:
            used, split, body = mesh, ("groups", "tm", "sub"), general
        return jax.shard_map(
            body,
            mesh=used,
            in_specs=(P(split, "cell", None),) + (P("sub", None),) * 6,
            out_specs=P(split, "cell", None),
            check_vma=False,
        )(frames, *weights)

    return run
```

```python
import math

import jax
import jax.numpy as jnp
from jax import lax
from jax.experimental import pallas as pl
from jax.experimental.pallas import tpu as pltpu
from jax.sharding import PartitionSpec as P

HEAD_DIM = 64
DILATION_FIRST = 16
DILATION_SECOND = 256
CHUNKS = (1, 1, 1, 1)
ORDER = (("s", 0), ("s", 1), ("t", 0), ("s", 2), ("t", 1), ("s", 3), ("t", 2), ("t", 3))
VMEM_LIMIT = 24 * 1024 * 1024


def with_halo(block, sides, width):
    for axis, dim in sides:
        count = lax.axis_size(axis)
        forward = [(i, i + 1) for i in range(count - 1)]
        backward = [(target, source) for source, target in forward]
        low = lax.ppermute(
            lax.slice_in_dim(block, block.shape[dim] - width, None, axis=dim), axis, forward
        )
        high = lax.ppermute(lax.slice_in_dim(block, 0, width, axis=dim), axis, backward)
        block = jnp.concatenate([low, block, high], axis=dim)
    return block


def shifted(shard, axis, by):
    size = lax.axis_size(axis)
    pairs = [(i, i + by) for i in range(size) if 0 <= i + by < size]
    return lax.ppermute(shard, axis, pairs)


def normalize(values):
    row_mean = jnp.mean(values, axis=-1, keepdims=True)
    centred = values - row_mean
    row_var = jnp.mean(centred * centred, axis=-1, keepdims=True)
    return centred * lax.rsqrt(row_var + 1e-05)


def attend(queries, key_part, value_part):
    frame_count, q_cells, features = queries.shape
    head_count = features // HEAD_DIM
    q_heads = queries.reshape(frame_count, q_cells, head_count, HEAD_DIM)
    k_heads = key_part.reshape(frame_count, -1, head_count, HEAD_DIM)
    v_heads = value_part.reshape(frame_count, -1, head_count, HEAD_DIM)
    scores = jnp.einsum(
        "fqhd,fkhd->fhqk", q_heads, k_heads, preferred_element_type=jnp.float32
    ) * HEAD_DIM ** (-0.5)
    row_max = jnp.max(scores, axis=-1, keepdims=True)
    exp_terms = jnp.exp(scores - row_max)
    attn_probs = (exp_terms / jnp.sum(exp_terms, axis=-1, keepdims=True)).astype(jnp.bfloat16)
    mixed = jnp.einsum("fhqk,fkhd->fqhd", attn_probs, v_heads, preferred_element_type=jnp.float32)
    return mixed.astype(jnp.bfloat16).reshape(frame_count, q_cells, features)


def gated_step(center, earlier, later_frames, weight):
    features = center.shape[-1]
    stacked = jnp.concatenate([earlier, center, later_frames], axis=-1).reshape(-1, 3 * features)
    preact = jnp.dot(stacked, weight, preferred_element_type=jnp.float32)
    gated_part = jnp.tanh(preact[:, :features]) * jax.nn.sigmoid(preact[:, features:])
    return (center.astype(jnp.float32) + gated_part.reshape(center.shape)).astype(jnp.bfloat16)


def general(frames, w_qkv, w_out, w_up, w_down, temporal_weight_first, temporal_weight_second):
    frames_local, cell_rows, features = frames.shape
    whole_qkv, whole_out, whole_up, whole_down, whole_tcn_a, whole_tcn_b = (
        lax.all_gather(w, "sub", axis=0, tiled=True)
        for w in (w_qkv, w_out, w_up, w_down, temporal_weight_first, temporal_weight_second)
    )
    working = lax.all_to_all(frames, "cell", split_axis=0, concat_axis=1, tiled=True)
    frame_count, cells_here = (working.shape[0], working.shape[1])
    residual = working.astype(jnp.float32)
    normed = normalize(residual).astype(jnp.bfloat16).reshape(-1, features)
    projected = jnp.dot(normed, whole_qkv, preferred_element_type=jnp.float32).astype(jnp.bfloat16)
    projected = projected.reshape(frame_count, cells_here, 3 * features)
    attended = attend(
        projected[..., :features],
        projected[..., features : 2 * features],
        projected[..., 2 * features :],
    )
    out_part = jnp.dot(
        attended.reshape(-1, features), whole_out, preferred_element_type=jnp.float32
    )
    mid_state = (residual + out_part.reshape(frame_count, cells_here, features)).astype(
        jnp.bfloat16
    )
    mid_float = lax.optimization_barrier(mid_state).astype(jnp.float32)
    normed_two = normalize(mid_float).astype(jnp.bfloat16).reshape(-1, features)
    hidden = jax.nn.gelu(jnp.dot(normed_two, whole_up, preferred_element_type=jnp.float32)).astype(
        jnp.bfloat16
    )
    down_part = jnp.dot(hidden, whole_down, preferred_element_type=jnp.float32).reshape(
        frame_count, cells_here, features
    )
    sectioned_frames = (mid_float + down_part).astype(jnp.bfloat16)
    sectioned_frames = lax.all_to_all(
        sectioned_frames, "cell", split_axis=1, concat_axis=0, tiled=True
    )
    padded_frames = with_halo(sectioned_frames, ((("tm", "sub"), 0),), DILATION_FIRST)
    earlier = padded_frames[:frames_local]
    later_frames = padded_frames[2 * DILATION_FIRST : 2 * DILATION_FIRST + frames_local]
    opening_layer = gated_step(sectioned_frames, earlier, later_frames, whole_tcn_a)
    shard_step_count = DILATION_SECOND // frames_local
    far_earlier = shifted(opening_layer, ("tm", "sub"), shard_step_count)
    far_later = shifted(opening_layer, ("tm", "sub"), -shard_step_count)
    return gated_step(opening_layer, far_earlier, far_later, whole_tcn_b)


ANYWHERE = pl.BlockSpec(memory_space=pl.ANY)
RESIDENT = pl.BlockSpec(memory_space=pltpu.VMEM)
SCALARS = pl.BlockSpec(memory_space=pltpu.SMEM)


def params():
    return pltpu.CompilerParams(vmem_limit_bytes=VMEM_LIMIT)


def moved(count):
    return pl.CostEstimate(flops=0, bytes_accessed=4 * count, transcendentals=0)


def pack_weights_kernel(before, *refs):
    *sources, packed = refs
    width = packed.shape[1]
    at = 0
    for source in sources:
        rows = source.shape[0]
        for column in range(0, source.shape[1], width):
            packed[at : at + rows] = source[:, column : column + width]
            at += rows


def pack_weights(before, weights, width):
    rows = sum(w.size for w in weights) // width
    return pl.pallas_call(
        pack_weights_kernel,
        out_shape=jax.ShapeDtypeStruct((rows, width), weights[0].dtype),
        in_specs=[ANYWHERE] + [RESIDENT] * len(weights),
        out_specs=RESIDENT,
        compiler_params=params(),
        cost_estimate=moved(rows * width),
        name="pack_weights",
    )(before, *weights)


def join_weights_kernel(place, before, mine, other, *wholes):
    width = mine.shape[1]
    for source, index in ((mine, place[0]), (other, 1 - place[0])):
        at = 0
        for whole in wholes:
            rows = whole.shape[0] // 2
            spot = pl.ds(pl.multiple_of(index * rows, 16), rows)
            for column in range(0, whole.shape[1], width):
                whole[spot, column : column + width] = source[at : at + rows]
                at += rows


def join_weights(place, before, mine, other, halves):
    return pl.pallas_call(
        join_weights_kernel,
        out_shape=[jax.ShapeDtypeStruct((2 * w.shape[0], w.shape[1]), w.dtype) for w in halves],
        in_specs=[SCALARS, ANYWHERE, RESIDENT, RESIDENT],
        out_specs=[RESIDENT] * len(halves),
        compiler_params=params(),
        cost_estimate=moved(2 * mine.size),
        name="join_weights",
    )(place, before, mine, other)


def pack_kernel(place, before, *refs):
    half = len(refs) // 2
    for source, packed in zip(refs[:half], refs[half:]):
        packed[...] = source[...]


def run_pack(place, before, grouped, begin, count):
    slots, _, cells, features = grouped.shape
    shape = (slots, 1, cells, features)

    def source(delta):
        return pl.BlockSpec(
            shape, lambda i, at: (0, begin + (at[4] ^ delta) * count + i, 0, 0)
        )

    return pl.pallas_call(
        pack_kernel,
        grid_spec=pltpu.PrefetchScalarGridSpec(
            num_scalar_prefetch=1,
            grid=(count,),
            in_specs=[ANYWHERE] + [source(delta) for delta in (1, 2, 3)],
            out_specs=[pl.BlockSpec(shape, lambda i, at: (0, i, 0, 0))] * 3,
        ),
        out_shape=[jax.ShapeDtypeStruct((slots, count, cells, features), grouped.dtype)] * 3,
        compiler_params=params(),
        cost_estimate=moved(3 * slots * count * cells * features),
        name="pack",
    )(place, before, grouped, grouped, grouped)


def section_kernel(
    place,
    before,
    own,
    near_cells,
    far_own,
    far_cells,
    w_qkv,
    w_out,
    w_up,
    w_down,
    even_ref,
    odd_ref,
):
    features = own.shape[-1]
    cells = 2 * own.shape[2]
    parts = []
    for mine, other in ((own, near_cells), (far_own, far_cells)):
        for slot in range(2):
            parts += [mine[slot, 0], other[slot, 0]]
    residual = jnp.concatenate(parts, axis=0).astype(jnp.float32)
    frame_count = 4
    normed = normalize(residual).astype(jnp.bfloat16)
    projected = jnp.dot(normed, w_qkv[...], preferred_element_type=jnp.float32).astype(jnp.bfloat16)
    pair_width = 2 * HEAD_DIM
    low = lax.broadcasted_iota(jnp.int32, (cells, pair_width), 1) < HEAD_DIM
    low_one = low.astype(jnp.bfloat16)
    high_one = 1 - low_one
    scale = HEAD_DIM ** (-0.5) * math.log2(math.e)
    rows = []
    for frame in range(frame_count):
        block = projected[frame * cells : (frame + 1) * cells]
        columns = []
        for pair in range(features // pair_width):
            at = pair * pair_width
            queries = block[:, at : at + pair_width]
            keys = block[:, features + at : features + at + pair_width]
            values = block[:, 2 * features + at : 2 * features + at + pair_width]
            split_keys = jnp.concatenate([keys * low_one, keys * high_one], axis=0)
            scores = lax.dot_general(
                queries, split_keys, (((1,), (1,)), ((), ())), preferred_element_type=jnp.float32
            )
            terms = []
            for head in range(2):
                own_scores = scores[:, head * cells : (head + 1) * cells]
                row_max = jnp.max(own_scores, axis=-1, keepdims=True)
                terms.append(jnp.exp2((own_scores - row_max) * scale).astype(jnp.bfloat16))
            split_values = jnp.concatenate(
                [
                    jnp.concatenate([values * low_one, low_one], axis=1),
                    jnp.concatenate([values * high_one, high_one], axis=1),
                ],
                axis=0,
            )
            mixed = jnp.dot(
                jnp.concatenate(terms, axis=1), split_values, preferred_element_type=jnp.float32
            )
            columns.append((mixed[:, :pair_width] / mixed[:, pair_width:]).astype(jnp.bfloat16))
        rows.append(jnp.concatenate(columns, axis=1))
    attended = jnp.concatenate(rows, axis=0)

    mid_state = (
        residual + jnp.dot(attended, w_out[...], preferred_element_type=jnp.float32)
    ).astype(jnp.bfloat16)
    mid_float = mid_state.astype(jnp.float32)
    normed_two = normalize(mid_float).astype(jnp.bfloat16)
    total = mid_float
    width = features
    for at in range(0, w_up.shape[1], width):
        lifted = jnp.dot(normed_two, w_up[:, at : at + width], preferred_element_type=jnp.float32)
        inner = lifted * (
            math.sqrt(2 / math.pi) + (math.sqrt(2 / math.pi) * 0.044715) * (lifted * lifted)
        )
        halved = 0.5 * lifted
        hidden = (halved + halved * jnp.tanh(inner)).astype(jnp.bfloat16)
        total = total + jnp.dot(hidden, w_down[at : at + width], preferred_element_type=jnp.float32)
    sectioned = total.astype(jnp.bfloat16)
    for block in range(2):
        even_ref[block, 0] = sectioned[(2 * block) * cells : (2 * block + 1) * cells]
        odd_ref[block, 0] = sectioned[(2 * block + 1) * cells : (2 * block + 2) * cells]


def gate(center, preact):
    features = center.shape[-1]
    gated = jnp.tanh(preact[:, :features]) * (
        0.5 + 0.5 * jnp.tanh(0.5 * preact[:, features:])
    )
    return (center.astype(jnp.float32) + gated).astype(jnp.bfloat16)


def temporal_kernel(
    place,
    before,
    even,
    odd,
    left_odd,
    right_even,
    w_first,
    w_second,
    out0,
    out1,
    out2,
    out3,
):
    near, is_first, is_last = place[1], place[2], place[3]
    far = 1 - near
    features = even.shape[-1]
    cells = even.shape[2]
    zero = jnp.zeros((cells, features), even.dtype)
    even_n, odd_n, even_f, odd_f = even[near, 0], odd[near, 0], even[far, 0], odd[far, 0]
    left_n = jnp.where(is_first == 1, zero, left_odd[near, 0])
    left_f = left_odd[jnp.where(is_first == 1, near, far), 0]
    right_n = right_even[jnp.where(is_last == 1, far, near), 0]
    right_f = jnp.where(is_last == 1, zero, right_even[far, 0])
    center = jnp.concatenate([even_n, odd_n, even_f, odd_f], axis=0)
    stacked = jnp.concatenate(
        [
            jnp.concatenate([left_n, even_n, left_f, even_f], axis=0),
            center,
            jnp.concatenate([odd_n, right_n, odd_f, right_f], axis=0),
        ],
        axis=1,
    )
    opening = gate(center, jnp.dot(stacked, w_first[...], preferred_element_type=jnp.float32))
    rows = 2 * cells
    near_part, far_part = opening[:rows], opening[rows:]
    both = jnp.concatenate([near_part, far_part], axis=1)
    result_n = gate(
        near_part, jnp.dot(both, w_second[features:], preferred_element_type=jnp.float32)
    )
    result_f = gate(
        far_part, jnp.dot(both, w_second[: 2 * features], preferred_element_type=jnp.float32)
    )
    same = jnp.where(near == 0, result_n, result_f)
    other = jnp.where(near == 0, result_f, result_n)
    half = cells // 2
    for slot in range(2):
        at = slot * cells
        out0[slot, 0] = same[at : at + half]
        out1[slot, 0] = same[at + half : at + cells]
        out2[slot, 0] = other[at : at + half]
        out3[slot, 0] = other[at + half : at + cells]


def run_section(place, before, grouped, begin, pieces, weights):
    slots, count, cells, features = pieces[0].shape
    ff = weights[2].shape[1]
    shape_in = (slots, 1, cells, features)
    own = pl.BlockSpec(shape_in, lambda i, at: (0, begin + at[4] * count + i, 0, 0))
    block_in = pl.BlockSpec(shape_in, lambda i, at: (0, i, 0, 0))
    block_out = pl.BlockSpec((2, 1, 2 * cells, features), lambda i, at: (0, i, 0, 0))
    shape = jax.ShapeDtypeStruct((2, count, 2 * cells, features), jnp.bfloat16)
    tokens = 2 * slots * count * 2 * cells
    macs = tokens * (features * (4 * features + 2 * ff) + 4 * cells * features)
    return pl.pallas_call(
        section_kernel,
        grid_spec=pltpu.PrefetchScalarGridSpec(
            num_scalar_prefetch=1,
            grid=(count,),
            in_specs=[ANYWHERE, own] + [block_in] * 3 + [RESIDENT] * 4,
            out_specs=[block_out, block_out],
        ),
        out_shape=[shape, shape],
        compiler_params=params(),
        cost_estimate=pl.CostEstimate(
            flops=6 * macs, bytes_accessed=8 * tokens * features, transcendentals=tokens * ff
        ),
        name="section",
    )(place, before, grouped, *pieces, *weights)


def run_temporal(place, before, even, odd, left_odd, right_even, weights):
    blocks, count, cells, features = even.shape
    block_in = pl.BlockSpec((blocks, 1, cells, features), lambda i, at: (0, i, 0, 0))
    block_out = pl.BlockSpec((2, 1, cells // 2, features), lambda i, at: (0, i, 0, 0))
    shape = jax.ShapeDtypeStruct((2, count, cells // 2, features), jnp.bfloat16)
    tokens = 2 * blocks * count * cells
    return pl.pallas_call(
        temporal_kernel,
        grid_spec=pltpu.PrefetchScalarGridSpec(
            num_scalar_prefetch=1,
            grid=(count,),
            in_specs=[ANYWHERE] + [block_in] * 4 + [RESIDENT] * 2,
            out_specs=[block_out] * 4,
        ),
        out_shape=[shape] * 4,
        compiler_params=params(),
        cost_estimate=pl.CostEstimate(
            flops=60 * tokens * features * features,
            bytes_accessed=8 * tokens * features,
            transcendentals=4 * tokens * features,
        ),
        name="temporal",
    )(place, before, even, odd, left_odd, right_even, *weights)


GROUP = ("far", "cell")
RING = ("near", "sub")


def paired(frames, w_qkv, w_out, w_up, w_down, temporal_weight_first, temporal_weight_second):
    frames_local, cells, features = frames.shape
    near_size, subs = lax.axis_size("near"), lax.axis_size("sub")
    sub, side = lax.axis_index("sub"), lax.axis_index("far")
    quarter = 2 * side + lax.axis_index("cell")
    ring = near_size * subs
    position = lax.axis_index("near") * subs + sub
    place = jnp.stack([sub, side, position == 0, position == ring - 1, quarter]).astype(jnp.int32)
    rightward = [(i, (i + 1) % ring) for i in range(ring)]
    leftward = [(target, source) for source, target in rightward]
    slots = frames_local // DILATION_FIRST
    grouped = frames.reshape(slots, DILATION_FIRST, cells, features)
    begins = [4 * sum(CHUNKS[:index]) for index in range(len(CHUNKS))]

    def exchange(piece, delta):
        return lax.ppermute(piece, GROUP, [(i, i ^ delta) for i in range(4)])

    def send(before, index):
        cut = run_pack(place, before, grouped, begins[index], CHUNKS[index])
        return cut[0], [exchange(piece, delta) for delta, piece in zip((1, 2, 3), cut)]

    def swap_core(packed):
        return lax.ppermute(packed, "sub", [(0, 1), (1, 0)])

    section_halves = (w_qkv, w_out, w_up, w_down)
    temporal_halves = (temporal_weight_first, temporal_weight_second)
    arrived = {}
    before, arrived[0] = send(place, 0)
    section_mine = pack_weights(before, section_halves, features)
    section_weights = join_weights(
        place, before, section_mine, swap_core(section_mine), section_halves
    )
    before, arrived[1] = send(section_weights[0], 1)
    temporal_mine = pack_weights(before, temporal_halves, features)
    temporal_weights = join_weights(
        place, before, temporal_mine, swap_core(temporal_mine), temporal_halves
    )
    before = temporal_weights[0]
    for index in range(2, len(CHUNKS)):
        before, arrived[index] = send(before, index)

    waiting, outs = {}, {}
    before = place
    for kind, index in ORDER:
        if kind == "s":
            even, odd = run_section(
                place, before, grouped, begins[index], arrived[index], section_weights
            )
            left_odd = lax.ppermute(odd, RING, rightward)
            right_even = lax.ppermute(even, RING, leftward)
            waiting[index] = (even, odd, left_odd, right_even)
            before = even
        else:
            sent = run_temporal(place, before, *waiting[index], temporal_weights)
            outs[index] = [sent[0]] + [exchange(sent[delta], delta) for delta in (1, 2, 3)]
            before = sent[0]
    result = jnp.zeros_like(grouped)
    for index, count in enumerate(CHUNKS):
        for delta in range(4):
            result = lax.dynamic_update_slice_in_dim(
                result, outs[index][delta], begins[index] + (quarter ^ delta) * count, axis=1
            )
    return result.reshape(frames.shape)


def solution(mesh):
    groups, tm, cell, sub = (mesh.shape[axis] for axis in ("groups", "tm", "cell", "sub"))

    def run(frames, *weights):
        frame_total, cells, _ = frames.shape
        video = frame_total // groups
        frames_local = video // (tm * sub)
        fits = (
            video == 2 * DILATION_SECOND
            and frames_local == 2 * DILATION_FIRST
            and tm % 2 == 0
            and cell == 2
            and sub == 2
            and (cells // cell) % 16 == 0
            and DILATION_FIRST == 4 * sum(CHUNKS)
        )
        if fits:
            devices = mesh.devices.reshape(groups, 2, tm // 2, cell, sub)
            axes = ("groups", "far", "near", "cell", "sub")
            used, split, body = jax.sharding.Mesh(devices, axes), ("groups", "far", "near", "sub"), paired
        else:
            used, split, body = mesh, ("groups", "tm", "sub"), general
        return jax.shard_map(
            body,
            mesh=used,
            in_specs=(P(split, "cell", None),) + (P("sub", None),) * 6,
            out_specs=P(split, "cell", None),
            check_vma=False,
        )(frames, *weights)

    return run
```

```python
import math

import jax
import jax.numpy as jnp
from jax import lax
from jax.experimental import pallas as pl
from jax.experimental.pallas import tpu as pltpu
from jax.sharding import PartitionSpec as P

HEAD_DIM = 64
DILATION_FIRST = 16
DILATION_SECOND = 256
GROUPS = ((0, 1), (2,), (3,))
ORDER = (("s", 0), ("s", 1), ("t", 0), ("s", 2), ("s", 3), ("t", 1), ("t", 2))
MIB = 1024 * 1024
SECTION_MIB = 14
TEMPORAL_MIB = 14


def with_halo(block, sides, width):
    for axis, dim in sides:
        count = lax.axis_size(axis)
        forward = [(i, i + 1) for i in range(count - 1)]
        backward = [(target, source) for source, target in forward]
        low = lax.ppermute(
            lax.slice_in_dim(block, block.shape[dim] - width, None, axis=dim), axis, forward
        )
        high = lax.ppermute(lax.slice_in_dim(block, 0, width, axis=dim), axis, backward)
        block = jnp.concatenate([low, block, high], axis=dim)
    return block


def shifted(shard, axis, by):
    size = lax.axis_size(axis)
    pairs = [(i, i + by) for i in range(size) if 0 <= i + by < size]
    return lax.ppermute(shard, axis, pairs)


def normalize(values):
    row_mean = jnp.mean(values, axis=-1, keepdims=True)
    centred = values - row_mean
    row_var = jnp.mean(centred * centred, axis=-1, keepdims=True)
    return centred * lax.rsqrt(row_var + 1e-05)


def attend(queries, key_part, value_part):
    frame_count, q_cells, features = queries.shape
    head_count = features // HEAD_DIM
    q_heads = queries.reshape(frame_count, q_cells, head_count, HEAD_DIM)
    k_heads = key_part.reshape(frame_count, -1, head_count, HEAD_DIM)
    v_heads = value_part.reshape(frame_count, -1, head_count, HEAD_DIM)
    scores = jnp.einsum(
        "fqhd,fkhd->fhqk", q_heads, k_heads, preferred_element_type=jnp.float32
    ) * HEAD_DIM ** (-0.5)
    row_max = jnp.max(scores, axis=-1, keepdims=True)
    exp_terms = jnp.exp(scores - row_max)
    attn_probs = (exp_terms / jnp.sum(exp_terms, axis=-1, keepdims=True)).astype(jnp.bfloat16)
    mixed = jnp.einsum("fhqk,fkhd->fqhd", attn_probs, v_heads, preferred_element_type=jnp.float32)
    return mixed.astype(jnp.bfloat16).reshape(frame_count, q_cells, features)


def gated_step(center, earlier, later_frames, weight):
    features = center.shape[-1]
    stacked = jnp.concatenate([earlier, center, later_frames], axis=-1).reshape(-1, 3 * features)
    preact = jnp.dot(stacked, weight, preferred_element_type=jnp.float32)
    gated_part = jnp.tanh(preact[:, :features]) * jax.nn.sigmoid(preact[:, features:])
    return (center.astype(jnp.float32) + gated_part.reshape(center.shape)).astype(jnp.bfloat16)


def general(frames, w_qkv, w_out, w_up, w_down, temporal_weight_first, temporal_weight_second):
    frames_local, cell_rows, features = frames.shape
    whole_qkv, whole_out, whole_up, whole_down, whole_tcn_a, whole_tcn_b = (
        lax.all_gather(w, "sub", axis=0, tiled=True)
        for w in (w_qkv, w_out, w_up, w_down, temporal_weight_first, temporal_weight_second)
    )
    working = lax.all_to_all(frames, "cell", split_axis=0, concat_axis=1, tiled=True)
    frame_count, cells_here = (working.shape[0], working.shape[1])
    residual = working.astype(jnp.float32)
    normed = normalize(residual).astype(jnp.bfloat16).reshape(-1, features)
    projected = jnp.dot(normed, whole_qkv, preferred_element_type=jnp.float32).astype(jnp.bfloat16)
    projected = projected.reshape(frame_count, cells_here, 3 * features)
    attended = attend(
        projected[..., :features],
        projected[..., features : 2 * features],
        projected[..., 2 * features :],
    )
    out_part = jnp.dot(
        attended.reshape(-1, features), whole_out, preferred_element_type=jnp.float32
    )
    mid_state = (residual + out_part.reshape(frame_count, cells_here, features)).astype(
        jnp.bfloat16
    )
    mid_float = lax.optimization_barrier(mid_state).astype(jnp.float32)
    normed_two = normalize(mid_float).astype(jnp.bfloat16).reshape(-1, features)
    hidden = jax.nn.gelu(jnp.dot(normed_two, whole_up, preferred_element_type=jnp.float32)).astype(
        jnp.bfloat16
    )
    down_part = jnp.dot(hidden, whole_down, preferred_element_type=jnp.float32).reshape(
        frame_count, cells_here, features
    )
    sectioned_frames = (mid_float + down_part).astype(jnp.bfloat16)
    sectioned_frames = lax.all_to_all(
        sectioned_frames, "cell", split_axis=1, concat_axis=0, tiled=True
    )
    padded_frames = with_halo(sectioned_frames, ((("tm", "sub"), 0),), DILATION_FIRST)
    earlier = padded_frames[:frames_local]
    later_frames = padded_frames[2 * DILATION_FIRST : 2 * DILATION_FIRST + frames_local]
    opening_layer = gated_step(sectioned_frames, earlier, later_frames, whole_tcn_a)
    shard_step_count = DILATION_SECOND // frames_local
    far_earlier = shifted(opening_layer, ("tm", "sub"), shard_step_count)
    far_later = shifted(opening_layer, ("tm", "sub"), -shard_step_count)
    return gated_step(opening_layer, far_earlier, far_later, whole_tcn_b)


ANYWHERE = pl.BlockSpec(memory_space=pl.ANY)
RESIDENT = pl.BlockSpec(memory_space=pltpu.VMEM)
SCALARS = pl.BlockSpec(memory_space=pltpu.SMEM)


def params(mib):
    return pltpu.CompilerParams(vmem_limit_bytes=mib * MIB)


def moved(count):
    return pl.CostEstimate(flops=0, bytes_accessed=4 * count, transcendentals=0)


def pack_weights_kernel(before, *refs):
    *sources, packed = refs
    width = packed.shape[1]
    at = 0
    for source in sources:
        rows = source.shape[0]
        for column in range(0, source.shape[1], width):
            packed[at : at + rows] = source[:, column : column + width]
            at += rows


def pack_weights(before, weights, width):
    rows = sum(w.size for w in weights) // width
    return pl.pallas_call(
        pack_weights_kernel,
        out_shape=jax.ShapeDtypeStruct((rows, width), weights[0].dtype),
        in_specs=[ANYWHERE] + [RESIDENT] * len(weights),
        out_specs=RESIDENT,
        compiler_params=params(8),
        cost_estimate=moved(rows * width),
        name="pack_weights",
    )(before, *weights)


def join_weights_kernel(place, before, mine, other, *wholes):
    width = mine.shape[1]
    for source, index in ((mine, place[0]), (other, 1 - place[0])):
        at = 0
        for whole in wholes:
            rows = whole.shape[0] // 2
            spot = pl.ds(pl.multiple_of(index * rows, 16), rows)
            for column in range(0, whole.shape[1], width):
                whole[spot, column : column + width] = source[at : at + rows]
                at += rows


def join_weights(place, before, mine, other, halves):
    return pl.pallas_call(
        join_weights_kernel,
        out_shape=[jax.ShapeDtypeStruct((2 * w.shape[0], w.shape[1]), w.dtype) for w in halves],
        in_specs=[SCALARS, ANYWHERE, RESIDENT, RESIDENT],
        out_specs=[RESIDENT] * len(halves),
        compiler_params=params(8),
        cost_estimate=moved(2 * mine.size),
        name="join_weights",
    )(place, before, mine, other)


def pack_kernel(before, source, packed):
    for part in range(packed.shape[0]):
        packed[part] = source[:, part]


def run_pack(before, grouped, unit, parts):
    slots, _, cells, features = grouped.shape
    return pl.pallas_call(
        pack_kernel,
        grid=(1,),
        in_specs=[
            ANYWHERE,
            pl.BlockSpec((slots, parts, cells, features), lambda i: (0, unit, 0, 0)),
        ],
        out_specs=pl.BlockSpec((parts, slots, cells, features), lambda i: (0, 0, 0, 0)),
        out_shape=jax.ShapeDtypeStruct((parts, slots, cells, features), grouped.dtype),
        compiler_params=params(4),
        cost_estimate=moved(parts * slots * cells * features),
        name="pack",
    )(before, grouped)


def unpack_kernel(before, buffer, received, result):
    for unit in range(received.shape[2]):

        @pl.when(pl.program_id(0) == unit)
        def _():
            for part in range(received.shape[0]):
                result[:, part] = received[part, :, unit]


def run_unpack(before, buffer, received, first_unit, shape):
    parts, slots, count, cells, features = received.shape
    return pl.pallas_call(
        unpack_kernel,
        grid=(count,),
        in_specs=[ANYWHERE, ANYWHERE, RESIDENT],
        out_specs=pl.BlockSpec(
            (slots, parts, cells, features), lambda i: (0, first_unit + i, 0, 0)
        ),
        out_shape=pltpu.HBM(shape, received.dtype),
        input_output_aliases={} if buffer is before else {1: 0},
        compiler_params=params(4),
        cost_estimate=moved(received.size),
        name="unpack",
    )(before, buffer, received)


def section_kernel(before, arrived, w_qkv, w_out, w_up, w_down, even_ref, odd_ref):
    features = arrived.shape[-1]
    cells = 2 * arrived.shape[2]
    parts = []
    for block in range(2):
        for slot in range(2):
            parts += [arrived[2 * block, slot], arrived[2 * block + 1, slot]]
    residual = jnp.concatenate(parts, axis=0).astype(jnp.float32)
    frame_count = 4
    normed = normalize(residual).astype(jnp.bfloat16)
    projected = jnp.dot(normed, w_qkv[...], preferred_element_type=jnp.float32).astype(jnp.bfloat16)
    pair_width = 2 * HEAD_DIM
    low = lax.broadcasted_iota(jnp.int32, (cells, pair_width), 1) < HEAD_DIM
    low_one = low.astype(jnp.bfloat16)
    high_one = 1 - low_one
    scale = HEAD_DIM ** (-0.5) * math.log2(math.e)
    rows = []
    for frame in range(frame_count):
        block = projected[frame * cells : (frame + 1) * cells]
        columns = []
        for pair in range(features // pair_width):
            at = pair * pair_width
            queries = block[:, at : at + pair_width]
            keys = block[:, features + at : features + at + pair_width]
            values = block[:, 2 * features + at : 2 * features + at + pair_width]
            split_keys = jnp.concatenate([keys * low_one, keys * high_one], axis=0)
            scores = lax.dot_general(
                queries, split_keys, (((1,), (1,)), ((), ())), preferred_element_type=jnp.float32
            )
            terms = []
            for head in range(2):
                own_scores = scores[:, head * cells : (head + 1) * cells]
                row_max = jnp.max(own_scores, axis=-1, keepdims=True)
                terms.append(jnp.exp2((own_scores - row_max) * scale).astype(jnp.bfloat16))
            split_values = jnp.concatenate(
                [
                    jnp.concatenate([values * low_one, low_one], axis=1),
                    jnp.concatenate([values * high_one, high_one], axis=1),
                ],
                axis=0,
            )
            mixed = jnp.dot(
                jnp.concatenate(terms, axis=1), split_values, preferred_element_type=jnp.float32
            )
            columns.append((mixed[:, :pair_width] / mixed[:, pair_width:]).astype(jnp.bfloat16))
        rows.append(jnp.concatenate(columns, axis=1))
    attended = jnp.concatenate(rows, axis=0)

    mid_state = (
        residual + jnp.dot(attended, w_out[...], preferred_element_type=jnp.float32)
    ).astype(jnp.bfloat16)
    mid_float = mid_state.astype(jnp.float32)
    normed_two = normalize(mid_float).astype(jnp.bfloat16)
    total = mid_float
    width = features
    for at in range(0, w_up.shape[1], width):
        lifted = jnp.dot(normed_two, w_up[:, at : at + width], preferred_element_type=jnp.float32)
        inner = lifted * (
            math.sqrt(2 / math.pi) + (math.sqrt(2 / math.pi) * 0.044715) * (lifted * lifted)
        )
        halved = 0.5 * lifted
        hidden = (halved + halved * jnp.tanh(inner)).astype(jnp.bfloat16)
        total = total + jnp.dot(hidden, w_down[at : at + width], preferred_element_type=jnp.float32)
    sectioned = total.astype(jnp.bfloat16)
    for block in range(2):
        even_ref[block] = sectioned[(2 * block) * cells : (2 * block + 1) * cells]
        odd_ref[block] = sectioned[(2 * block + 1) * cells : (2 * block + 2) * cells]


def gate(center, preact):
    features = center.shape[-1]
    gated = jnp.tanh(preact[:, :features]) * (
        0.5 + 0.5 * jnp.tanh(0.5 * preact[:, features:])
    )
    return (center.astype(jnp.float32) + gated).astype(jnp.bfloat16)


def temporal_kernel(place, before, *refs):
    *inputs, w_first, w_second, out = refs
    is_first, is_last = place[1], place[2]
    for unit in range(len(inputs) // 4):
        even, odd, left_odd, right_even = inputs[4 * unit : 4 * unit + 4]
        _, cells, features = even.shape
        zero = jnp.zeros((cells, features), even.dtype)
        even_n, odd_n, even_f, odd_f = even[0], odd[0], even[1], odd[1]
        left_n = jnp.where(is_first == 1, zero, left_odd[0])
        left_f = left_odd[jnp.where(is_first == 1, 0, 1)]
        right_n = right_even[jnp.where(is_last == 1, 1, 0)]
        right_f = jnp.where(is_last == 1, zero, right_even[1])
        center = jnp.concatenate([even_n, odd_n, even_f, odd_f], axis=0)
        stacked = jnp.concatenate(
            [
                jnp.concatenate([left_n, even_n, left_f, even_f], axis=0),
                center,
                jnp.concatenate([odd_n, right_n, odd_f, right_f], axis=0),
            ],
            axis=1,
        )
        opening = gate(center, jnp.dot(stacked, w_first[...], preferred_element_type=jnp.float32))
        rows = 2 * cells
        near_part, far_part = opening[:rows], opening[rows:]
        both = jnp.concatenate([near_part, far_part], axis=1)
        result_n = gate(
            near_part, jnp.dot(both, w_second[features:], preferred_element_type=jnp.float32)
        )
        result_f = gate(
            far_part, jnp.dot(both, w_second[: 2 * features], preferred_element_type=jnp.float32)
        )
        half = cells // 2
        for block, result in enumerate((result_n, result_f)):
            for slot in range(2):
                at = slot * cells
                out[2 * block, slot, unit] = result[at : at + half]
                out[2 * block + 1, slot, unit] = result[at + half : at + cells]


def run_section(before, arrived, weights):
    parts, slots, cells, features = arrived.shape
    ff = weights[2].shape[1]
    shape = jax.ShapeDtypeStruct((2, 2 * cells, features), jnp.bfloat16)
    tokens = parts * slots * cells
    macs = tokens * (features * (4 * features + 2 * ff) + 4 * cells * features)
    return pl.pallas_call(
        section_kernel,
        in_specs=[ANYWHERE] + [RESIDENT] * 5,
        out_specs=[RESIDENT] * 2,
        out_shape=[shape, shape],
        compiler_params=params(SECTION_MIB),
        cost_estimate=pl.CostEstimate(
            flops=6 * macs, bytes_accessed=8 * tokens * features, transcendentals=tokens * ff
        ),
        name="section",
    )(before, arrived, *weights)


def run_temporal(place, before, units, weights):
    blocks, cells, features = units[0][0].shape
    count = len(units)
    shape = jax.ShapeDtypeStruct((2 * blocks, 2, count, cells // 2, features), jnp.bfloat16)
    tokens = 2 * blocks * count * cells
    return pl.pallas_call(
        temporal_kernel,
        in_specs=[SCALARS, ANYWHERE] + [RESIDENT] * (4 * count + 2),
        out_specs=RESIDENT,
        out_shape=shape,
        compiler_params=params(TEMPORAL_MIB),
        cost_estimate=pl.CostEstimate(
            flops=60 * tokens * features * features,
            bytes_accessed=8 * tokens * features,
            transcendentals=4 * tokens * features,
        ),
        name="temporal",
    )(place, before, *[part for unit in units for part in unit], *weights)


GROUP = ("far", "cell")
RING = ("near", "sub")


def paired(frames, w_qkv, w_out, w_up, w_down, temporal_weight_first, temporal_weight_second):
    frames_local, cells, features = frames.shape
    near_size, subs = lax.axis_size("near"), lax.axis_size("sub")
    sub = lax.axis_index("sub")
    ring = near_size * subs
    position = lax.axis_index("near") * subs + sub
    place = jnp.stack([sub, position == 0, position == ring - 1]).astype(jnp.int32)
    rightward = [(i, (i + 1) % ring) for i in range(ring)]
    leftward = [(target, source) for source, target in rightward]
    slots = frames_local // DILATION_FIRST
    parts = 4
    grouped = frames.reshape(slots, DILATION_FIRST, cells, features)
    pinned = pltpu.with_memory_space_constraint(grouped, pltpu.HBM)

    def send(before, unit):
        cut = run_pack(before, pinned, unit, parts)
        return cut, lax.all_to_all(cut, GROUP, 0, 0)

    def swap_core(packed):
        return lax.ppermute(packed, "sub", [(0, 1), (1, 0)])

    section_halves = (w_qkv, w_out, w_up, w_down)
    temporal_halves = (temporal_weight_first, temporal_weight_second)
    arrived = {}
    before, arrived[0] = send(place, 0)
    section_mine = pack_weights(before, section_halves, features)
    before, arrived[1] = send(section_mine, 1)
    temporal_mine = pack_weights(before, temporal_halves, features)
    before, arrived[2] = send(temporal_mine, 2)
    before, arrived[3] = send(before, 3)
    section_weights = join_weights(
        place, before, section_mine, swap_core(section_mine), section_halves
    )
    temporal_weights = join_weights(
        place, section_weights[0], temporal_mine, swap_core(temporal_mine), temporal_halves
    )
    waiting, backs = {}, {}
    before = temporal_weights[0]
    for kind, index in ORDER:
        if kind == "s":
            even, odd = run_section(before, arrived[index], section_weights)
            left_odd = lax.ppermute(odd, RING, rightward)
            right_even = lax.ppermute(even, RING, leftward)
            waiting[index] = (even, odd, left_odd, right_even)
            before = even
        else:
            units = [waiting[unit] for unit in GROUPS[index]]
            before = run_temporal(place, before, units, temporal_weights)
            backs[index] = lax.all_to_all(before, GROUP, 0, 0)
    result = before
    for index, group in enumerate(GROUPS):
        result = run_unpack(before, result, backs[index], group[0], grouped.shape)
    return result.reshape(frames.shape)


def solution(mesh):
    groups, tm, cell, sub = (mesh.shape[axis] for axis in ("groups", "tm", "cell", "sub"))

    def run(frames, *weights):
        frame_total, cells, _ = frames.shape
        video = frame_total // groups
        frames_local = video // (tm * sub)
        fits = (
            video == 2 * DILATION_SECOND
            and frames_local == 2 * DILATION_FIRST
            and tm % 2 == 0
            and cell == 2
            and sub == 2
            and (cells // cell) % 16 == 0
            and DILATION_FIRST == 4 * sum(len(group) for group in GROUPS)
        )
        if fits:
            devices = mesh.devices.reshape(groups, 2, tm // 2, cell, sub)
            axes = ("groups", "far", "near", "cell", "sub")
            used, split, body = jax.sharding.Mesh(devices, axes), ("groups", "far", "near", "sub"), paired
        else:
            used, split, body = mesh, ("groups", "tm", "sub"), general
        return jax.shard_map(
            body,
            mesh=used,
            in_specs=(P(split, "cell", None),) + (P("sub", None),) * 6,
            out_specs=P(split, "cell", None),
            check_vma=False,
        )(frames, *weights)

    return run
```

```python
import functools
import math

import jax
import jax.numpy as jnp
from jax import lax
from jax.experimental import pallas as pl
from jax.experimental.pallas import tpu as pltpu
from jax.sharding import PartitionSpec as P

HEAD_DIM = 64
DILATION_FIRST = 16
DILATION_SECOND = 256
CHUNKS = (2, 2)
ORDER = (("s", 0), ("s", 1), ("t", 0), ("t", 1))
MIB = 1024 * 1024


def with_halo(block, sides, width):
    for axis, dim in sides:
        count = lax.axis_size(axis)
        forward = [(i, i + 1) for i in range(count - 1)]
        backward = [(target, source) for source, target in forward]
        low = lax.ppermute(
            lax.slice_in_dim(block, block.shape[dim] - width, None, axis=dim), axis, forward
        )
        high = lax.ppermute(lax.slice_in_dim(block, 0, width, axis=dim), axis, backward)
        block = jnp.concatenate([low, block, high], axis=dim)
    return block


def shifted(shard, axis, by):
    size = lax.axis_size(axis)
    pairs = [(i, i + by) for i in range(size) if 0 <= i + by < size]
    return lax.ppermute(shard, axis, pairs)


def normalize(values):
    row_mean = jnp.mean(values, axis=-1, keepdims=True)
    centred = values - row_mean
    row_var = jnp.mean(centred * centred, axis=-1, keepdims=True)
    return centred * lax.rsqrt(row_var + 1e-05)


def attend(queries, key_part, value_part):
    frame_count, q_cells, features = queries.shape
    head_count = features // HEAD_DIM
    q_heads = queries.reshape(frame_count, q_cells, head_count, HEAD_DIM)
    k_heads = key_part.reshape(frame_count, -1, head_count, HEAD_DIM)
    v_heads = value_part.reshape(frame_count, -1, head_count, HEAD_DIM)
    scores = jnp.einsum(
        "fqhd,fkhd->fhqk", q_heads, k_heads, preferred_element_type=jnp.float32
    ) * HEAD_DIM ** (-0.5)
    row_max = jnp.max(scores, axis=-1, keepdims=True)
    exp_terms = jnp.exp(scores - row_max)
    attn_probs = (exp_terms / jnp.sum(exp_terms, axis=-1, keepdims=True)).astype(jnp.bfloat16)
    mixed = jnp.einsum("fhqk,fkhd->fqhd", attn_probs, v_heads, preferred_element_type=jnp.float32)
    return mixed.astype(jnp.bfloat16).reshape(frame_count, q_cells, features)


def gated_step(center, earlier, later_frames, weight):
    features = center.shape[-1]
    stacked = jnp.concatenate([earlier, center, later_frames], axis=-1).reshape(-1, 3 * features)
    preact = jnp.dot(stacked, weight, preferred_element_type=jnp.float32)
    gated_part = jnp.tanh(preact[:, :features]) * jax.nn.sigmoid(preact[:, features:])
    return (center.astype(jnp.float32) + gated_part.reshape(center.shape)).astype(jnp.bfloat16)


def general(frames, w_qkv, w_out, w_up, w_down, temporal_weight_first, temporal_weight_second):
    frames_local, cell_rows, features = frames.shape
    whole_qkv, whole_out, whole_up, whole_down, whole_tcn_a, whole_tcn_b = (
        lax.all_gather(w, "sub", axis=0, tiled=True)
        for w in (w_qkv, w_out, w_up, w_down, temporal_weight_first, temporal_weight_second)
    )
    working = lax.all_to_all(frames, "cell", split_axis=0, concat_axis=1, tiled=True)
    frame_count, cells_here = (working.shape[0], working.shape[1])
    residual = working.astype(jnp.float32)
    normed = normalize(residual).astype(jnp.bfloat16).reshape(-1, features)
    projected = jnp.dot(normed, whole_qkv, preferred_element_type=jnp.float32).astype(jnp.bfloat16)
    projected = projected.reshape(frame_count, cells_here, 3 * features)
    attended = attend(
        projected[..., :features],
        projected[..., features : 2 * features],
        projected[..., 2 * features :],
    )
    out_part = jnp.dot(
        attended.reshape(-1, features), whole_out, preferred_element_type=jnp.float32
    )
    mid_state = (residual + out_part.reshape(frame_count, cells_here, features)).astype(
        jnp.bfloat16
    )
    mid_float = lax.optimization_barrier(mid_state).astype(jnp.float32)
    normed_two = normalize(mid_float).astype(jnp.bfloat16).reshape(-1, features)
    hidden = jax.nn.gelu(jnp.dot(normed_two, whole_up, preferred_element_type=jnp.float32)).astype(
        jnp.bfloat16
    )
    down_part = jnp.dot(hidden, whole_down, preferred_element_type=jnp.float32).reshape(
        frame_count, cells_here, features
    )
    sectioned_frames = (mid_float + down_part).astype(jnp.bfloat16)
    sectioned_frames = lax.all_to_all(
        sectioned_frames, "cell", split_axis=1, concat_axis=0, tiled=True
    )
    padded_frames = with_halo(sectioned_frames, ((("tm", "sub"), 0),), DILATION_FIRST)
    earlier = padded_frames[:frames_local]
    later_frames = padded_frames[2 * DILATION_FIRST : 2 * DILATION_FIRST + frames_local]
    opening_layer = gated_step(sectioned_frames, earlier, later_frames, whole_tcn_a)
    shard_step_count = DILATION_SECOND // frames_local
    far_earlier = shifted(opening_layer, ("tm", "sub"), shard_step_count)
    far_later = shifted(opening_layer, ("tm", "sub"), -shard_step_count)
    return gated_step(opening_layer, far_earlier, far_later, whole_tcn_b)


ANYWHERE = pl.BlockSpec(memory_space=pl.ANY)
RESIDENT = pl.BlockSpec(memory_space=pltpu.VMEM)
SCALARS = pl.BlockSpec(memory_space=pltpu.SMEM)


def params(mib):
    return pltpu.CompilerParams(vmem_limit_bytes=mib * MIB)


def moved(count):
    return pl.CostEstimate(flops=0, bytes_accessed=count, transcendentals=0)


def pack_weights_kernel(counts, before, *refs):
    sources, packed = refs[: sum(counts)], refs[sum(counts) :]
    for count, target in zip(counts, packed):
        group, sources = sources[:count], sources[count:]
        width = target.shape[1]
        at = 0
        for source in group:
            rows = source.shape[0]
            for column in range(0, source.shape[1], width):
                target[at : at + rows] = source[:, column : column + width]
                at += rows


def pack_weights(before, groups, width):
    flat = [w for group in groups for w in group]
    rows = [sum(w.size for w in group) // width for group in groups]
    return pl.pallas_call(
        functools.partial(pack_weights_kernel, tuple(len(group) for group in groups)),
        out_shape=[jax.ShapeDtypeStruct((count, width), flat[0].dtype) for count in rows],
        in_specs=[ANYWHERE] + [RESIDENT] * len(flat),
        out_specs=[RESIDENT] * len(groups),
        compiler_params=params(8),
        cost_estimate=moved(sum(rows) * width),
        name="pack_weights",
    )(before, *flat)


def join_weights_kernel(counts, place, before, *refs):
    packed, wholes = refs[: 2 * len(counts)], refs[2 * len(counts) :]
    for index, count in enumerate(counts):
        group, wholes = wholes[:count], wholes[count:]
        mine, other = packed[2 * index : 2 * index + 2]
        width = mine.shape[1]
        for source, core in ((mine, place[0]), (other, 1 - place[0])):
            at = 0
            for whole in group:
                rows = whole.shape[0] // 2
                spot = pl.ds(pl.multiple_of(core * rows, 16), rows)
                for column in range(0, whole.shape[1], width):
                    whole[spot, column : column + width] = source[at : at + rows]
                    at += rows


def join_weights(place, before, packed, groups):
    flat = [w for group in groups for w in group]
    return pl.pallas_call(
        functools.partial(join_weights_kernel, tuple(len(group) for group in groups)),
        out_shape=[jax.ShapeDtypeStruct((2 * w.shape[0], w.shape[1]), w.dtype) for w in flat],
        in_specs=[SCALARS, ANYWHERE] + [RESIDENT] * (2 * len(groups)),
        out_specs=[RESIDENT] * len(flat),
        compiler_params=params(8),
        cost_estimate=moved(sum(w.size for w in flat)),
        name="join_weights",
    )(place, before, *[half for pair in packed for half in pair])


def pack_kernel(place, before, *refs):
    half = len(refs) // 2
    for source, packed in zip(refs[:half], refs[half:]):
        packed[...] = source[...]


def run_pack(place, before, grouped, begin, count):
    slots, _, cells, features = grouped.shape
    shape = (slots, 1, cells, features)

    def source(delta):
        return pl.BlockSpec(
            shape, lambda i, at: (0, begin + (at[4] ^ delta) * count + i, 0, 0)
        )

    return pl.pallas_call(
        pack_kernel,
        grid_spec=pltpu.PrefetchScalarGridSpec(
            num_scalar_prefetch=1,
            grid=(count,),
            in_specs=[ANYWHERE] + [source(delta) for delta in (1, 2, 3)],
            out_specs=[pl.BlockSpec(shape, lambda i, at: (0, i, 0, 0))] * 3,
        ),
        out_shape=[jax.ShapeDtypeStruct((slots, count, cells, features), grouped.dtype)] * 3,
        compiler_params=params(4),
        cost_estimate=moved(3 * slots * count * cells * features),
        name="pack",
    )(place, before, grouped, grouped, grouped)


def section_kernel(
    place,
    before,
    own,
    near_cells,
    far_own,
    far_cells,
    w_qkv,
    w_out,
    w_up,
    w_down,
    even_ref,
    odd_ref,
):
    features = own.shape[-1]
    cells = 2 * own.shape[2]
    parts = []
    for mine, other in ((own, near_cells), (far_own, far_cells)):
        for slot in range(2):
            parts += [mine[slot, 0], other[slot, 0]]
    residual = jnp.concatenate(parts, axis=0).astype(jnp.float32)
    frame_count = 4
    normed = normalize(residual).astype(jnp.bfloat16)
    projected = jnp.dot(normed, w_qkv[...], preferred_element_type=jnp.float32).astype(jnp.bfloat16)
    pair_width = 2 * HEAD_DIM
    low = lax.broadcasted_iota(jnp.int32, (cells, pair_width), 1) < HEAD_DIM
    low_one = low.astype(jnp.bfloat16)
    high_one = 1 - low_one
    scale = HEAD_DIM ** (-0.5) * math.log2(math.e)
    rows = []
    for frame in range(frame_count):
        block = projected[frame * cells : (frame + 1) * cells]
        columns = []
        for pair in range(features // pair_width):
            at = pair * pair_width
            queries = block[:, at : at + pair_width]
            keys = block[:, features + at : features + at + pair_width]
            values = block[:, 2 * features + at : 2 * features + at + pair_width]
            split_keys = jnp.concatenate([keys * low_one, keys * high_one], axis=0)
            scores = lax.dot_general(
                queries, split_keys, (((1,), (1,)), ((), ())), preferred_element_type=jnp.float32
            )
            terms = []
            for head in range(2):
                own_scores = scores[:, head * cells : (head + 1) * cells]
                row_max = jnp.max(own_scores, axis=-1, keepdims=True)
                terms.append(jnp.exp2((own_scores - row_max) * scale).astype(jnp.bfloat16))
            split_values = jnp.concatenate(
                [
                    jnp.concatenate([values * low_one, low_one], axis=1),
                    jnp.concatenate([values * high_one, high_one], axis=1),
                ],
                axis=0,
            )
            mixed = jnp.dot(
                jnp.concatenate(terms, axis=1), split_values, preferred_element_type=jnp.float32
            )
            columns.append((mixed[:, :pair_width] / mixed[:, pair_width:]).astype(jnp.bfloat16))
        rows.append(jnp.concatenate(columns, axis=1))
    attended = jnp.concatenate(rows, axis=0)

    mid_state = (
        residual + jnp.dot(attended, w_out[...], preferred_element_type=jnp.float32)
    ).astype(jnp.bfloat16)
    mid_float = mid_state.astype(jnp.float32)
    normed_two = normalize(mid_float).astype(jnp.bfloat16)
    total = mid_float
    width = features
    for at in range(0, w_up.shape[1], width):
        lifted = jnp.dot(normed_two, w_up[:, at : at + width], preferred_element_type=jnp.float32)
        inner = lifted * (
            math.sqrt(2 / math.pi) + (math.sqrt(2 / math.pi) * 0.044715) * (lifted * lifted)
        )
        halved = 0.5 * lifted
        hidden = (halved + halved * jnp.tanh(inner)).astype(jnp.bfloat16)
        total = total + jnp.dot(hidden, w_down[at : at + width], preferred_element_type=jnp.float32)
    sectioned = total.astype(jnp.bfloat16)
    for block in range(2):
        even_ref[block, 0] = sectioned[(2 * block) * cells : (2 * block + 1) * cells]
        odd_ref[block, 0] = sectioned[(2 * block + 1) * cells : (2 * block + 2) * cells]


def gate(center, preact):
    features = center.shape[-1]
    gated = jnp.tanh(preact[:, :features]) * (
        0.5 + 0.5 * jnp.tanh(0.5 * preact[:, features:])
    )
    return (center.astype(jnp.float32) + gated).astype(jnp.bfloat16)


def temporal_kernel(
    place,
    before,
    even,
    odd,
    left_odd,
    right_even,
    w_first,
    w_second,
    out0,
    out1,
    out2,
    out3,
):
    near, is_first, is_last = place[1], place[2], place[3]
    far = 1 - near
    features = even.shape[-1]
    cells = even.shape[2]
    zero = jnp.zeros((cells, features), even.dtype)
    even_n, odd_n, even_f, odd_f = even[near, 0], odd[near, 0], even[far, 0], odd[far, 0]
    left_n = jnp.where(is_first == 1, zero, left_odd[near, 0])
    left_f = left_odd[jnp.where(is_first == 1, near, far), 0]
    right_n = right_even[jnp.where(is_last == 1, far, near), 0]
    right_f = jnp.where(is_last == 1, zero, right_even[far, 0])
    center = jnp.concatenate([even_n, odd_n, even_f, odd_f], axis=0)
    stacked = jnp.concatenate(
        [
            jnp.concatenate([left_n, even_n, left_f, even_f], axis=0),
            center,
            jnp.concatenate([odd_n, right_n, odd_f, right_f], axis=0),
        ],
        axis=1,
    )
    opening = gate(center, jnp.dot(stacked, w_first[...], preferred_element_type=jnp.float32))
    rows = 2 * cells
    near_part, far_part = opening[:rows], opening[rows:]
    both = jnp.concatenate([near_part, far_part], axis=1)
    result_n = gate(
        near_part, jnp.dot(both, w_second[features:], preferred_element_type=jnp.float32)
    )
    result_f = gate(
        far_part, jnp.dot(both, w_second[: 2 * features], preferred_element_type=jnp.float32)
    )
    same = jnp.where(near == 0, result_n, result_f)
    other = jnp.where(near == 0, result_f, result_n)
    half = cells // 2
    for slot in range(2):
        at = slot * cells
        out0[slot, 0] = same[at : at + half]
        out1[slot, 0] = same[at + half : at + cells]
        out2[slot, 0] = other[at : at + half]
        out3[slot, 0] = other[at + half : at + cells]


def run_section(place, before, grouped, begin, pieces, weights):
    slots, count, cells, features = pieces[0].shape
    ff = weights[2].shape[1]
    shape_in = (slots, 1, cells, features)
    own = pl.BlockSpec(shape_in, lambda i, at: (0, begin + at[4] * count + i, 0, 0))
    block_in = pl.BlockSpec(shape_in, lambda i, at: (0, i, 0, 0))
    block_out = pl.BlockSpec((2, 1, 2 * cells, features), lambda i, at: (0, i, 0, 0))
    shape = jax.ShapeDtypeStruct((2, count, 2 * cells, features), jnp.bfloat16)
    tokens = 2 * slots * count * 2 * cells
    macs = tokens * (features * (4 * features + 2 * ff) + 4 * cells * features)
    return pl.pallas_call(
        section_kernel,
        grid_spec=pltpu.PrefetchScalarGridSpec(
            num_scalar_prefetch=1,
            grid=(count,),
            in_specs=[ANYWHERE, own] + [block_in] * 3 + [RESIDENT] * 4,
            out_specs=[block_out, block_out],
        ),
        out_shape=[shape, shape],
        compiler_params=params(16),
        cost_estimate=pl.CostEstimate(
            flops=macs // 8, bytes_accessed=tokens * features, transcendentals=0
        ),
        name="section",
    )(place, before, grouped, *pieces, *weights)


def run_temporal(place, before, even, odd, left_odd, right_even, weights):
    blocks, count, cells, features = even.shape
    block_in = pl.BlockSpec((blocks, 1, cells, features), lambda i, at: (0, i, 0, 0))
    block_out = pl.BlockSpec((2, 1, cells // 2, features), lambda i, at: (0, i, 0, 0))
    shape = jax.ShapeDtypeStruct((2, count, cells // 2, features), jnp.bfloat16)
    tokens = 2 * blocks * count * cells
    return pl.pallas_call(
        temporal_kernel,
        grid_spec=pltpu.PrefetchScalarGridSpec(
            num_scalar_prefetch=1,
            grid=(count,),
            in_specs=[ANYWHERE] + [block_in] * 4 + [RESIDENT] * 2,
            out_specs=[block_out] * 4,
        ),
        out_shape=[shape] * 4,
        compiler_params=params(16),
        cost_estimate=pl.CostEstimate(
            flops=tokens * features * features // 4,
            bytes_accessed=tokens * features,
            transcendentals=0,
        ),
        name="temporal",
    )(place, before, even, odd, left_odd, right_even, *weights)


GROUP = ("far", "cell")
RING = ("near", "sub")


def paired(frames, w_qkv, w_out, w_up, w_down, temporal_weight_first, temporal_weight_second):
    frames_local, cells, features = frames.shape
    near_size, subs = lax.axis_size("near"), lax.axis_size("sub")
    sub, side = lax.axis_index("sub"), lax.axis_index("far")
    quarter = 2 * side + lax.axis_index("cell")
    ring = near_size * subs
    position = lax.axis_index("near") * subs + sub
    place = jnp.stack([sub, side, position == 0, position == ring - 1, quarter]).astype(jnp.int32)
    rightward = [(i, (i + 1) % ring) for i in range(ring)]
    leftward = [(target, source) for source, target in rightward]
    slots = frames_local // DILATION_FIRST
    grouped = frames.reshape(slots, DILATION_FIRST, cells, features)
    begins = [4 * sum(CHUNKS[:index]) for index in range(len(CHUNKS))]

    def exchange(piece, delta):
        return lax.ppermute(piece, GROUP, [(i, i ^ delta) for i in range(4)])

    pinned = pltpu.with_memory_space_constraint(grouped, pltpu.HBM)

    def send(before, index):
        cut = run_pack(place, before, pinned, begins[index], CHUNKS[index])
        return cut[0], [exchange(piece, delta) for delta, piece in zip((1, 2, 3), cut)]

    def swap_core(packed):
        return packed, lax.ppermute(packed, "sub", [(0, 1), (1, 0)])

    section_halves = (w_qkv, w_out, w_up, w_down)
    temporal_halves = (temporal_weight_first, temporal_weight_second)
    halves = (section_halves, temporal_halves)
    arrived = {}
    before, arrived[0] = send(place, 0)
    packed = pack_weights(before, halves, features)
    before = packed[0]
    for index in range(1, len(CHUNKS)):
        before, arrived[index] = send(before, index)
    joined = join_weights(place, before, [swap_core(w) for w in packed], halves)
    section_weights, temporal_weights = joined[:4], joined[4:]

    waiting, outs = {}, {}
    before = joined[0]
    for kind, index in ORDER:
        if kind == "s":
            even, odd = run_section(
                place, before, pinned, begins[index], arrived[index], section_weights
            )
            left_odd = lax.ppermute(odd, RING, rightward)
            right_even = lax.ppermute(even, RING, leftward)
            waiting[index] = (even, odd, left_odd, right_even)
            before = even
        else:
            sent = run_temporal(place, before, *waiting[index], temporal_weights)
            outs[index] = [sent[0]] + [exchange(sent[delta], delta) for delta in (1, 2, 3)]
            before = sent[0]
    result = jnp.zeros_like(grouped)
    for index, count in enumerate(CHUNKS):
        for delta in range(4):
            result = lax.dynamic_update_slice_in_dim(
                result, outs[index][delta], begins[index] + (quarter ^ delta) * count, axis=1
            )
    return result.reshape(frames.shape)


def solution(mesh):
    groups, tm, cell, sub = (mesh.shape[axis] for axis in ("groups", "tm", "cell", "sub"))

    def run(frames, *weights):
        frame_total, cells, _ = frames.shape
        video = frame_total // groups
        frames_local = video // (tm * sub)
        fits = (
            video == 2 * DILATION_SECOND
            and frames_local == 2 * DILATION_FIRST
            and tm % 2 == 0
            and cell == 2
            and sub == 2
            and (cells // cell) % 16 == 0
            and DILATION_FIRST == 4 * sum(CHUNKS)
        )
        if fits:
            devices = mesh.devices.reshape(groups, 2, tm // 2, cell, sub)
            axes = ("groups", "far", "near", "cell", "sub")
            used, split, body = jax.sharding.Mesh(devices, axes), ("groups", "far", "near", "sub"), paired
        else:
            used, split, body = mesh, ("groups", "tm", "sub"), general
        return jax.shard_map(
            body,
            mesh=used,
            in_specs=(P(split, "cell", None),) + (P("sub", None),) * 6,
            out_specs=P(split, "cell", None),
            check_vma=False,
        )(frames, *weights)

    return run
```

```python
import functools
import math

import jax
import jax.numpy as jnp
from jax import lax
from jax.experimental import pallas as pl
from jax.experimental.pallas import tpu as pltpu
from jax.sharding import PartitionSpec as P

HEAD_DIM = 64
DILATION_FIRST = 16
DILATION_SECOND = 256
CHUNKS = (2, 2)
ORDER = (("s", 0), ("s", 1), ("t", 0), ("t", 1))
MIB = 1024 * 1024


def with_halo(block, sides, width):
    for axis, dim in sides:
        count = lax.axis_size(axis)
        forward = [(i, i + 1) for i in range(count - 1)]
        backward = [(target, source) for source, target in forward]
        low = lax.ppermute(
            lax.slice_in_dim(block, block.shape[dim] - width, None, axis=dim), axis, forward
        )
        high = lax.ppermute(lax.slice_in_dim(block, 0, width, axis=dim), axis, backward)
        block = jnp.concatenate([low, block, high], axis=dim)
    return block


def shifted(shard, axis, by):
    size = lax.axis_size(axis)
    pairs = [(i, i + by) for i in range(size) if 0 <= i + by < size]
    return lax.ppermute(shard, axis, pairs)


def normalize(values):
    row_mean = jnp.mean(values, axis=-1, keepdims=True)
    centred = values - row_mean
    row_var = jnp.mean(centred * centred, axis=-1, keepdims=True)
    return centred * lax.rsqrt(row_var + 1e-05)


def attend(queries, key_part, value_part):
    frame_count, q_cells, features = queries.shape
    head_count = features // HEAD_DIM
    q_heads = queries.reshape(frame_count, q_cells, head_count, HEAD_DIM)
    k_heads = key_part.reshape(frame_count, -1, head_count, HEAD_DIM)
    v_heads = value_part.reshape(frame_count, -1, head_count, HEAD_DIM)
    scores = jnp.einsum(
        "fqhd,fkhd->fhqk", q_heads, k_heads, preferred_element_type=jnp.float32
    ) * HEAD_DIM ** (-0.5)
    row_max = jnp.max(scores, axis=-1, keepdims=True)
    exp_terms = jnp.exp(scores - row_max)
    attn_probs = (exp_terms / jnp.sum(exp_terms, axis=-1, keepdims=True)).astype(jnp.bfloat16)
    mixed = jnp.einsum("fhqk,fkhd->fqhd", attn_probs, v_heads, preferred_element_type=jnp.float32)
    return mixed.astype(jnp.bfloat16).reshape(frame_count, q_cells, features)


def gated_step(center, earlier, later_frames, weight):
    features = center.shape[-1]
    stacked = jnp.concatenate([earlier, center, later_frames], axis=-1).reshape(-1, 3 * features)
    preact = jnp.dot(stacked, weight, preferred_element_type=jnp.float32)
    gated_part = jnp.tanh(preact[:, :features]) * jax.nn.sigmoid(preact[:, features:])
    return (center.astype(jnp.float32) + gated_part.reshape(center.shape)).astype(jnp.bfloat16)


def general(frames, w_qkv, w_out, w_up, w_down, temporal_weight_first, temporal_weight_second):
    frames_local, cell_rows, features = frames.shape
    whole_qkv, whole_out, whole_up, whole_down, whole_tcn_a, whole_tcn_b = (
        lax.all_gather(w, "sub", axis=0, tiled=True)
        for w in (w_qkv, w_out, w_up, w_down, temporal_weight_first, temporal_weight_second)
    )
    working = lax.all_to_all(frames, "cell", split_axis=0, concat_axis=1, tiled=True)
    frame_count, cells_here = (working.shape[0], working.shape[1])
    residual = working.astype(jnp.float32)
    normed = normalize(residual).astype(jnp.bfloat16).reshape(-1, features)
    projected = jnp.dot(normed, whole_qkv, preferred_element_type=jnp.float32).astype(jnp.bfloat16)
    projected = projected.reshape(frame_count, cells_here, 3 * features)
    attended = attend(
        projected[..., :features],
        projected[..., features : 2 * features],
        projected[..., 2 * features :],
    )
    out_part = jnp.dot(
        attended.reshape(-1, features), whole_out, preferred_element_type=jnp.float32
    )
    mid_state = (residual + out_part.reshape(frame_count, cells_here, features)).astype(
        jnp.bfloat16
    )
    mid_float = lax.optimization_barrier(mid_state).astype(jnp.float32)
    normed_two = normalize(mid_float).astype(jnp.bfloat16).reshape(-1, features)
    hidden = jax.nn.gelu(jnp.dot(normed_two, whole_up, preferred_element_type=jnp.float32)).astype(
        jnp.bfloat16
    )
    down_part = jnp.dot(hidden, whole_down, preferred_element_type=jnp.float32).reshape(
        frame_count, cells_here, features
    )
    sectioned_frames = (mid_float + down_part).astype(jnp.bfloat16)
    sectioned_frames = lax.all_to_all(
        sectioned_frames, "cell", split_axis=1, concat_axis=0, tiled=True
    )
    padded_frames = with_halo(sectioned_frames, ((("tm", "sub"), 0),), DILATION_FIRST)
    earlier = padded_frames[:frames_local]
    later_frames = padded_frames[2 * DILATION_FIRST : 2 * DILATION_FIRST + frames_local]
    opening_layer = gated_step(sectioned_frames, earlier, later_frames, whole_tcn_a)
    shard_step_count = DILATION_SECOND // frames_local
    far_earlier = shifted(opening_layer, ("tm", "sub"), shard_step_count)
    far_later = shifted(opening_layer, ("tm", "sub"), -shard_step_count)
    return gated_step(opening_layer, far_earlier, far_later, whole_tcn_b)


ANYWHERE = pl.BlockSpec(memory_space=pl.ANY)
RESIDENT = pl.BlockSpec(memory_space=pltpu.VMEM)
SCALARS = pl.BlockSpec(memory_space=pltpu.SMEM)


def params(mib):
    return pltpu.CompilerParams(vmem_limit_bytes=mib * MIB)


def moved(count):
    return pl.CostEstimate(flops=0, bytes_accessed=count, transcendentals=0)


def pack_weights_kernel(counts, before, *refs):
    sources, packed = refs[: sum(counts)], refs[sum(counts) :]
    for count, target in zip(counts, packed):
        group, sources = sources[:count], sources[count:]
        width = target.shape[1]
        at = 0
        for source in group:
            rows = source.shape[0]
            for column in range(0, source.shape[1], width):
                target[at : at + rows] = source[:, column : column + width]
                at += rows


def pack_weights(before, groups, width):
    flat = [w for group in groups for w in group]
    rows = [sum(w.size for w in group) // width for group in groups]
    return pl.pallas_call(
        functools.partial(pack_weights_kernel, tuple(len(group) for group in groups)),
        out_shape=[jax.ShapeDtypeStruct((count, width), flat[0].dtype) for count in rows],
        in_specs=[ANYWHERE] + [RESIDENT] * len(flat),
        out_specs=[RESIDENT] * len(groups),
        compiler_params=params(8),
        cost_estimate=moved(sum(rows) * width),
        name="pack_weights",
    )(before, *flat)


def join_weights_kernel(counts, place, before, *refs):
    packed, wholes = refs[: 2 * len(counts)], refs[2 * len(counts) :]
    for index, count in enumerate(counts):
        group, wholes = wholes[:count], wholes[count:]
        mine, other = packed[2 * index : 2 * index + 2]
        width = mine.shape[1]
        for source, core in ((mine, place[0]), (other, 1 - place[0])):
            at = 0
            for whole in group:
                rows = whole.shape[0] // 2
                spot = pl.ds(pl.multiple_of(core * rows, 16), rows)
                for column in range(0, whole.shape[1], width):
                    whole[spot, column : column + width] = source[at : at + rows]
                    at += rows


def join_weights(place, before, packed, groups):
    flat = [w for group in groups for w in group]
    return pl.pallas_call(
        functools.partial(join_weights_kernel, tuple(len(group) for group in groups)),
        out_shape=[jax.ShapeDtypeStruct((2 * w.shape[0], w.shape[1]), w.dtype) for w in flat],
        in_specs=[SCALARS, ANYWHERE] + [RESIDENT] * (2 * len(groups)),
        out_specs=[RESIDENT] * len(flat),
        compiler_params=params(8),
        cost_estimate=moved(sum(w.size for w in flat)),
        name="join_weights",
    )(place, before, *[half for pair in packed for half in pair])


def pack_kernel(place, before, *refs):
    half = len(refs) // 2
    for source, packed in zip(refs[:half], refs[half:]):
        packed[...] = source[...]


def run_pack(place, before, grouped, begin, count):
    slots, _, cells, features = grouped.shape
    shape = (slots, count, cells, features)

    def source(delta):
        return pl.BlockSpec(shape, lambda i, at: (0, begin // count + (at[4] ^ delta), 0, 0))

    return pl.pallas_call(
        pack_kernel,
        grid_spec=pltpu.PrefetchScalarGridSpec(
            num_scalar_prefetch=1,
            grid=(1,),
            in_specs=[ANYWHERE] + [source(delta) for delta in (1, 2, 3)],
            out_specs=[pl.BlockSpec(shape, lambda i, at: (0, 0, 0, 0))] * 3,
        ),
        out_shape=[jax.ShapeDtypeStruct((slots, count, cells, features), grouped.dtype)] * 3,
        compiler_params=params(6),
        cost_estimate=moved(3 * slots * count * cells * features),
        name="pack",
    )(place, before, grouped, grouped, grouped)


def section_kernel(
    place,
    before,
    own,
    near_cells,
    far_own,
    far_cells,
    w_qkv,
    w_out,
    w_up,
    w_down,
    even_ref,
    odd_ref,
):
    features = own.shape[-1]
    cells = 2 * own.shape[2]
    parts = []
    for mine, other in ((own, near_cells), (far_own, far_cells)):
        for slot in range(2):
            parts += [mine[slot, 0], other[slot, 0]]
    residual = jnp.concatenate(parts, axis=0).astype(jnp.float32)
    frame_count = 4
    normed = normalize(residual).astype(jnp.bfloat16)
    projected = jnp.dot(normed, w_qkv[...], preferred_element_type=jnp.float32).astype(jnp.bfloat16)
    pair_width = 2 * HEAD_DIM
    low = lax.broadcasted_iota(jnp.int32, (cells, pair_width), 1) < HEAD_DIM
    low_one = low.astype(jnp.bfloat16)
    high_one = 1 - low_one
    scale = HEAD_DIM ** (-0.5) * math.log2(math.e)
    rows = []
    for frame in range(frame_count):
        block = projected[frame * cells : (frame + 1) * cells]
        columns = []
        for pair in range(features // pair_width):
            at = pair * pair_width
            queries = block[:, at : at + pair_width]
            keys = block[:, features + at : features + at + pair_width]
            values = block[:, 2 * features + at : 2 * features + at + pair_width]
            split_keys = jnp.concatenate([keys * low_one, keys * high_one], axis=0)
            scores = lax.dot_general(
                queries, split_keys, (((1,), (1,)), ((), ())), preferred_element_type=jnp.float32
            )
            terms = []
            for head in range(2):
                own_scores = scores[:, head * cells : (head + 1) * cells]
                row_max = jnp.max(own_scores, axis=-1, keepdims=True)
                terms.append(jnp.exp2((own_scores - row_max) * scale).astype(jnp.bfloat16))
            split_values = jnp.concatenate(
                [
                    jnp.concatenate([values * low_one, low_one], axis=1),
                    jnp.concatenate([values * high_one, high_one], axis=1),
                ],
                axis=0,
            )
            mixed = jnp.dot(
                jnp.concatenate(terms, axis=1), split_values, preferred_element_type=jnp.float32
            )
            inverse = pl.reciprocal(mixed[:, pair_width:], approx=True)
            columns.append((mixed[:, :pair_width] * inverse).astype(jnp.bfloat16))
        rows.append(jnp.concatenate(columns, axis=1))
    attended = jnp.concatenate(rows, axis=0)

    mid_state = (
        residual + jnp.dot(attended, w_out[...], preferred_element_type=jnp.float32)
    ).astype(jnp.bfloat16)
    mid_float = mid_state.astype(jnp.float32)
    normed_two = normalize(mid_float).astype(jnp.bfloat16)
    total = mid_float
    width = math.gcd(w_up.shape[1], 512)
    for at in range(0, w_up.shape[1], width):
        lifted = jnp.dot(normed_two, w_up[:, at : at + width], preferred_element_type=jnp.float32)
        lifted = lifted.astype(jnp.bfloat16)
        inner = lifted * (
            math.sqrt(2 / math.pi) + (math.sqrt(2 / math.pi) * 0.044715) * (lifted * lifted)
        )
        halved = 0.5 * lifted
        hidden = halved + halved * jnp.tanh(inner)
        total = total + jnp.dot(hidden, w_down[at : at + width], preferred_element_type=jnp.float32)
    sectioned = total.astype(jnp.bfloat16)
    for block in range(2):
        even_ref[block, 0] = sectioned[(2 * block) * cells : (2 * block + 1) * cells]
        odd_ref[block, 0] = sectioned[(2 * block + 1) * cells : (2 * block + 2) * cells]


def gate(center, preact):
    features = center.shape[-1]
    preact = preact.astype(jnp.bfloat16)
    opened = 0.5 + 0.5 * jnp.tanh(0.5 * preact[:, features:])
    return center + jnp.tanh(preact[:, :features]) * opened


def temporal_kernel(
    place,
    before,
    even,
    odd,
    left_odd,
    right_even,
    w_first,
    w_second,
    out0,
    out1,
    out2,
    out3,
):
    near, is_first, is_last = place[1], place[2], place[3]
    far = 1 - near
    features = even.shape[-1]
    cells = even.shape[2]
    zero = jnp.zeros((cells, features), even.dtype)
    even_n, odd_n, even_f, odd_f = even[near, 0], odd[near, 0], even[far, 0], odd[far, 0]
    left_n = jnp.where(is_first == 1, zero, left_odd[near, 0])
    left_f = left_odd[jnp.where(is_first == 1, near, far), 0]
    right_n = right_even[jnp.where(is_last == 1, far, near), 0]
    right_f = jnp.where(is_last == 1, zero, right_even[far, 0])
    center = jnp.concatenate([even_n, odd_n, even_f, odd_f], axis=0)
    stacked = jnp.concatenate(
        [
            jnp.concatenate([left_n, even_n, left_f, even_f], axis=0),
            center,
            jnp.concatenate([odd_n, right_n, odd_f, right_f], axis=0),
        ],
        axis=1,
    )
    opening = gate(center, jnp.dot(stacked, w_first[...], preferred_element_type=jnp.float32))
    rows = 2 * cells
    near_part, far_part = opening[:rows], opening[rows:]
    both = jnp.concatenate([near_part, far_part], axis=1)
    result_n = gate(
        near_part, jnp.dot(both, w_second[features:], preferred_element_type=jnp.float32)
    )
    result_f = gate(
        far_part, jnp.dot(both, w_second[: 2 * features], preferred_element_type=jnp.float32)
    )
    same = jnp.where(near == 0, result_n, result_f)
    other = jnp.where(near == 0, result_f, result_n)
    half = cells // 2
    for slot in range(2):
        at = slot * cells
        out0[slot, 0] = same[at : at + half]
        out1[slot, 0] = same[at + half : at + cells]
        out2[slot, 0] = other[at : at + half]
        out3[slot, 0] = other[at + half : at + cells]


def run_section(place, before, grouped, begin, pieces, weights):
    slots, count, cells, features = pieces[0].shape
    ff = weights[2].shape[1]
    shape_in = (slots, 1, cells, features)
    own = pl.BlockSpec(shape_in, lambda i, at: (0, begin + at[4] * count + i, 0, 0))
    block_in = pl.BlockSpec(shape_in, lambda i, at: (0, i, 0, 0))
    block_out = pl.BlockSpec((2, 1, 2 * cells, features), lambda i, at: (0, i, 0, 0))
    shape = jax.ShapeDtypeStruct((2, count, 2 * cells, features), jnp.bfloat16)
    tokens = 2 * slots * count * 2 * cells
    macs = tokens * (features * (4 * features + 2 * ff) + 4 * cells * features)
    return pl.pallas_call(
        section_kernel,
        grid_spec=pltpu.PrefetchScalarGridSpec(
            num_scalar_prefetch=1,
            grid=(count,),
            in_specs=[ANYWHERE, own] + [block_in] * 3 + [RESIDENT] * 4,
            out_specs=[block_out, block_out],
        ),
        out_shape=[shape, shape],
        compiler_params=params(16),
        cost_estimate=pl.CostEstimate(
            flops=macs // 8, bytes_accessed=tokens * features, transcendentals=0
        ),
        name="section",
    )(place, before, grouped, *pieces, *weights)


def run_temporal(place, before, even, odd, left_odd, right_even, weights):
    blocks, count, cells, features = even.shape
    block_in = pl.BlockSpec((blocks, 1, cells, features), lambda i, at: (0, i, 0, 0))
    block_out = pl.BlockSpec((2, 1, cells // 2, features), lambda i, at: (0, i, 0, 0))
    shape = pltpu.HBM((2, count, cells // 2, features), jnp.bfloat16)
    tokens = 2 * blocks * count * cells
    return pl.pallas_call(
        temporal_kernel,
        grid_spec=pltpu.PrefetchScalarGridSpec(
            num_scalar_prefetch=1,
            grid=(count,),
            in_specs=[ANYWHERE] + [block_in] * 4 + [RESIDENT] * 2,
            out_specs=[block_out] * 4,
        ),
        out_shape=[shape] * 4,
        compiler_params=params(16),
        cost_estimate=pl.CostEstimate(
            flops=tokens * features * features // 4,
            bytes_accessed=tokens * features,
            transcendentals=0,
        ),
        name="temporal",
    )(place, before, even, odd, left_odd, right_even, *weights)


GROUP = ("far", "cell")
RING = ("near", "sub")


def paired(frames, w_qkv, w_out, w_up, w_down, temporal_weight_first, temporal_weight_second):
    frames_local, cells, features = frames.shape
    near_size, subs = lax.axis_size("near"), lax.axis_size("sub")
    sub, side = lax.axis_index("sub"), lax.axis_index("far")
    quarter = 2 * side + lax.axis_index("cell")
    ring = near_size * subs
    position = lax.axis_index("near") * subs + sub
    place = jnp.stack([sub, side, position == 0, position == ring - 1, quarter]).astype(jnp.int32)
    rightward = [(i, (i + 1) % ring) for i in range(ring)]
    leftward = [(target, source) for source, target in rightward]
    slots = frames_local // DILATION_FIRST
    grouped = frames.reshape(slots, DILATION_FIRST, cells, features)
    begins = [4 * sum(CHUNKS[:index]) for index in range(len(CHUNKS))]

    def exchange(piece, delta):
        return lax.ppermute(piece, GROUP, [(i, i ^ delta) for i in range(4)])

    pinned = pltpu.with_memory_space_constraint(grouped, pltpu.HBM)

    def send(before, index):
        cut = run_pack(place, before, pinned, begins[index], CHUNKS[index])
        return cut[0], [exchange(piece, delta) for delta, piece in zip((1, 2, 3), cut)]

    def swap_core(packed):
        return packed, lax.ppermute(packed, "sub", [(0, 1), (1, 0)])

    section_halves = (w_qkv, w_out, w_up, w_down)
    temporal_halves = (temporal_weight_first, temporal_weight_second)
    halves = (section_halves, temporal_halves)
    arrived = {}
    before, arrived[0] = send(place, 0)
    packed = pack_weights(before, halves, features)
    before = packed[0]
    for index in range(1, len(CHUNKS)):
        before, arrived[index] = send(before, index)
    joined = join_weights(place, before, [swap_core(w) for w in packed], halves)
    section_weights, temporal_weights = joined[:4], joined[4:]

    waiting, outs = {}, {}
    before = joined[0]
    for kind, index in ORDER:
        if kind == "s":
            even, odd = run_section(
                place, before, pinned, begins[index], arrived[index], section_weights
            )
            left_odd = lax.ppermute(odd, RING, rightward)
            right_even = lax.ppermute(even, RING, leftward)
            waiting[index] = (even, odd, left_odd, right_even)
            before = even
        else:
            sent = run_temporal(place, before, *waiting[index], temporal_weights)
            outs[index] = [sent[0]] + [exchange(sent[delta], delta) for delta in (1, 2, 3)]
            before = sent[0]
    result = jnp.zeros_like(grouped)
    for index, count in enumerate(CHUNKS):
        for delta in range(4):
            result = lax.dynamic_update_slice_in_dim(
                result, outs[index][delta], begins[index] + (quarter ^ delta) * count, axis=1
            )
    return result.reshape(frames.shape)


def solution(mesh):
    groups, tm, cell, sub = (mesh.shape[axis] for axis in ("groups", "tm", "cell", "sub"))

    def run(frames, *weights):
        frame_total, cells, _ = frames.shape
        video = frame_total // groups
        frames_local = video // (tm * sub)
        fits = (
            video == 2 * DILATION_SECOND
            and frames_local == 2 * DILATION_FIRST
            and tm % 2 == 0
            and cell == 2
            and sub == 2
            and (cells // cell) % 16 == 0
            and DILATION_FIRST == 4 * sum(CHUNKS)
        )
        if fits:
            devices = mesh.devices.reshape(groups, 2, tm // 2, cell, sub)
            axes = ("groups", "far", "near", "cell", "sub")
            used, split, body = jax.sharding.Mesh(devices, axes), ("groups", "far", "near", "sub"), paired
        else:
            used, split, body = mesh, ("groups", "tm", "sub"), general
        return jax.shard_map(
            body,
            mesh=used,
            in_specs=(P(split, "cell", None),) + (P("sub", None),) * 6,
            out_specs=P(split, "cell", None),
            check_vma=False,
        )(frames, *weights)

    return run
```

```python
import math

import jax
import jax.numpy as jnp
from jax import lax
from jax.experimental import pallas as pl
from jax.experimental.pallas import tpu as pltpu
from jax.sharding import PartitionSpec as P

HEAD_DIM = 64
DILATION_FIRST = 16
DILATION_SECOND = 256
CHUNKS = 2
MIB = 1024 * 1024


def with_halo(block, sides, width):
    for axis, dim in sides:
        count = lax.axis_size(axis)
        forward = [(i, i + 1) for i in range(count - 1)]
        backward = [(target, source) for source, target in forward]
        low = lax.ppermute(
            lax.slice_in_dim(block, block.shape[dim] - width, None, axis=dim), axis, forward
        )
        high = lax.ppermute(lax.slice_in_dim(block, 0, width, axis=dim), axis, backward)
        block = jnp.concatenate([low, block, high], axis=dim)
    return block


def shifted(shard, axis, by):
    size = lax.axis_size(axis)
    pairs = [(i, i + by) for i in range(size) if 0 <= i + by < size]
    return lax.ppermute(shard, axis, pairs)


def normalize(values):
    row_mean = jnp.mean(values, axis=-1, keepdims=True)
    centred = values - row_mean
    row_var = jnp.mean(centred * centred, axis=-1, keepdims=True)
    return centred * lax.rsqrt(row_var + 1e-05)


def attend(queries, key_part, value_part):
    frame_count, q_cells, features = queries.shape
    head_count = features // HEAD_DIM
    q_heads = queries.reshape(frame_count, q_cells, head_count, HEAD_DIM)
    k_heads = key_part.reshape(frame_count, -1, head_count, HEAD_DIM)
    v_heads = value_part.reshape(frame_count, -1, head_count, HEAD_DIM)
    scores = jnp.einsum(
        "fqhd,fkhd->fhqk", q_heads, k_heads, preferred_element_type=jnp.float32
    ) * HEAD_DIM ** (-0.5)
    row_max = jnp.max(scores, axis=-1, keepdims=True)
    exp_terms = jnp.exp(scores - row_max)
    attn_probs = (exp_terms / jnp.sum(exp_terms, axis=-1, keepdims=True)).astype(jnp.bfloat16)
    mixed = jnp.einsum("fhqk,fkhd->fqhd", attn_probs, v_heads, preferred_element_type=jnp.float32)
    return mixed.astype(jnp.bfloat16).reshape(frame_count, q_cells, features)


def gated_step(center, earlier, later_frames, weight):
    features = center.shape[-1]
    stacked = jnp.concatenate([earlier, center, later_frames], axis=-1).reshape(-1, 3 * features)
    preact = jnp.dot(stacked, weight, preferred_element_type=jnp.float32)
    gated_part = jnp.tanh(preact[:, :features]) * jax.nn.sigmoid(preact[:, features:])
    return (center.astype(jnp.float32) + gated_part.reshape(center.shape)).astype(jnp.bfloat16)


def general(frames, w_qkv, w_out, w_up, w_down, temporal_weight_first, temporal_weight_second):
    frames_local, cell_rows, features = frames.shape
    whole_qkv, whole_out, whole_up, whole_down, whole_tcn_a, whole_tcn_b = (
        lax.all_gather(w, "sub", axis=0, tiled=True)
        for w in (w_qkv, w_out, w_up, w_down, temporal_weight_first, temporal_weight_second)
    )
    working = lax.all_to_all(frames, "cell", split_axis=0, concat_axis=1, tiled=True)
    frame_count, cells_here = (working.shape[0], working.shape[1])
    residual = working.astype(jnp.float32)
    normed = normalize(residual).astype(jnp.bfloat16).reshape(-1, features)
    projected = jnp.dot(normed, whole_qkv, preferred_element_type=jnp.float32).astype(jnp.bfloat16)
    projected = projected.reshape(frame_count, cells_here, 3 * features)
    attended = attend(
        projected[..., :features],
        projected[..., features : 2 * features],
        projected[..., 2 * features :],
    )
    out_part = jnp.dot(
        attended.reshape(-1, features), whole_out, preferred_element_type=jnp.float32
    )
    mid_state = (residual + out_part.reshape(frame_count, cells_here, features)).astype(
        jnp.bfloat16
    )
    mid_float = lax.optimization_barrier(mid_state).astype(jnp.float32)
    normed_two = normalize(mid_float).astype(jnp.bfloat16).reshape(-1, features)
    hidden = jax.nn.gelu(jnp.dot(normed_two, whole_up, preferred_element_type=jnp.float32)).astype(
        jnp.bfloat16
    )
    down_part = jnp.dot(hidden, whole_down, preferred_element_type=jnp.float32).reshape(
        frame_count, cells_here, features
    )
    sectioned_frames = (mid_float + down_part).astype(jnp.bfloat16)
    sectioned_frames = lax.all_to_all(
        sectioned_frames, "cell", split_axis=1, concat_axis=0, tiled=True
    )
    padded_frames = with_halo(sectioned_frames, ((("tm", "sub"), 0),), DILATION_FIRST)
    earlier = padded_frames[:frames_local]
    later_frames = padded_frames[2 * DILATION_FIRST : 2 * DILATION_FIRST + frames_local]
    opening_layer = gated_step(sectioned_frames, earlier, later_frames, whole_tcn_a)
    shard_step_count = DILATION_SECOND // frames_local
    far_earlier = shifted(opening_layer, ("tm", "sub"), shard_step_count)
    far_later = shifted(opening_layer, ("tm", "sub"), -shard_step_count)
    return gated_step(opening_layer, far_earlier, far_later, whole_tcn_b)


ANYWHERE = pl.BlockSpec(memory_space=pl.ANY)
RESIDENT = pl.BlockSpec(memory_space=pltpu.VMEM)
SCALARS = pl.BlockSpec(memory_space=pltpu.SMEM)


def params(mib):
    return pltpu.CompilerParams(vmem_limit_bytes=mib * MIB)


def moved(count):
    return pl.CostEstimate(flops=0, bytes_accessed=count, transcendentals=0)


def pack_weights_kernel(before, *refs):
    *sources, packed = refs
    width = packed.shape[1]
    at = 0
    for source in sources:
        rows = source.shape[0]
        for column in range(0, source.shape[1], width):
            packed[at : at + rows] = source[:, column : column + width]
            at += rows


def pack_weights(before, weights, width):
    rows = sum(w.size for w in weights) // width
    return pl.pallas_call(
        pack_weights_kernel,
        out_shape=jax.ShapeDtypeStruct((rows, width), weights[0].dtype),
        in_specs=[ANYWHERE] + [RESIDENT] * len(weights),
        out_specs=RESIDENT,
        compiler_params=params(8),
        cost_estimate=moved(rows * width),
        name="pack_weights",
    )(before, *weights)


def join_weights_kernel(place, before, mine, other, *wholes):
    width = mine.shape[1]
    for source, core in ((mine, place[0]), (other, 1 - place[0])):
        at = 0
        for whole in wholes:
            rows = whole.shape[0] // 2
            spot = pl.ds(pl.multiple_of(core * rows, 16), rows)
            for column in range(0, whole.shape[1], width):
                whole[spot, column : column + width] = source[at : at + rows]
                at += rows


def join_weights(place, before, mine, other, halves):
    return pl.pallas_call(
        join_weights_kernel,
        out_shape=[jax.ShapeDtypeStruct((2 * w.shape[0], w.shape[1]), w.dtype) for w in halves],
        in_specs=[SCALARS, ANYWHERE, RESIDENT, RESIDENT],
        out_specs=[RESIDENT] * len(halves),
        compiler_params=params(8),
        cost_estimate=moved(mine.size),
        name="join_weights",
    )(place, before, mine, other)


def pack_kernel(place, before, *refs):
    half = len(refs) // 2
    for source, packed in zip(refs[:half], refs[half:]):
        packed[...] = source[...]


def run_pack(place, before, grouped, units, first, chunks, deltas):
    slots, _, cells, features = grouped.shape
    shape = (slots, units, cells, features)

    def source(delta):
        return pl.BlockSpec(shape, lambda i, at: (0, 4 * (first + i) + (at[4] ^ delta), 0, 0))

    out = jax.ShapeDtypeStruct((slots, chunks * units, cells, features), grouped.dtype)
    return pl.pallas_call(
        pack_kernel,
        grid_spec=pltpu.PrefetchScalarGridSpec(
            num_scalar_prefetch=1,
            grid=(chunks,),
            in_specs=[ANYWHERE] + [source(delta) for delta in deltas],
            out_specs=[pl.BlockSpec(shape, lambda i, at: (0, i, 0, 0))] * len(deltas),
        ),
        out_shape=[out] * len(deltas),
        compiler_params=params(6),
        cost_estimate=moved(len(deltas) * slots * units * cells * features),
        name="pack",
    )(place, before, *[grouped] * len(deltas))


def section_kernel(
    place,
    before,
    mine,
    other,
    w_qkv,
    w_out,
    w_up,
    w_down,
    even_ref,
    odd_ref,
):
    slots, units, half, features = mine.shape
    cells = 2 * half
    parts = []
    for slot in range(slots):
        for unit in range(units):
            parts += [mine[slot, unit], other[slot, unit]]
    residual = jnp.concatenate(parts, axis=0).astype(jnp.float32)
    frame_count = slots * units
    normed = normalize(residual).astype(jnp.bfloat16)
    projected = jnp.dot(normed, w_qkv[...], preferred_element_type=jnp.float32).astype(jnp.bfloat16)
    pair_width = 2 * HEAD_DIM
    low = lax.broadcasted_iota(jnp.int32, (cells, pair_width), 1) < HEAD_DIM
    low_one = low.astype(jnp.bfloat16)
    high_one = 1 - low_one
    scale = HEAD_DIM ** (-0.5) * math.log2(math.e)
    rows = []
    for frame in range(frame_count):
        block = projected[frame * cells : (frame + 1) * cells]
        columns = []
        for pair in range(features // pair_width):
            at = pair * pair_width
            queries = block[:, at : at + pair_width]
            keys = block[:, features + at : features + at + pair_width]
            values = block[:, 2 * features + at : 2 * features + at + pair_width]
            split_keys = jnp.concatenate([keys * low_one, keys * high_one], axis=0)
            scores = lax.dot_general(
                queries, split_keys, (((1,), (1,)), ((), ())), preferred_element_type=jnp.float32
            )
            terms = []
            for head in range(2):
                own_scores = scores[:, head * cells : (head + 1) * cells]
                row_max = jnp.max(own_scores, axis=-1, keepdims=True)
                terms.append(jnp.exp2((own_scores - row_max) * scale).astype(jnp.bfloat16))
            split_values = jnp.concatenate(
                [
                    jnp.concatenate([values * low_one, low_one], axis=1),
                    jnp.concatenate([values * high_one, high_one], axis=1),
                ],
                axis=0,
            )
            mixed = jnp.dot(
                jnp.concatenate(terms, axis=1), split_values, preferred_element_type=jnp.float32
            )
            inverse = pl.reciprocal(mixed[:, pair_width:], approx=True)
            columns.append((mixed[:, :pair_width] * inverse).astype(jnp.bfloat16))
        rows.append(jnp.concatenate(columns, axis=1))
    attended = jnp.concatenate(rows, axis=0)

    mid_state = (
        residual + jnp.dot(attended, w_out[...], preferred_element_type=jnp.float32)
    ).astype(jnp.bfloat16)
    mid_float = mid_state.astype(jnp.float32)
    normed_two = normalize(mid_float).astype(jnp.bfloat16)
    total = mid_float
    width = math.gcd(w_up.shape[1], 512)
    for at in range(0, w_up.shape[1], width):
        lifted = jnp.dot(normed_two, w_up[:, at : at + width], preferred_element_type=jnp.float32)
        lifted = lifted.astype(jnp.bfloat16)
        inner = lifted * (
            math.sqrt(2 / math.pi) + (math.sqrt(2 / math.pi) * 0.044715) * (lifted * lifted)
        )
        halved = 0.5 * lifted
        hidden = halved + halved * jnp.tanh(inner)
        total = total + jnp.dot(hidden, w_down[at : at + width], preferred_element_type=jnp.float32)
    sectioned = total.astype(jnp.bfloat16)
    for unit in range(units):
        even_ref[unit] = sectioned[unit * cells : (unit + 1) * cells]
        odd_ref[unit] = sectioned[(units + unit) * cells : (units + unit + 1) * cells]


def gate(center, preact):
    features = center.shape[-1]
    preact = preact.astype(jnp.bfloat16)
    opened = 0.5 + 0.5 * jnp.tanh(0.5 * preact[:, features:])
    return center + jnp.tanh(preact[:, :features]) * opened


def temporal_kernel(place, before, *refs):
    *fields, w_first, w_second, out0, out1, out2, out3 = refs
    near, is_first, is_last = place[1], place[2], place[3]
    cells, features = fields[0].shape[1:]
    zero = jnp.zeros((cells, features), fields[0].dtype)
    pairs = [(fields[i][0], fields[i + 4][0]) for i in range(4)]
    even_n, odd_n, left_a, right_a = [jnp.where(near == 0, a, b) for a, b in pairs]
    even_f, odd_f, left_b, right_b = [jnp.where(near == 0, b, a) for a, b in pairs]
    left_n = jnp.where(is_first == 1, zero, left_a)
    left_f = jnp.where(is_first == 1, left_a, left_b)
    right_n = jnp.where(is_last == 1, right_b, right_a)
    right_f = jnp.where(is_last == 1, zero, right_b)
    center = jnp.concatenate([even_n, odd_n, even_f, odd_f], axis=0)
    stacked = jnp.concatenate(
        [
            jnp.concatenate([left_n, even_n, left_f, even_f], axis=0),
            center,
            jnp.concatenate([odd_n, right_n, odd_f, right_f], axis=0),
        ],
        axis=1,
    )
    opening = gate(center, jnp.dot(stacked, w_first[...], preferred_element_type=jnp.float32))
    rows = 2 * cells
    near_part, far_part = opening[:rows], opening[rows:]
    both = jnp.concatenate([near_part, far_part], axis=1)
    result_n = gate(
        near_part, jnp.dot(both, w_second[features:], preferred_element_type=jnp.float32)
    )
    result_f = gate(
        far_part, jnp.dot(both, w_second[: 2 * features], preferred_element_type=jnp.float32)
    )
    same = jnp.where(near == 0, result_n, result_f)
    other = jnp.where(near == 0, result_f, result_n)
    half = cells // 2
    for slot in range(2):
        at = slot * cells
        out0[slot, 0] = same[at : at + half]
        out1[slot, 0] = same[at + half : at + cells]
        out2[slot, 0] = other[at : at + half]
        out3[slot, 0] = other[at + half : at + cells]


def run_section(place, before, mine, other, weights, units, chunks, from_frames):
    slots, _, half, features = mine.shape
    shape_in = (slots, units, half, features)
    piece = pl.BlockSpec(shape_in, lambda i, at: (0, i, 0, 0))
    own = pl.BlockSpec(shape_in, lambda i, at: (0, 4 * i + at[4], 0, 0))
    block_out = pl.BlockSpec((units, 2 * half, features), lambda i, at: (i, 0, 0))
    place_out = pltpu.HBM if from_frames else jax.ShapeDtypeStruct
    shape = place_out((chunks * units, 2 * half, features), jnp.bfloat16)
    return pl.pallas_call(
        section_kernel,
        grid_spec=pltpu.PrefetchScalarGridSpec(
            num_scalar_prefetch=1,
            grid=(chunks,),
            in_specs=[ANYWHERE, own if from_frames else piece, piece] + [RESIDENT] * 4,
            out_specs=[block_out, block_out],
        ),
        out_shape=[shape, shape],
        compiler_params=params(16),
        cost_estimate=moved(chunks * units * half * features),
        name="section",
    )(place, before, mine, other, *weights)


def run_temporal(place, before, own, far, weights, begin, count):
    _, cells, features = own[0].shape
    block_own = pl.BlockSpec((1, cells, features), lambda i, at: (begin + i, 0, 0))
    block_far = pl.BlockSpec((1, cells, features), lambda i, at: (i, 0, 0))
    block_out = pl.BlockSpec((2, 1, cells // 2, features), lambda i, at: (0, i, 0, 0))
    shape = pltpu.HBM((2, count, cells // 2, features), jnp.bfloat16)
    return pl.pallas_call(
        temporal_kernel,
        grid_spec=pltpu.PrefetchScalarGridSpec(
            num_scalar_prefetch=1,
            grid=(count,),
            in_specs=[ANYWHERE] + [block_own] * 4 + [block_far] * 4 + [RESIDENT] * 2,
            out_specs=[block_out] * 4,
        ),
        out_shape=[shape] * 4,
        compiler_params=params(16),
        cost_estimate=moved(count * cells * features),
        name="temporal",
    )(place, before, *own, *far, *weights)


GROUP = ("far", "cell")
RING = ("near", "sub")


def paired(frames, w_qkv, w_out, w_up, w_down, temporal_weight_first, temporal_weight_second):
    frames_local, cells, features = frames.shape
    near_size, subs = lax.axis_size("near"), lax.axis_size("sub")
    sub, side = lax.axis_index("sub"), lax.axis_index("far")
    quarter = 2 * side + lax.axis_index("cell")
    ring = near_size * subs
    position = lax.axis_index("near") * subs + sub
    place = jnp.stack([sub, side, position == 0, position == ring - 1, quarter]).astype(jnp.int32)
    rightward = [(i, (i + 1) % ring) for i in range(ring)]
    leftward = [(target, source) for source, target in rightward]
    slots = frames_local // DILATION_FIRST
    grouped = frames.reshape(slots, DILATION_FIRST, cells, features)
    pinned = pltpu.with_memory_space_constraint(grouped, pltpu.HBM)
    units = DILATION_FIRST // 4 // CHUNKS

    def exchange(piece, delta):
        return lax.ppermute(piece, GROUP, [(i, i ^ delta) for i in range(4)])

    def halo(even, odd):
        return [even, odd, lax.ppermute(odd, RING, rightward), lax.ppermute(even, RING, leftward)]

    halves = (w_qkv, w_out, w_up, w_down, temporal_weight_first, temporal_weight_second)
    (beside,) = run_pack(place, place, pinned, units, 0, CHUNKS, (1,))
    cuts = [run_pack(place, beside, pinned, units, 0, 1, (2, 3))]
    mine = pack_weights(cuts[0][0], halves, features)
    for index in range(1, CHUNKS):
        cuts.append(run_pack(place, mine, pinned, units, index, 1, (2, 3)))
    beside = exchange(beside, 1)
    crossed = [[exchange(piece, delta) for delta, piece in zip((2, 3), cut)] for cut in cuts]
    other = lax.ppermute(mine, "sub", [(0, 1), (1, 0)])
    weights = join_weights(place, mine, mine, other, halves)
    section_weights, temporal_weights = weights[:4], weights[4:]

    even, odd = run_section(
        place, weights[0], pinned, beside, section_weights, units, CHUNKS, True
    )
    own = [pltpu.with_memory_space_constraint(field, pltpu.HBM) for field in halo(even, odd)]
    before = even
    far = []
    for pieces in crossed:
        even, odd = run_section(place, before, *pieces, section_weights, units, 1, False)
        far.append(halo(even, odd))
        before = even
    outs = []
    for index in range(CHUNKS):
        sent = run_temporal(
            place, before, own, far[index], temporal_weights, index * units, units
        )
        outs.append([sent[0]] + [exchange(sent[delta], delta) for delta in (1, 2, 3)])
        before = sent[0]
    result = jnp.zeros_like(grouped)
    for index, received in enumerate(outs):
        for delta in range(4):
            at = (4 * index + (quarter ^ delta)) * units
            result = lax.dynamic_update_slice_in_dim(result, received[delta], at, axis=1)
    return result.reshape(frames.shape)


def solution(mesh):
    groups, tm, cell, sub = (mesh.shape[axis] for axis in ("groups", "tm", "cell", "sub"))

    def run(frames, *weights):
        frame_total, cells, _ = frames.shape
        video = frame_total // groups
        frames_local = video // (tm * sub)
        fits = (
            video == 2 * DILATION_SECOND
            and frames_local == 2 * DILATION_FIRST
            and tm % 2 == 0
            and cell == 2
            and sub == 2
            and (cells // cell) % 16 == 0
            and DILATION_FIRST % (4 * CHUNKS) == 0
        )
        if fits:
            devices = mesh.devices.reshape(groups, 2, tm // 2, cell, sub)
            axes = ("groups", "far", "near", "cell", "sub")
            used, split, body = jax.sharding.Mesh(devices, axes), ("groups", "far", "near", "sub"), paired
        else:
            used, split, body = mesh, ("groups", "tm", "sub"), general
        return jax.shard_map(
            body,
            mesh=used,
            in_specs=(P(split, "cell", None),) + (P("sub", None),) * 6,
            out_specs=P(split, "cell", None),
            check_vma=False,
        )(frames, *weights)

    return run
```

```python
import functools
import math

import jax
import jax.numpy as jnp
from jax import lax
from jax.experimental import pallas as pl
from jax.experimental.pallas import tpu as pltpu
from jax.sharding import PartitionSpec as P

HEAD_DIM = 64
DILATION_FIRST = 16
DILATION_SECOND = 256
CHUNKS = 2
ORDER = (("s", 0), ("s", 1), ("t", 0), ("t", 1))
MIB = 1024 * 1024


def with_halo(block, sides, width):
    for axis, dim in sides:
        count = lax.axis_size(axis)
        forward = [(i, i + 1) for i in range(count - 1)]
        backward = [(target, source) for source, target in forward]
        low = lax.ppermute(
            lax.slice_in_dim(block, block.shape[dim] - width, None, axis=dim), axis, forward
        )
        high = lax.ppermute(lax.slice_in_dim(block, 0, width, axis=dim), axis, backward)
        block = jnp.concatenate([low, block, high], axis=dim)
    return block


def shifted(shard, axis, by):
    size = lax.axis_size(axis)
    pairs = [(i, i + by) for i in range(size) if 0 <= i + by < size]
    return lax.ppermute(shard, axis, pairs)


def normalize(values):
    row_mean = jnp.mean(values, axis=-1, keepdims=True)
    centred = values - row_mean
    row_var = jnp.mean(centred * centred, axis=-1, keepdims=True)
    return centred * lax.rsqrt(row_var + 1e-05)


def attend(queries, key_part, value_part):
    frame_count, q_cells, features = queries.shape
    head_count = features // HEAD_DIM
    q_heads = queries.reshape(frame_count, q_cells, head_count, HEAD_DIM)
    k_heads = key_part.reshape(frame_count, -1, head_count, HEAD_DIM)
    v_heads = value_part.reshape(frame_count, -1, head_count, HEAD_DIM)
    scores = jnp.einsum(
        "fqhd,fkhd->fhqk", q_heads, k_heads, preferred_element_type=jnp.float32
    ) * HEAD_DIM ** (-0.5)
    row_max = jnp.max(scores, axis=-1, keepdims=True)
    exp_terms = jnp.exp(scores - row_max)
    attn_probs = (exp_terms / jnp.sum(exp_terms, axis=-1, keepdims=True)).astype(jnp.bfloat16)
    mixed = jnp.einsum("fhqk,fkhd->fqhd", attn_probs, v_heads, preferred_element_type=jnp.float32)
    return mixed.astype(jnp.bfloat16).reshape(frame_count, q_cells, features)


def gated_step(center, earlier, later_frames, weight):
    features = center.shape[-1]
    stacked = jnp.concatenate([earlier, center, later_frames], axis=-1).reshape(-1, 3 * features)
    preact = jnp.dot(stacked, weight, preferred_element_type=jnp.float32)
    gated_part = jnp.tanh(preact[:, :features]) * jax.nn.sigmoid(preact[:, features:])
    return (center.astype(jnp.float32) + gated_part.reshape(center.shape)).astype(jnp.bfloat16)


def general(frames, w_qkv, w_out, w_up, w_down, temporal_weight_first, temporal_weight_second):
    frames_local, cell_rows, features = frames.shape
    whole_qkv, whole_out, whole_up, whole_down, whole_tcn_a, whole_tcn_b = (
        lax.all_gather(w, "sub", axis=0, tiled=True)
        for w in (w_qkv, w_out, w_up, w_down, temporal_weight_first, temporal_weight_second)
    )
    working = lax.all_to_all(frames, "cell", split_axis=0, concat_axis=1, tiled=True)
    frame_count, cells_here = (working.shape[0], working.shape[1])
    residual = working.astype(jnp.float32)
    normed = normalize(residual).astype(jnp.bfloat16).reshape(-1, features)
    projected = jnp.dot(normed, whole_qkv, preferred_element_type=jnp.float32).astype(jnp.bfloat16)
    projected = projected.reshape(frame_count, cells_here, 3 * features)
    attended = attend(
        projected[..., :features],
        projected[..., features : 2 * features],
        projected[..., 2 * features :],
    )
    out_part = jnp.dot(
        attended.reshape(-1, features), whole_out, preferred_element_type=jnp.float32
    )
    mid_state = (residual + out_part.reshape(frame_count, cells_here, features)).astype(
        jnp.bfloat16
    )
    mid_float = lax.optimization_barrier(mid_state).astype(jnp.float32)
    normed_two = normalize(mid_float).astype(jnp.bfloat16).reshape(-1, features)
    hidden = jax.nn.gelu(jnp.dot(normed_two, whole_up, preferred_element_type=jnp.float32)).astype(
        jnp.bfloat16
    )
    down_part = jnp.dot(hidden, whole_down, preferred_element_type=jnp.float32).reshape(
        frame_count, cells_here, features
    )
    sectioned_frames = (mid_float + down_part).astype(jnp.bfloat16)
    sectioned_frames = lax.all_to_all(
        sectioned_frames, "cell", split_axis=1, concat_axis=0, tiled=True
    )
    padded_frames = with_halo(sectioned_frames, ((("tm", "sub"), 0),), DILATION_FIRST)
    earlier = padded_frames[:frames_local]
    later_frames = padded_frames[2 * DILATION_FIRST : 2 * DILATION_FIRST + frames_local]
    opening_layer = gated_step(sectioned_frames, earlier, later_frames, whole_tcn_a)
    shard_step_count = DILATION_SECOND // frames_local
    far_earlier = shifted(opening_layer, ("tm", "sub"), shard_step_count)
    far_later = shifted(opening_layer, ("tm", "sub"), -shard_step_count)
    return gated_step(opening_layer, far_earlier, far_later, whole_tcn_b)


ANYWHERE = pl.BlockSpec(memory_space=pl.ANY)
RESIDENT = pl.BlockSpec(memory_space=pltpu.VMEM)
SCALARS = pl.BlockSpec(memory_space=pltpu.SMEM)


TOKEN = jax.ShapeDtypeStruct((8, 128), jnp.float32)
TOKEN_SPEC = pl.BlockSpec((8, 128), lambda *at: (0, 0))


def params(mib):
    return pltpu.CompilerParams(vmem_limit_bytes=mib * MIB)


def moved(count):
    return pl.CostEstimate(flops=0, bytes_accessed=count, transcendentals=0)


def pack_weights_kernel(before, *refs):
    *sources, packed = refs
    width = packed.shape[1]
    at = 0
    for source in sources:
        rows = source.shape[0]
        for column in range(0, source.shape[1], width):
            packed[at : at + rows] = source[:, column : column + width]
            at += rows


def pack_weights(before, weights, width):
    rows = sum(w.size for w in weights) // width
    return pl.pallas_call(
        pack_weights_kernel,
        out_shape=jax.ShapeDtypeStruct((rows, width), weights[0].dtype),
        in_specs=[ANYWHERE] + [RESIDENT] * len(weights),
        out_specs=RESIDENT,
        compiler_params=params(8),
        cost_estimate=moved(rows * width),
        name="pack_weights",
    )(before, *weights)


def join_weights_kernel(place, before, mine, other, *wholes):
    width = mine.shape[1]
    for source, core in ((mine, place[0]), (other, 1 - place[0])):
        at = 0
        for whole in wholes:
            rows = whole.shape[0] // 2
            spot = pl.ds(pl.multiple_of(core * rows, 16), rows)
            for column in range(0, whole.shape[1], width):
                whole[spot, column : column + width] = source[at : at + rows]
                at += rows


def join_weights(place, before, mine, other, halves):
    return pl.pallas_call(
        join_weights_kernel,
        out_shape=[jax.ShapeDtypeStruct((2 * w.shape[0], w.shape[1]), w.dtype) for w in halves],
        in_specs=[SCALARS, ANYWHERE, RESIDENT, RESIDENT],
        out_specs=[RESIDENT] * len(halves),
        compiler_params=params(8),
        cost_estimate=moved(mine.size),
        name="join_weights",
    )(place, before, mine, other)


def pack_kernel(chunks, place, *refs):
    sources, (both, *cuts) = refs[: 3 * chunks], refs[3 * chunks :]
    units = sources[0].shape[1]
    for chunk in range(chunks):
        both[:, chunk * units : (chunk + 1) * units] = sources[chunk][...]
    for source, packed in zip(sources[chunks:], cuts):
        packed[...] = source[...]


def run_pack(place, grouped, units, chunks):
    slots, _, cells, features = grouped.shape
    shape = (slots, units, cells, features)
    wanted = [(delta, chunk) for chunk in range(chunks) for delta in (2, 3)]
    beside = [(1, chunk) for chunk in range(chunks)]

    def source(delta, chunk):
        return pl.BlockSpec(shape, lambda i, at: (0, 4 * chunk + (at[4] ^ delta), 0, 0))

    whole = (slots, chunks * units, cells, features)
    both, *cuts = pl.pallas_call(
        functools.partial(pack_kernel, chunks),
        grid_spec=pltpu.PrefetchScalarGridSpec(
            num_scalar_prefetch=1,
            grid=(1,),
            in_specs=[source(*piece) for piece in beside + wanted],
            out_specs=[pl.BlockSpec(whole, lambda i, at: (0, 0, 0, 0))]
            + [pl.BlockSpec(shape, lambda i, at: (0, 0, 0, 0))] * len(wanted),
        ),
        out_shape=[jax.ShapeDtypeStruct(whole, grouped.dtype)]
        + [jax.ShapeDtypeStruct(shape, grouped.dtype)] * len(wanted),
        compiler_params=params(8),
        cost_estimate=moved(grouped.size),
        name="pack",
    )(place, *[grouped] * len(beside + wanted))
    return both, [cuts[2 * chunk : 2 * chunk + 2] for chunk in range(chunks)]


def section_kernel(
    place,
    before,
    mine,
    other,
    w_qkv,
    w_out,
    w_up,
    w_down,
    even_ref,
    odd_ref,
    token,
):
    token[...] = jnp.zeros_like(token)
    slots, units, half, features = mine.shape
    cells = 2 * half
    parts = []
    for slot in range(slots):
        for unit in range(units):
            parts += [mine[slot, unit], other[slot, unit]]
    residual = jnp.concatenate(parts, axis=0).astype(jnp.float32)
    frame_count = slots * units
    normed = normalize(residual).astype(jnp.bfloat16)
    projected = jnp.dot(normed, w_qkv[...], preferred_element_type=jnp.float32).astype(jnp.bfloat16)
    pair_width = 2 * HEAD_DIM
    low = lax.broadcasted_iota(jnp.int32, (cells, pair_width), 1) < HEAD_DIM
    low_one = low.astype(jnp.bfloat16)
    high_one = 1 - low_one
    scale = HEAD_DIM ** (-0.5) * math.log2(math.e)
    rows = []
    for frame in range(frame_count):
        block = projected[frame * cells : (frame + 1) * cells]
        columns = []
        for pair in range(features // pair_width):
            at = pair * pair_width
            queries = block[:, at : at + pair_width]
            keys = block[:, features + at : features + at + pair_width]
            values = block[:, 2 * features + at : 2 * features + at + pair_width]
            split_keys = jnp.concatenate([keys * low_one, keys * high_one], axis=0)
            scores = lax.dot_general(
                queries, split_keys, (((1,), (1,)), ((), ())), preferred_element_type=jnp.float32
            )
            terms = []
            for head in range(2):
                own_scores = scores[:, head * cells : (head + 1) * cells]
                row_max = jnp.max(own_scores, axis=-1, keepdims=True)
                terms.append(jnp.exp2((own_scores - row_max) * scale).astype(jnp.bfloat16))
            split_values = jnp.concatenate(
                [
                    jnp.concatenate([values * low_one, low_one], axis=1),
                    jnp.concatenate([values * high_one, high_one], axis=1),
                ],
                axis=0,
            )
            mixed = jnp.dot(
                jnp.concatenate(terms, axis=1), split_values, preferred_element_type=jnp.float32
            )
            inverse = pl.reciprocal(mixed[:, pair_width:], approx=True)
            columns.append((mixed[:, :pair_width] * inverse).astype(jnp.bfloat16))
        rows.append(jnp.concatenate(columns, axis=1))
    attended = jnp.concatenate(rows, axis=0)

    mid_state = (
        residual + jnp.dot(attended, w_out[...], preferred_element_type=jnp.float32)
    ).astype(jnp.bfloat16)
    mid_float = mid_state.astype(jnp.float32)
    normed_two = normalize(mid_float).astype(jnp.bfloat16)
    total = mid_float
    width = math.gcd(w_up.shape[1], 512)
    for at in range(0, w_up.shape[1], width):
        lifted = jnp.dot(normed_two, w_up[:, at : at + width], preferred_element_type=jnp.float32)
        lifted = lifted.astype(jnp.bfloat16)
        inner = lifted * (
            math.sqrt(2 / math.pi) + (math.sqrt(2 / math.pi) * 0.044715) * (lifted * lifted)
        )
        halved = 0.5 * lifted
        hidden = halved + halved * jnp.tanh(inner)
        total = total + jnp.dot(hidden, w_down[at : at + width], preferred_element_type=jnp.float32)
    sectioned = total.astype(jnp.bfloat16)
    for unit in range(units):
        even_ref[unit] = sectioned[unit * cells : (unit + 1) * cells]
        odd_ref[unit] = sectioned[(units + unit) * cells : (units + unit + 1) * cells]


def gate(center, preact):
    features = center.shape[-1]
    preact = preact.astype(jnp.bfloat16)
    opened = 0.5 + 0.5 * jnp.tanh(0.5 * preact[:, features:])
    return center + jnp.tanh(preact[:, :features]) * opened


def temporal_kernel(place, before, *refs):
    *fields, w_first, w_second, out0, out1, out2, out3, token = refs
    token[...] = jnp.zeros_like(token)
    near, is_first, is_last = place[1], place[2], place[3]
    units, cells, features = fields[0].shape
    flat = [field[...].reshape(units * cells, features) for field in fields]
    zero = jnp.zeros_like(flat[0])
    pairs = [(flat[i], flat[i + 4]) for i in range(4)]
    even_n, odd_n, left_a, right_a = [jnp.where(near == 0, a, b) for a, b in pairs]
    even_f, odd_f, left_b, right_b = [jnp.where(near == 0, b, a) for a, b in pairs]
    left_n = jnp.where(is_first == 1, zero, left_a)
    left_f = jnp.where(is_first == 1, left_a, left_b)
    right_n = jnp.where(is_last == 1, right_b, right_a)
    right_f = jnp.where(is_last == 1, zero, right_b)
    center = jnp.concatenate([even_n, odd_n, even_f, odd_f], axis=0)
    stacked = jnp.concatenate(
        [
            jnp.concatenate([left_n, even_n, left_f, even_f], axis=0),
            center,
            jnp.concatenate([odd_n, right_n, odd_f, right_f], axis=0),
        ],
        axis=1,
    )
    opening = gate(center, jnp.dot(stacked, w_first[...], preferred_element_type=jnp.float32))
    rows = 2 * units * cells
    near_part, far_part = opening[:rows], opening[rows:]
    both = jnp.concatenate([near_part, far_part], axis=1)
    result_n = gate(
        near_part, jnp.dot(both, w_second[features:], preferred_element_type=jnp.float32)
    )
    result_f = gate(
        far_part, jnp.dot(both, w_second[: 2 * features], preferred_element_type=jnp.float32)
    )
    same = jnp.where(near == 0, result_n, result_f)
    other = jnp.where(near == 0, result_f, result_n)
    half = cells // 2
    for slot in range(2):
        for unit in range(units):
            at = (slot * units + unit) * cells
            out0[slot, unit] = same[at : at + half]
            out1[slot, unit] = same[at + half : at + cells]
            out2[slot, unit] = other[at : at + half]
            out3[slot, unit] = other[at + half : at + cells]


def run_section(place, before, mine, other, weights, units, chunks, from_frames):
    slots, _, half, features = mine.shape
    shape_in = (slots, units, half, features)
    piece = pl.BlockSpec(shape_in, lambda i, at: (0, i, 0, 0))
    own = pl.BlockSpec(shape_in, lambda i, at: (0, 4 * i + at[4], 0, 0))
    block_out = pl.BlockSpec((units, 2 * half, features), lambda i, at: (i, 0, 0))
    place_out = pltpu.HBM if from_frames else jax.ShapeDtypeStruct
    shape = place_out((chunks * units, 2 * half, features), jnp.bfloat16)
    return pl.pallas_call(
        section_kernel,
        grid_spec=pltpu.PrefetchScalarGridSpec(
            num_scalar_prefetch=1,
            grid=(chunks,),
            in_specs=[ANYWHERE, own if from_frames else piece, piece] + [RESIDENT] * 4,
            out_specs=[block_out, block_out, TOKEN_SPEC],
        ),
        out_shape=[shape, shape, TOKEN],
        compiler_params=params(16),
        cost_estimate=moved(chunks * units * half * features),
        name="section",
    )(place, before, mine, other, *weights)


def run_temporal(place, before, own, far, weights, chunk, count):
    _, cells, features = own[0].shape
    block_own = pl.BlockSpec((count, cells, features), lambda i, at: (chunk, 0, 0))
    block_far = pl.BlockSpec((count, cells, features), lambda i, at: (0, 0, 0))
    block_out = pl.BlockSpec((2, count, cells // 2, features), lambda i, at: (0, 0, 0, 0))
    shape = pltpu.HBM((2, count, cells // 2, features), jnp.bfloat16)
    return pl.pallas_call(
        temporal_kernel,
        grid_spec=pltpu.PrefetchScalarGridSpec(
            num_scalar_prefetch=1,
            grid=(1,),
            in_specs=[ANYWHERE] + [block_own] * 4 + [block_far] * 4 + [RESIDENT] * 2,
            out_specs=[block_out] * 4 + [TOKEN_SPEC],
        ),
        out_shape=[shape] * 4 + [TOKEN],
        compiler_params=params(28),
        cost_estimate=moved(count * cells * features),
        name="temporal",
    )(place, before, *own, *far, *weights)


GROUP = ("far", "cell")
RING = ("near", "sub")


def paired(frames, w_qkv, w_out, w_up, w_down, temporal_weight_first, temporal_weight_second):
    frames_local, cells, features = frames.shape
    near_size, subs = lax.axis_size("near"), lax.axis_size("sub")
    sub, side = lax.axis_index("sub"), lax.axis_index("far")
    quarter = 2 * side + lax.axis_index("cell")
    ring = near_size * subs
    position = lax.axis_index("near") * subs + sub
    place = jnp.stack([sub, side, position == 0, position == ring - 1, quarter]).astype(jnp.int32)
    rightward = [(i, (i + 1) % ring) for i in range(ring)]
    leftward = [(target, source) for source, target in rightward]
    slots = frames_local // DILATION_FIRST
    grouped = frames.reshape(slots, DILATION_FIRST, cells, features)
    pinned = pltpu.with_memory_space_constraint(grouped, pltpu.HBM)
    units = DILATION_FIRST // 4 // CHUNKS

    def exchange(piece, delta):
        return lax.ppermute(piece, GROUP, [(i, i ^ delta) for i in range(4)])

    def halo(even, odd):
        return [even, odd, lax.ppermute(odd, RING, rightward), lax.ppermute(even, RING, leftward)]

    halves = (w_qkv, w_out, w_up, w_down, temporal_weight_first, temporal_weight_second)
    beside, cuts = run_pack(place, pinned, units, CHUNKS)
    mine = pack_weights(cuts[0][0], halves, features)
    beside = exchange(beside, 1)
    crossed = [[exchange(piece, delta) for delta, piece in zip((2, 3), cut)] for cut in cuts]
    other = lax.ppermute(mine, "sub", [(0, 1), (1, 0)])
    weights = join_weights(place, mine, mine, other, halves)
    section_weights, temporal_weights = weights[:4], weights[4:]

    even, odd, before = run_section(
        place, place, pinned, beside, section_weights, units, CHUNKS, True
    )
    own = [pltpu.with_memory_space_constraint(field, pltpu.HBM) for field in halo(even, odd)]
    far, outs = [], []
    for kind, index in ORDER:
        if kind == "s":
            even, odd, before = run_section(
                place, before, *crossed[index], section_weights, units, 1, False
            )
            far.append(halo(even, odd))
        else:
            *sent, before = run_temporal(
                place, before, own, far[index], temporal_weights, index, units
            )
            outs.append([sent[0]] + [exchange(sent[delta], delta) for delta in (1, 2, 3)])
    result = jnp.zeros_like(grouped)
    for index, received in enumerate(outs):
        for delta in range(4):
            at = (4 * index + (quarter ^ delta)) * units
            result = lax.dynamic_update_slice_in_dim(result, received[delta], at, axis=1)
    return result.reshape(frames.shape)


def solution(mesh):
    groups, tm, cell, sub = (mesh.shape[axis] for axis in ("groups", "tm", "cell", "sub"))

    def run(frames, *weights):
        frame_total, cells, _ = frames.shape
        video = frame_total // groups
        frames_local = video // (tm * sub)
        fits = (
            video == 2 * DILATION_SECOND
            and frames_local == 2 * DILATION_FIRST
            and tm % 2 == 0
            and cell == 2
            and sub == 2
            and (cells // cell) % 16 == 0
            and DILATION_FIRST % (4 * CHUNKS) == 0
        )
        if fits:
            devices = mesh.devices.reshape(groups, 2, tm // 2, cell, sub)
            axes = ("groups", "far", "near", "cell", "sub")
            used, split, body = jax.sharding.Mesh(devices, axes), ("groups", "far", "near", "sub"), paired
        else:
            used, split, body = mesh, ("groups", "tm", "sub"), general
        return jax.shard_map(
            body,
            mesh=used,
            in_specs=(P(split, "cell", None),) + (P("sub", None),) * 6,
            out_specs=P(split, "cell", None),
            check_vma=False,
        )(frames, *weights)

    return run
```

```python
import functools
import math

import jax
import jax.numpy as jnp
from jax import lax
from jax.experimental import pallas as pl
from jax.experimental.pallas import tpu as pltpu
from jax.sharding import PartitionSpec as P

HEAD_DIM = 64
DILATION_FIRST = 16
DILATION_SECOND = 256
CHUNKS = 2
ORDER = (("s", 0), ("s", 1), ("t", 0), ("t", 1))
MIB = 1024 * 1024


def with_halo(block, sides, width):
    for axis, dim in sides:
        count = lax.axis_size(axis)
        forward = [(i, i + 1) for i in range(count - 1)]
        backward = [(target, source) for source, target in forward]
        low = lax.ppermute(
            lax.slice_in_dim(block, block.shape[dim] - width, None, axis=dim), axis, forward
        )
        high = lax.ppermute(lax.slice_in_dim(block, 0, width, axis=dim), axis, backward)
        block = jnp.concatenate([low, block, high], axis=dim)
    return block


def shifted(shard, axis, by):
    size = lax.axis_size(axis)
    pairs = [(i, i + by) for i in range(size) if 0 <= i + by < size]
    return lax.ppermute(shard, axis, pairs)


def normalize(values):
    row_mean = jnp.mean(values, axis=-1, keepdims=True)
    centred = values - row_mean
    row_var = jnp.mean(centred * centred, axis=-1, keepdims=True)
    return centred * lax.rsqrt(row_var + 1e-05)


def attend(queries, key_part, value_part):
    frame_count, q_cells, features = queries.shape
    head_count = features // HEAD_DIM
    q_heads = queries.reshape(frame_count, q_cells, head_count, HEAD_DIM)
    k_heads = key_part.reshape(frame_count, -1, head_count, HEAD_DIM)
    v_heads = value_part.reshape(frame_count, -1, head_count, HEAD_DIM)
    scores = jnp.einsum(
        "fqhd,fkhd->fhqk", q_heads, k_heads, preferred_element_type=jnp.float32
    ) * HEAD_DIM ** (-0.5)
    row_max = jnp.max(scores, axis=-1, keepdims=True)
    exp_terms = jnp.exp(scores - row_max)
    attn_probs = (exp_terms / jnp.sum(exp_terms, axis=-1, keepdims=True)).astype(jnp.bfloat16)
    mixed = jnp.einsum("fhqk,fkhd->fqhd", attn_probs, v_heads, preferred_element_type=jnp.float32)
    return mixed.astype(jnp.bfloat16).reshape(frame_count, q_cells, features)


def gated_step(center, earlier, later_frames, weight):
    features = center.shape[-1]
    stacked = jnp.concatenate([earlier, center, later_frames], axis=-1).reshape(-1, 3 * features)
    preact = jnp.dot(stacked, weight, preferred_element_type=jnp.float32)
    gated_part = jnp.tanh(preact[:, :features]) * jax.nn.sigmoid(preact[:, features:])
    return (center.astype(jnp.float32) + gated_part.reshape(center.shape)).astype(jnp.bfloat16)


def general(frames, w_qkv, w_out, w_up, w_down, temporal_weight_first, temporal_weight_second):
    frames_local, cell_rows, features = frames.shape
    whole_qkv, whole_out, whole_up, whole_down, whole_tcn_a, whole_tcn_b = (
        lax.all_gather(w, "sub", axis=0, tiled=True)
        for w in (w_qkv, w_out, w_up, w_down, temporal_weight_first, temporal_weight_second)
    )
    working = lax.all_to_all(frames, "cell", split_axis=0, concat_axis=1, tiled=True)
    frame_count, cells_here = (working.shape[0], working.shape[1])
    residual = working.astype(jnp.float32)
    normed = normalize(residual).astype(jnp.bfloat16).reshape(-1, features)
    projected = jnp.dot(normed, whole_qkv, preferred_element_type=jnp.float32).astype(jnp.bfloat16)
    projected = projected.reshape(frame_count, cells_here, 3 * features)
    attended = attend(
        projected[..., :features],
        projected[..., features : 2 * features],
        projected[..., 2 * features :],
    )
    out_part = jnp.dot(
        attended.reshape(-1, features), whole_out, preferred_element_type=jnp.float32
    )
    mid_state = (residual + out_part.reshape(frame_count, cells_here, features)).astype(
        jnp.bfloat16
    )
    mid_float = lax.optimization_barrier(mid_state).astype(jnp.float32)
    normed_two = normalize(mid_float).astype(jnp.bfloat16).reshape(-1, features)
    hidden = jax.nn.gelu(jnp.dot(normed_two, whole_up, preferred_element_type=jnp.float32)).astype(
        jnp.bfloat16
    )
    down_part = jnp.dot(hidden, whole_down, preferred_element_type=jnp.float32).reshape(
        frame_count, cells_here, features
    )
    sectioned_frames = (mid_float + down_part).astype(jnp.bfloat16)
    sectioned_frames = lax.all_to_all(
        sectioned_frames, "cell", split_axis=1, concat_axis=0, tiled=True
    )
    padded_frames = with_halo(sectioned_frames, ((("tm", "sub"), 0),), DILATION_FIRST)
    earlier = padded_frames[:frames_local]
    later_frames = padded_frames[2 * DILATION_FIRST : 2 * DILATION_FIRST + frames_local]
    opening_layer = gated_step(sectioned_frames, earlier, later_frames, whole_tcn_a)
    shard_step_count = DILATION_SECOND // frames_local
    far_earlier = shifted(opening_layer, ("tm", "sub"), shard_step_count)
    far_later = shifted(opening_layer, ("tm", "sub"), -shard_step_count)
    return gated_step(opening_layer, far_earlier, far_later, whole_tcn_b)


ANYWHERE = pl.BlockSpec(memory_space=pl.ANY)
RESIDENT = pl.BlockSpec(memory_space=pltpu.VMEM)
SCALARS = pl.BlockSpec(memory_space=pltpu.SMEM)


TOKEN = jax.ShapeDtypeStruct((8, 128), jnp.float32)
TOKEN_SPEC = pl.BlockSpec((8, 128), lambda *at: (0, 0))


def params(mib):
    return pltpu.CompilerParams(vmem_limit_bytes=mib * MIB)


def moved(count):
    return pl.CostEstimate(flops=0, bytes_accessed=count, transcendentals=0)


def pack_weights_kernel(before, *refs):
    *sources, packed = refs
    width = packed.shape[1]
    at = 0
    for source in sources:
        rows = source.shape[0]
        for column in range(0, source.shape[1], width):
            packed[at : at + rows] = source[:, column : column + width]
            at += rows


def pack_weights(before, weights, width):
    rows = sum(w.size for w in weights) // width
    return pl.pallas_call(
        pack_weights_kernel,
        out_shape=jax.ShapeDtypeStruct((rows, width), weights[0].dtype),
        in_specs=[ANYWHERE] + [RESIDENT] * len(weights),
        out_specs=RESIDENT,
        compiler_params=params(8),
        cost_estimate=moved(rows * width),
        name="pack_weights",
    )(before, *weights)


def join_weights_kernel(place, before, mine, other, *wholes):
    width = mine.shape[1]
    for source, core in ((mine, place[0]), (other, 1 - place[0])):
        at = 0
        for whole in wholes:
            rows = whole.shape[0] // 2
            spot = pl.ds(pl.multiple_of(core * rows, 16), rows)
            for column in range(0, whole.shape[1], width):
                whole[spot, column : column + width] = source[at : at + rows]
                at += rows


def join_weights(place, before, mine, other, halves):
    return pl.pallas_call(
        join_weights_kernel,
        out_shape=[jax.ShapeDtypeStruct((2 * w.shape[0], w.shape[1]), w.dtype) for w in halves],
        in_specs=[SCALARS, ANYWHERE, RESIDENT, RESIDENT],
        out_specs=[RESIDENT] * len(halves),
        compiler_params=params(8),
        cost_estimate=moved(mine.size),
        name="join_weights",
    )(place, before, mine, other)


def pack_kernel(chunks, place, *refs):
    sources, (both, *cuts) = refs[: 3 * chunks], refs[3 * chunks :]
    units = sources[0].shape[1]
    for chunk in range(chunks):
        both[:, chunk * units : (chunk + 1) * units] = sources[chunk][...]
    for source, packed in zip(sources[chunks:], cuts):
        packed[...] = source[...]


def run_pack(place, grouped, units, chunks):
    slots, _, cells, features = grouped.shape
    shape = (slots, units, cells, features)
    wanted = [(delta, chunk) for chunk in range(chunks) for delta in (2, 3)]
    beside = [(1, chunk) for chunk in range(chunks)]

    def source(delta, chunk):
        return pl.BlockSpec(shape, lambda i, at: (0, 4 * chunk + (at[4] ^ delta), 0, 0))

    whole = (slots, chunks * units, cells, features)
    both, *cuts = pl.pallas_call(
        functools.partial(pack_kernel, chunks),
        grid_spec=pltpu.PrefetchScalarGridSpec(
            num_scalar_prefetch=1,
            grid=(1,),
            in_specs=[source(*piece) for piece in beside + wanted],
            out_specs=[RESIDENT] * (1 + len(wanted)),
        ),
        out_shape=[jax.ShapeDtypeStruct(whole, grouped.dtype)]
        + [jax.ShapeDtypeStruct(shape, grouped.dtype)] * len(wanted),
        compiler_params=params(8),
        cost_estimate=moved(grouped.size),
        name="pack",
    )(place, *[grouped] * len(beside + wanted))
    return both, [cuts[2 * chunk : 2 * chunk + 2] for chunk in range(chunks)]


def section_kernel(
    place,
    before,
    mine,
    other,
    w_qkv,
    w_out,
    w_up,
    w_down,
    even_ref,
    odd_ref,
    token,
):
    token[...] = jnp.zeros_like(token)
    slots, units, half, features = mine.shape
    cells = 2 * half
    parts = []
    for slot in range(slots):
        for unit in range(units):
            parts += [mine[slot, unit], other[slot, unit]]
    residual = jnp.concatenate(parts, axis=0).astype(jnp.float32)
    frame_count = slots * units
    normed = normalize(residual).astype(jnp.bfloat16)
    projected = jnp.dot(normed, w_qkv[...], preferred_element_type=jnp.float32).astype(jnp.bfloat16)
    pair_width = 2 * HEAD_DIM
    low = lax.broadcasted_iota(jnp.int32, (cells, pair_width), 1) < HEAD_DIM
    low_one = low.astype(jnp.bfloat16)
    high_one = 1 - low_one
    scale = HEAD_DIM ** (-0.5) * math.log2(math.e)
    rows = []
    for frame in range(frame_count):
        block = projected[frame * cells : (frame + 1) * cells]
        columns = []
        for pair in range(features // pair_width):
            at = pair * pair_width
            queries = block[:, at : at + pair_width]
            keys = block[:, features + at : features + at + pair_width]
            values = block[:, 2 * features + at : 2 * features + at + pair_width]
            split_keys = jnp.concatenate([keys * low_one, keys * high_one], axis=0)
            scores = lax.dot_general(
                queries, split_keys, (((1,), (1,)), ((), ())), preferred_element_type=jnp.float32
            )
            terms = []
            for head in range(2):
                own_scores = scores[:, head * cells : (head + 1) * cells]
                row_max = jnp.max(own_scores, axis=-1, keepdims=True)
                terms.append(jnp.exp2((own_scores - row_max) * scale).astype(jnp.bfloat16))
            split_values = jnp.concatenate(
                [
                    jnp.concatenate([values * low_one, low_one], axis=1),
                    jnp.concatenate([values * high_one, high_one], axis=1),
                ],
                axis=0,
            )
            mixed = jnp.dot(
                jnp.concatenate(terms, axis=1), split_values, preferred_element_type=jnp.float32
            )
            inverse = pl.reciprocal(mixed[:, pair_width:], approx=True)
            columns.append((mixed[:, :pair_width] * inverse).astype(jnp.bfloat16))
        rows.append(jnp.concatenate(columns, axis=1))
    attended = jnp.concatenate(rows, axis=0)

    mid_state = (
        residual + jnp.dot(attended, w_out[...], preferred_element_type=jnp.float32)
    ).astype(jnp.bfloat16)
    mid_float = mid_state.astype(jnp.float32)
    normed_two = normalize(mid_float).astype(jnp.bfloat16)
    total = mid_float
    width = math.gcd(w_up.shape[1], 512)
    for at in range(0, w_up.shape[1], width):
        lifted = jnp.dot(normed_two, w_up[:, at : at + width], preferred_element_type=jnp.float32)
        lifted = lifted.astype(jnp.bfloat16)
        inner = lifted * (
            math.sqrt(2 / math.pi) + (math.sqrt(2 / math.pi) * 0.044715) * (lifted * lifted)
        )
        halved = 0.5 * lifted
        hidden = halved + halved * jnp.tanh(inner)
        total = total + jnp.dot(hidden, w_down[at : at + width], preferred_element_type=jnp.float32)
    sectioned = total.astype(jnp.bfloat16)
    for unit in range(units):
        even_ref[unit] = sectioned[unit * cells : (unit + 1) * cells]
        odd_ref[unit] = sectioned[(units + unit) * cells : (units + unit + 1) * cells]


def gate(center, preact):
    features = center.shape[-1]
    preact = preact.astype(jnp.bfloat16)
    opened = 0.5 + 0.5 * jnp.tanh(0.5 * preact[:, features:])
    return center + jnp.tanh(preact[:, :features]) * opened


def temporal_kernel(place, before, *refs):
    *fields, w_first, w_second, out0, out1, out2, out3, token, stacked, results = refs
    token[...] = jnp.zeros_like(token)
    side, is_first, is_last = place[1], place[2], place[3]
    units, cells, features = fields[0].shape
    slab = units * cells
    rows = 2 * slab
    for index in range(2):
        even, odd, left, right = fields[4 * index : 4 * index + 4]
        base = pl.multiple_of(jnp.where(side == index, 0, rows), slab)
        left_base = pl.multiple_of(jnp.where(is_first == 1, rows - base, base), slab)
        right_base = pl.multiple_of(jnp.where(is_last == 1, rows - base, base), slab)
        for unit in range(units):
            low, high = unit * cells, slab + unit * cells
            even_rows = pl.ds(pl.multiple_of(base + low, cells), cells)
            odd_rows = pl.ds(pl.multiple_of(base + high, cells), cells)
            stacked[even_rows, features : 2 * features] = even[unit]
            stacked[odd_rows, features : 2 * features] = odd[unit]
            stacked[odd_rows, :features] = even[unit]
            stacked[even_rows, 2 * features :] = odd[unit]
            left_rows = pl.ds(pl.multiple_of(left_base + low, cells), cells)
            right_rows = pl.ds(pl.multiple_of(right_base + high, cells), cells)
            stacked[left_rows, :features] = left[unit]
            stacked[right_rows, 2 * features :] = right[unit]

    @pl.when(is_first == 1)
    def _():
        stacked[:slab, :features] = jnp.zeros((slab, features), stacked.dtype)

    @pl.when(is_last == 1)
    def _():
        stacked[rows + slab :, 2 * features :] = jnp.zeros((slab, features), stacked.dtype)

    opening = gate(
        stacked[:, features : 2 * features],
        jnp.dot(stacked[...], w_first[...], preferred_element_type=jnp.float32),
    )
    near_part, far_part = opening[:rows], opening[rows:]
    both = jnp.concatenate([near_part, far_part], axis=1)
    results[:rows] = gate(
        near_part, jnp.dot(both, w_second[features:], preferred_element_type=jnp.float32)
    )
    results[rows:] = gate(
        far_part, jnp.dot(both, w_second[: 2 * features], preferred_element_type=jnp.float32)
    )
    half = cells // 2
    for index, (near_out, far_out) in enumerate(((out0, out1), (out2, out3))):
        base = jnp.where(side == index, 0, rows)
        for slot in range(2):
            for unit in range(units):
                at = base + (slot * units + unit) * cells
                near_out[slot, unit] = results[pl.ds(pl.multiple_of(at, half), half)]
                far_out[slot, unit] = results[pl.ds(pl.multiple_of(at + half, half), half)]


def run_section(place, before, mine, other, weights, units, chunks, from_frames):
    slots, _, half, features = mine.shape
    shape_in = (slots, units, half, features)
    piece = pl.BlockSpec(shape_in, lambda i, at: (0, i, 0, 0))
    own = pl.BlockSpec(shape_in, lambda i, at: (0, 4 * i + at[4], 0, 0))
    block_out = pl.BlockSpec((units, 2 * half, features), lambda i, at: (i, 0, 0))
    place_out = pltpu.HBM if from_frames else jax.ShapeDtypeStruct
    shape = place_out((chunks * units, 2 * half, features), jnp.bfloat16)
    return pl.pallas_call(
        section_kernel,
        grid_spec=pltpu.PrefetchScalarGridSpec(
            num_scalar_prefetch=1,
            grid=(chunks,),
            in_specs=([ANYWHERE, own, piece] if from_frames else [ANYWHERE, RESIDENT, RESIDENT])
            + [RESIDENT] * 4,
            out_specs=([block_out] * 2 if from_frames else [RESIDENT] * 2) + [TOKEN_SPEC],
        ),
        out_shape=[shape, shape, TOKEN],
        compiler_params=params(16),
        cost_estimate=moved(chunks * units * half * features),
        name="section",
    )(place, before, mine, other, *weights)


def run_temporal(place, before, own, far, weights, chunk, count):
    _, cells, features = own[0].shape
    block_own = pl.BlockSpec((count, cells, features), lambda i, at: (chunk, 0, 0))
    block_far = pl.BlockSpec((count, cells, features), lambda i, at: (0, 0, 0))
    block_out = pl.BlockSpec((2, count, cells // 2, features), lambda i, at: (0, 0, 0, 0))
    shape = pltpu.HBM((2, count, cells // 2, features), jnp.bfloat16)
    return pl.pallas_call(
        temporal_kernel,
        grid_spec=pltpu.PrefetchScalarGridSpec(
            num_scalar_prefetch=1,
            grid=(1,),
            in_specs=[ANYWHERE] + [block_own] * 4 + [block_far] * 4 + [RESIDENT] * 2,
            out_specs=[block_out] * 4 + [TOKEN_SPEC],
            scratch_shapes=[
                pltpu.VMEM((4 * count * cells, 3 * features), jnp.bfloat16),
                pltpu.VMEM((4 * count * cells, features), jnp.bfloat16),
            ],
        ),
        out_shape=[shape] * 4 + [TOKEN],
        compiler_params=params(28),
        cost_estimate=moved(count * cells * features),
        name="temporal",
    )(place, before, *own, *far, *weights)


def unpack_kernel(place, before, buffer, *refs):
    *pieces, result = refs
    for delta, piece in enumerate(pieces):

        @pl.when(pl.program_id(0) == delta)
        def _():
            result[...] = piece[...]


def run_unpack(place, before, buffer, pieces, chunk, shape):
    piece = pieces[0].shape
    return pl.pallas_call(
        unpack_kernel,
        grid_spec=pltpu.PrefetchScalarGridSpec(
            num_scalar_prefetch=1,
            grid=(4,),
            in_specs=[ANYWHERE, ANYWHERE] + [RESIDENT] * 4,
            out_specs=pl.BlockSpec(piece, lambda i, at: (0, 4 * chunk + (at[4] ^ i), 0, 0)),
        ),
        out_shape=pltpu.HBM(shape, pieces[0].dtype),
        input_output_aliases={} if chunk == 0 else {2: 0},
        compiler_params=params(8),
        cost_estimate=moved(4 * pieces[0].size),
        name="unpack",
    )(place, before, buffer, *pieces)


GROUP = ("far", "cell")
RING = ("near", "sub")


def paired(frames, w_qkv, w_out, w_up, w_down, temporal_weight_first, temporal_weight_second):
    frames_local, cells, features = frames.shape
    near_size, subs = lax.axis_size("near"), lax.axis_size("sub")
    sub, side = lax.axis_index("sub"), lax.axis_index("far")
    quarter = 2 * side + lax.axis_index("cell")
    ring = near_size * subs
    position = lax.axis_index("near") * subs + sub
    place = jnp.stack([sub, side, position == 0, position == ring - 1, quarter]).astype(jnp.int32)
    rightward = [(i, (i + 1) % ring) for i in range(ring)]
    leftward = [(target, source) for source, target in rightward]
    slots = frames_local // DILATION_FIRST
    grouped = frames.reshape(slots, DILATION_FIRST, cells, features)
    pinned = pltpu.with_memory_space_constraint(grouped, pltpu.HBM)
    units = DILATION_FIRST // 4 // CHUNKS

    def exchange(piece, delta):
        return lax.ppermute(piece, GROUP, [(i, i ^ delta) for i in range(4)])

    def halo(even, odd):
        return [even, odd, lax.ppermute(odd, RING, rightward), lax.ppermute(even, RING, leftward)]

    halves = (w_qkv, w_out, w_up, w_down, temporal_weight_first, temporal_weight_second)
    beside, cuts = run_pack(place, pinned, units, CHUNKS)
    mine = pack_weights(cuts[0][0], halves, features)
    beside = exchange(beside, 1)
    crossed = [[exchange(piece, delta) for delta, piece in zip((2, 3), cut)] for cut in cuts]
    other = lax.ppermute(mine, "sub", [(0, 1), (1, 0)])
    weights = join_weights(place, mine, mine, other, halves)
    section_weights, temporal_weights = weights[:4], weights[4:]

    even, odd, before = run_section(
        place, place, pinned, beside, section_weights, units, CHUNKS, True
    )
    own = [pltpu.with_memory_space_constraint(field, pltpu.HBM) for field in halo(even, odd)]
    far, outs = [], []
    for kind, index in ORDER:
        if kind == "s":
            even, odd, before = run_section(
                place, before, *crossed[index], section_weights, units, 1, False
            )
            far.append(halo(even, odd))
        else:
            *sent, before = run_temporal(
                place, before, own, far[index], temporal_weights, index, units
            )
            outs.append([sent[0]] + [exchange(sent[delta], delta) for delta in (1, 2, 3)])
    result = before
    for index, received in enumerate(outs):
        result = run_unpack(place, before, result, received, index, grouped.shape)
    return result.reshape(frames.shape)


def solution(mesh):
    groups, tm, cell, sub = (mesh.shape[axis] for axis in ("groups", "tm", "cell", "sub"))

    def run(frames, *weights):
        frame_total, cells, _ = frames.shape
        video = frame_total // groups
        frames_local = video // (tm * sub)
        fits = (
            video == 2 * DILATION_SECOND
            and frames_local == 2 * DILATION_FIRST
            and tm % 2 == 0
            and cell == 2
            and sub == 2
            and (cells // cell) % 16 == 0
            and DILATION_FIRST % (4 * CHUNKS) == 0
        )
        if fits:
            devices = mesh.devices.reshape(groups, 2, tm // 2, cell, sub)
            axes = ("groups", "far", "near", "cell", "sub")
            used, split, body = jax.sharding.Mesh(devices, axes), ("groups", "far", "near", "sub"), paired
        else:
            used, split, body = mesh, ("groups", "tm", "sub"), general
        return jax.shard_map(
            body,
            mesh=used,
            in_specs=(P(split, "cell", None),) + (P("sub", None),) * 6,
            out_specs=P(split, "cell", None),
            check_vma=False,
        )(frames, *weights)

    return run
```

```python
import functools
import math

import jax
import jax.numpy as jnp
from jax import lax
from jax.experimental import pallas as pl
from jax.experimental.pallas import tpu as pltpu
from jax.sharding import PartitionSpec as P

HEAD_DIM = 64
DILATION_FIRST = 16
DILATION_SECOND = 256
CHUNKS = 2
ORDER = (("s", 0), ("s", 1), ("t", 0), ("t", 1))
MIB = 1024 * 1024


def with_halo(block, sides, width):
    for axis, dim in sides:
        count = lax.axis_size(axis)
        forward = [(i, i + 1) for i in range(count - 1)]
        backward = [(target, source) for source, target in forward]
        low = lax.ppermute(
            lax.slice_in_dim(block, block.shape[dim] - width, None, axis=dim), axis, forward
        )
        high = lax.ppermute(lax.slice_in_dim(block, 0, width, axis=dim), axis, backward)
        block = jnp.concatenate([low, block, high], axis=dim)
    return block


def shifted(shard, axis, by):
    size = lax.axis_size(axis)
    pairs = [(i, i + by) for i in range(size) if 0 <= i + by < size]
    return lax.ppermute(shard, axis, pairs)


def normalize(values):
    row_mean = jnp.mean(values, axis=-1, keepdims=True)
    centred = values - row_mean
    row_var = jnp.mean(centred * centred, axis=-1, keepdims=True)
    return centred * lax.rsqrt(row_var + 1e-05)


def attend(queries, key_part, value_part):
    frame_count, q_cells, features = queries.shape
    head_count = features // HEAD_DIM
    q_heads = queries.reshape(frame_count, q_cells, head_count, HEAD_DIM)
    k_heads = key_part.reshape(frame_count, -1, head_count, HEAD_DIM)
    v_heads = value_part.reshape(frame_count, -1, head_count, HEAD_DIM)
    scores = jnp.einsum(
        "fqhd,fkhd->fhqk", q_heads, k_heads, preferred_element_type=jnp.float32
    ) * HEAD_DIM ** (-0.5)
    row_max = jnp.max(scores, axis=-1, keepdims=True)
    exp_terms = jnp.exp(scores - row_max)
    attn_probs = (exp_terms / jnp.sum(exp_terms, axis=-1, keepdims=True)).astype(jnp.bfloat16)
    mixed = jnp.einsum("fhqk,fkhd->fqhd", attn_probs, v_heads, preferred_element_type=jnp.float32)
    return mixed.astype(jnp.bfloat16).reshape(frame_count, q_cells, features)


def gated_step(center, earlier, later_frames, weight):
    features = center.shape[-1]
    stacked = jnp.concatenate([earlier, center, later_frames], axis=-1).reshape(-1, 3 * features)
    preact = jnp.dot(stacked, weight, preferred_element_type=jnp.float32)
    gated_part = jnp.tanh(preact[:, :features]) * jax.nn.sigmoid(preact[:, features:])
    return (center.astype(jnp.float32) + gated_part.reshape(center.shape)).astype(jnp.bfloat16)


def general(frames, w_qkv, w_out, w_up, w_down, temporal_weight_first, temporal_weight_second):
    frames_local, cell_rows, features = frames.shape
    whole_qkv, whole_out, whole_up, whole_down, whole_tcn_a, whole_tcn_b = (
        lax.all_gather(w, "sub", axis=0, tiled=True)
        for w in (w_qkv, w_out, w_up, w_down, temporal_weight_first, temporal_weight_second)
    )
    working = lax.all_to_all(frames, "cell", split_axis=0, concat_axis=1, tiled=True)
    frame_count, cells_here = (working.shape[0], working.shape[1])
    residual = working.astype(jnp.float32)
    normed = normalize(residual).astype(jnp.bfloat16).reshape(-1, features)
    projected = jnp.dot(normed, whole_qkv, preferred_element_type=jnp.float32).astype(jnp.bfloat16)
    projected = projected.reshape(frame_count, cells_here, 3 * features)
    attended = attend(
        projected[..., :features],
        projected[..., features : 2 * features],
        projected[..., 2 * features :],
    )
    out_part = jnp.dot(
        attended.reshape(-1, features), whole_out, preferred_element_type=jnp.float32
    )
    mid_state = (residual + out_part.reshape(frame_count, cells_here, features)).astype(
        jnp.bfloat16
    )
    mid_float = lax.optimization_barrier(mid_state).astype(jnp.float32)
    normed_two = normalize(mid_float).astype(jnp.bfloat16).reshape(-1, features)
    hidden = jax.nn.gelu(jnp.dot(normed_two, whole_up, preferred_element_type=jnp.float32)).astype(
        jnp.bfloat16
    )
    down_part = jnp.dot(hidden, whole_down, preferred_element_type=jnp.float32).reshape(
        frame_count, cells_here, features
    )
    sectioned_frames = (mid_float + down_part).astype(jnp.bfloat16)
    sectioned_frames = lax.all_to_all(
        sectioned_frames, "cell", split_axis=1, concat_axis=0, tiled=True
    )
    padded_frames = with_halo(sectioned_frames, ((("tm", "sub"), 0),), DILATION_FIRST)
    earlier = padded_frames[:frames_local]
    later_frames = padded_frames[2 * DILATION_FIRST : 2 * DILATION_FIRST + frames_local]
    opening_layer = gated_step(sectioned_frames, earlier, later_frames, whole_tcn_a)
    shard_step_count = DILATION_SECOND // frames_local
    far_earlier = shifted(opening_layer, ("tm", "sub"), shard_step_count)
    far_later = shifted(opening_layer, ("tm", "sub"), -shard_step_count)
    return gated_step(opening_layer, far_earlier, far_later, whole_tcn_b)


ANYWHERE = pl.BlockSpec(memory_space=pl.ANY)
RESIDENT = pl.BlockSpec(memory_space=pltpu.VMEM)
SCALARS = pl.BlockSpec(memory_space=pltpu.SMEM)


TOKEN = jax.ShapeDtypeStruct((8, 128), jnp.float32)
TOKEN_SPEC = pl.BlockSpec((8, 128), lambda *at: (0, 0))


def params(mib):
    return pltpu.CompilerParams(vmem_limit_bytes=mib * MIB)


def moved(count):
    return pl.CostEstimate(flops=0, bytes_accessed=count, transcendentals=0)


def pack_weights_kernel(before, *refs):
    *sources, packed = refs
    width = packed.shape[1]
    at = 0
    for source in sources:
        rows = source.shape[0]
        for column in range(0, source.shape[1], width):
            packed[at : at + rows] = source[:, column : column + width]
            at += rows


def pack_weights(before, weights, width):
    rows = sum(w.size for w in weights) // width
    return pl.pallas_call(
        pack_weights_kernel,
        out_shape=jax.ShapeDtypeStruct((rows, width), weights[0].dtype),
        in_specs=[ANYWHERE] + [RESIDENT] * len(weights),
        out_specs=RESIDENT,
        compiler_params=params(8),
        cost_estimate=moved(rows * width),
        name="pack_weights",
    )(before, *weights)


def join_weights_kernel(place, before, mine, other, *wholes):
    width = mine.shape[1]
    for source, core in ((mine, place[0]), (other, 1 - place[0])):
        at = 0
        for whole in wholes:
            rows = whole.shape[0] // 2
            spot = pl.ds(pl.multiple_of(core * rows, 16), rows)
            for column in range(0, whole.shape[1], width):
                whole[spot, column : column + width] = source[at : at + rows]
                at += rows


def join_weights(place, before, mine, other, halves):
    return pl.pallas_call(
        join_weights_kernel,
        out_shape=[jax.ShapeDtypeStruct((2 * w.shape[0], w.shape[1]), w.dtype) for w in halves],
        in_specs=[SCALARS, ANYWHERE, RESIDENT, RESIDENT],
        out_specs=[RESIDENT] * len(halves),
        compiler_params=params(8),
        cost_estimate=moved(mine.size),
        name="join_weights",
    )(place, before, mine, other)


def pack_kernel(chunks, place, *refs):
    sources, (both, *cuts) = refs[: 3 * chunks], refs[3 * chunks :]
    units = sources[0].shape[1]
    for chunk in range(chunks):
        both[:, chunk * units : (chunk + 1) * units] = sources[chunk][...]
    for source, packed in zip(sources[chunks:], cuts):
        packed[...] = source[...]


def run_pack(place, grouped, units, chunks):
    slots, _, cells, features = grouped.shape
    shape = (slots, units, cells, features)
    wanted = [(delta, chunk) for chunk in range(chunks) for delta in (2, 3)]
    beside = [(1, chunk) for chunk in range(chunks)]

    def source(delta, chunk):
        return pl.BlockSpec(shape, lambda i, at: (0, 4 * chunk + (at[4] ^ delta), 0, 0))

    whole = (slots, chunks * units, cells, features)
    both, *cuts = pl.pallas_call(
        functools.partial(pack_kernel, chunks),
        grid_spec=pltpu.PrefetchScalarGridSpec(
            num_scalar_prefetch=1,
            grid=(1,),
            in_specs=[source(*piece) for piece in beside + wanted],
            out_specs=[RESIDENT] * (1 + len(wanted)),
        ),
        out_shape=[jax.ShapeDtypeStruct(whole, grouped.dtype)]
        + [jax.ShapeDtypeStruct(shape, grouped.dtype)] * len(wanted),
        compiler_params=params(8),
        cost_estimate=moved(grouped.size),
        name="pack",
    )(place, *[grouped] * len(beside + wanted))
    return both, [cuts[2 * chunk : 2 * chunk + 2] for chunk in range(chunks)]


def section_kernel(
    place,
    before,
    mine,
    other,
    w_qkv,
    w_out,
    w_up,
    w_down,
    even_ref,
    odd_ref,
    token,
):
    token[...] = jnp.zeros_like(token)
    slots, units, half, features = mine.shape
    cells = 2 * half
    parts = []
    for slot in range(slots):
        for unit in range(units):
            parts += [mine[slot, unit], other[slot, unit]]
    residual = jnp.concatenate(parts, axis=0).astype(jnp.float32)
    frame_count = slots * units
    normed = normalize(residual).astype(jnp.bfloat16)
    projected = jnp.dot(normed, w_qkv[...], preferred_element_type=jnp.float32).astype(jnp.bfloat16)
    pair_width = 2 * HEAD_DIM
    low = lax.broadcasted_iota(jnp.int32, (cells, pair_width), 1) < HEAD_DIM
    low_one = low.astype(jnp.bfloat16)
    high_one = 1 - low_one
    scale = HEAD_DIM ** (-0.5) * math.log2(math.e)
    rows = []
    for frame in range(frame_count):
        block = projected[frame * cells : (frame + 1) * cells]
        columns = []
        for pair in range(features // pair_width):
            at = pair * pair_width
            queries = block[:, at : at + pair_width]
            keys = block[:, features + at : features + at + pair_width]
            values = block[:, 2 * features + at : 2 * features + at + pair_width]
            split_keys = jnp.concatenate([keys * low_one, keys * high_one], axis=0)
            scores = lax.dot_general(
                queries, split_keys, (((1,), (1,)), ((), ())), preferred_element_type=jnp.float32
            )
            terms = []
            for head in range(2):
                own_scores = scores[:, head * cells : (head + 1) * cells]
                row_max = jnp.max(own_scores, axis=-1, keepdims=True)
                terms.append(jnp.exp2((own_scores - row_max) * scale).astype(jnp.bfloat16))
            split_values = jnp.concatenate(
                [
                    jnp.concatenate([values * low_one, low_one], axis=1),
                    jnp.concatenate([values * high_one, high_one], axis=1),
                ],
                axis=0,
            )
            mixed = jnp.dot(
                jnp.concatenate(terms, axis=1), split_values, preferred_element_type=jnp.float32
            )
            inverse = pl.reciprocal(mixed[:, pair_width:], approx=True)
            columns.append((mixed[:, :pair_width] * inverse).astype(jnp.bfloat16))
        rows.append(jnp.concatenate(columns, axis=1))
    attended = jnp.concatenate(rows, axis=0)

    mid_state = (
        residual + jnp.dot(attended, w_out[...], preferred_element_type=jnp.float32)
    ).astype(jnp.bfloat16)
    mid_float = mid_state.astype(jnp.float32)
    normed_two = normalize(mid_float).astype(jnp.bfloat16)
    total = mid_float
    width = math.gcd(w_up.shape[1], 512)
    for at in range(0, w_up.shape[1], width):
        lifted = jnp.dot(normed_two, w_up[:, at : at + width], preferred_element_type=jnp.float32)
        lifted = lifted.astype(jnp.bfloat16)
        inner = lifted * (
            math.sqrt(2 / math.pi) + (math.sqrt(2 / math.pi) * 0.044715) * (lifted * lifted)
        )
        halved = 0.5 * lifted
        hidden = halved + halved * jnp.tanh(inner)
        total = total + jnp.dot(hidden, w_down[at : at + width], preferred_element_type=jnp.float32)
    sectioned = total.astype(jnp.bfloat16)
    for unit in range(units):
        even_ref[unit] = sectioned[unit * cells : (unit + 1) * cells]
        odd_ref[unit] = sectioned[(units + unit) * cells : (units + unit + 1) * cells]


def gate(center, preact):
    features = center.shape[-1]
    preact = preact.astype(jnp.bfloat16)
    opened = 0.5 + 0.5 * jnp.tanh(0.5 * preact[:, features:])
    return center + jnp.tanh(preact[:, :features]) * opened


def temporal_kernel(chunk, place, before, *refs):
    *fields, w_first, w_second, out0, out1, out2, out3, token = refs
    token[...] = jnp.zeros_like(token)
    near, is_first, is_last = place[1], place[2], place[3]
    units, cells, features = fields[4].shape
    spans = [slice(chunk * units, (chunk + 1) * units)] * 4 + [slice(0, units)] * 4
    flat = [field[at].reshape(units * cells, features) for field, at in zip(fields, spans)]
    zero = jnp.zeros_like(flat[0])
    pairs = [(flat[i], flat[i + 4]) for i in range(4)]
    even_n, odd_n, left_a, right_a = [jnp.where(near == 0, a, b) for a, b in pairs]
    even_f, odd_f, left_b, right_b = [jnp.where(near == 0, b, a) for a, b in pairs]
    left_n = jnp.where(is_first == 1, zero, left_a)
    left_f = jnp.where(is_first == 1, left_a, left_b)
    right_n = jnp.where(is_last == 1, right_b, right_a)
    right_f = jnp.where(is_last == 1, zero, right_b)
    center = jnp.concatenate([even_n, odd_n, even_f, odd_f], axis=0)
    stacked = jnp.concatenate(
        [
            jnp.concatenate([left_n, even_n, left_f, even_f], axis=0),
            center,
            jnp.concatenate([odd_n, right_n, odd_f, right_f], axis=0),
        ],
        axis=1,
    )
    opening = gate(center, jnp.dot(stacked, w_first[...], preferred_element_type=jnp.float32))
    rows = 2 * units * cells
    near_part, far_part = opening[:rows], opening[rows:]
    both = jnp.concatenate([near_part, far_part], axis=1)
    result_n = gate(
        near_part, jnp.dot(both, w_second[features:], preferred_element_type=jnp.float32)
    )
    result_f = gate(
        far_part, jnp.dot(both, w_second[: 2 * features], preferred_element_type=jnp.float32)
    )
    same = jnp.where(near == 0, result_n, result_f)
    other = jnp.where(near == 0, result_f, result_n)
    half = cells // 2
    for slot in range(2):
        for unit in range(units):
            at = (slot * units + unit) * cells
            out0[slot, unit] = same[at : at + half]
            out1[slot, unit] = same[at + half : at + cells]
            out2[slot, unit] = other[at : at + half]
            out3[slot, unit] = other[at + half : at + cells]


def run_section(place, before, mine, other, weights, units, chunks, from_frames):
    slots, _, half, features = mine.shape
    shape_in = (slots, units, half, features)
    piece = pl.BlockSpec(shape_in, lambda i, at: (0, i, 0, 0))
    own = pl.BlockSpec(shape_in, lambda i, at: (0, 4 * i + at[4], 0, 0))
    block_out = pl.BlockSpec((units, 2 * half, features), lambda i, at: (i, 0, 0))
    shape = jax.ShapeDtypeStruct((chunks * units, 2 * half, features), jnp.bfloat16)
    return pl.pallas_call(
        section_kernel,
        grid_spec=pltpu.PrefetchScalarGridSpec(
            num_scalar_prefetch=1,
            grid=(chunks,),
            in_specs=([ANYWHERE, own, piece] if from_frames else [ANYWHERE, RESIDENT, RESIDENT])
            + [RESIDENT] * 4,
            out_specs=([block_out] * 2 if from_frames else [RESIDENT] * 2) + [TOKEN_SPEC],
        ),
        out_shape=[shape, shape, TOKEN],
        compiler_params=params(16),
        cost_estimate=moved(chunks * units * half * features),
        name="section",
    )(place, before, mine, other, *weights)


def run_temporal(place, before, own, far, weights, chunk, count, last):
    _, cells, features = own[0].shape
    shape = (2, count, cells // 2, features)
    block_out = pl.BlockSpec(shape, lambda i, at: (0, 0, 0, 0))
    block_own = pl.BlockSpec((count, cells, features), lambda i, at: (chunk, 0, 0))
    kept = (jax.ShapeDtypeStruct if last else pltpu.HBM)(shape, jnp.bfloat16)
    return pl.pallas_call(
        functools.partial(temporal_kernel, 0 if last else chunk),
        grid_spec=pltpu.PrefetchScalarGridSpec(
            num_scalar_prefetch=1,
            grid=(1,),
            in_specs=[ANYWHERE] + [block_own if last else RESIDENT] * 4 + [RESIDENT] * 6,
            out_specs=[RESIDENT if last else block_out] * 4 + [TOKEN_SPEC],
        ),
        out_shape=[kept] * 4 + [TOKEN],
        compiler_params=params(24),
        cost_estimate=moved(count * cells * features),
        name="temporal",
    )(place, before, *own, *far, *weights)


GROUP = ("far", "cell")
RING = ("near", "sub")


def paired(frames, w_qkv, w_out, w_up, w_down, temporal_weight_first, temporal_weight_second):
    frames_local, cells, features = frames.shape
    near_size, subs = lax.axis_size("near"), lax.axis_size("sub")
    sub, side = lax.axis_index("sub"), lax.axis_index("far")
    quarter = 2 * side + lax.axis_index("cell")
    ring = near_size * subs
    position = lax.axis_index("near") * subs + sub
    place = jnp.stack([sub, side, position == 0, position == ring - 1, quarter]).astype(jnp.int32)
    rightward = [(i, (i + 1) % ring) for i in range(ring)]
    leftward = [(target, source) for source, target in rightward]
    slots = frames_local // DILATION_FIRST
    grouped = frames.reshape(slots, DILATION_FIRST, cells, features)
    pinned = pltpu.with_memory_space_constraint(grouped, pltpu.HBM)
    units = DILATION_FIRST // 4 // CHUNKS

    def exchange(piece, delta):
        return lax.ppermute(piece, GROUP, [(i, i ^ delta) for i in range(4)])

    def halo(even, odd):
        return [even, odd, lax.ppermute(odd, RING, rightward), lax.ppermute(even, RING, leftward)]

    halves = (w_qkv, w_out, w_up, w_down, temporal_weight_first, temporal_weight_second)
    beside, cuts = run_pack(place, pinned, units, CHUNKS)
    mine = pack_weights(cuts[0][0], halves, features)
    beside = exchange(beside, 1)
    crossed = [[exchange(piece, delta) for delta, piece in zip((2, 3), cut)] for cut in cuts]
    other = lax.ppermute(mine, "sub", [(0, 1), (1, 0)])
    weights = join_weights(place, mine, mine, other, halves)
    section_weights, temporal_weights = weights[:4], weights[4:]

    even, odd, before = run_section(
        place, place, pinned, beside, section_weights, units, CHUNKS, True
    )
    own = halo(even, odd)
    far, outs = [], []
    for kind, index in ORDER:
        if kind == "s":
            even, odd, before = run_section(
                place, before, *crossed[index], section_weights, units, 1, False
            )
            far.append(halo(even, odd))
        else:
            *sent, before = run_temporal(
                place, before, own, far[index], temporal_weights, index, units, index == CHUNKS - 1
            )
            outs.append([sent[0]] + [exchange(sent[delta], delta) for delta in (1, 2, 3)])
    result = jnp.zeros_like(grouped)
    for index, received in enumerate(outs):
        for delta in range(4):
            at = (4 * index + (quarter ^ delta)) * units
            result = lax.dynamic_update_slice_in_dim(result, received[delta], at, axis=1)
    return result.reshape(frames.shape)


def solution(mesh):
    groups, tm, cell, sub = (mesh.shape[axis] for axis in ("groups", "tm", "cell", "sub"))

    def run(frames, *weights):
        frame_total, cells, _ = frames.shape
        video = frame_total // groups
        frames_local = video // (tm * sub)
        fits = (
            video == 2 * DILATION_SECOND
            and frames_local == 2 * DILATION_FIRST
            and tm % 2 == 0
            and cell == 2
            and sub == 2
            and (cells // cell) % 16 == 0
            and DILATION_FIRST % (4 * CHUNKS) == 0
        )
        if fits:
            devices = mesh.devices.reshape(groups, 2, tm // 2, cell, sub)
            axes = ("groups", "far", "near", "cell", "sub")
            used, split, body = jax.sharding.Mesh(devices, axes), ("groups", "far", "near", "sub"), paired
        else:
            used, split, body = mesh, ("groups", "tm", "sub"), general
        return jax.shard_map(
            body,
            mesh=used,
            in_specs=(P(split, "cell", None),) + (P("sub", None),) * 6,
            out_specs=P(split, "cell", None),
            check_vma=False,
        )(frames, *weights)

    return run
```

```python
import functools
import math

import jax
import jax.numpy as jnp
from jax import lax
from jax.experimental import pallas as pl
from jax.experimental.pallas import tpu as pltpu
from jax.sharding import PartitionSpec as P

HEAD_DIM = 64
DILATION_FIRST = 16
DILATION_SECOND = 256
CHUNKS = 2
ORDER = (("s", 0), ("s", 1), ("t", 0), ("t", 1))
MIB = 1024 * 1024


def with_halo(block, sides, width):
    for axis, dim in sides:
        count = lax.axis_size(axis)
        forward = [(i, i + 1) for i in range(count - 1)]
        backward = [(target, source) for source, target in forward]
        low = lax.ppermute(
            lax.slice_in_dim(block, block.shape[dim] - width, None, axis=dim), axis, forward
        )
        high = lax.ppermute(lax.slice_in_dim(block, 0, width, axis=dim), axis, backward)
        block = jnp.concatenate([low, block, high], axis=dim)
    return block


def shifted(shard, axis, by):
    size = lax.axis_size(axis)
    pairs = [(i, i + by) for i in range(size) if 0 <= i + by < size]
    return lax.ppermute(shard, axis, pairs)


def normalize(values):
    row_mean = jnp.mean(values, axis=-1, keepdims=True)
    centred = values - row_mean
    row_var = jnp.mean(centred * centred, axis=-1, keepdims=True)
    return centred * lax.rsqrt(row_var + 1e-05)


def attend(queries, key_part, value_part):
    frame_count, q_cells, features = queries.shape
    head_count = features // HEAD_DIM
    q_heads = queries.reshape(frame_count, q_cells, head_count, HEAD_DIM)
    k_heads = key_part.reshape(frame_count, -1, head_count, HEAD_DIM)
    v_heads = value_part.reshape(frame_count, -1, head_count, HEAD_DIM)
    scores = jnp.einsum(
        "fqhd,fkhd->fhqk", q_heads, k_heads, preferred_element_type=jnp.float32
    ) * HEAD_DIM ** (-0.5)
    row_max = jnp.max(scores, axis=-1, keepdims=True)
    exp_terms = jnp.exp(scores - row_max)
    attn_probs = (exp_terms / jnp.sum(exp_terms, axis=-1, keepdims=True)).astype(jnp.bfloat16)
    mixed = jnp.einsum("fhqk,fkhd->fqhd", attn_probs, v_heads, preferred_element_type=jnp.float32)
    return mixed.astype(jnp.bfloat16).reshape(frame_count, q_cells, features)


def gated_step(center, earlier, later_frames, weight):
    features = center.shape[-1]
    stacked = jnp.concatenate([earlier, center, later_frames], axis=-1).reshape(-1, 3 * features)
    preact = jnp.dot(stacked, weight, preferred_element_type=jnp.float32)
    gated_part = jnp.tanh(preact[:, :features]) * jax.nn.sigmoid(preact[:, features:])
    return (center.astype(jnp.float32) + gated_part.reshape(center.shape)).astype(jnp.bfloat16)


def general(frames, w_qkv, w_out, w_up, w_down, temporal_weight_first, temporal_weight_second):
    frames_local, cell_rows, features = frames.shape
    whole_qkv, whole_out, whole_up, whole_down, whole_tcn_a, whole_tcn_b = (
        lax.all_gather(w, "sub", axis=0, tiled=True)
        for w in (w_qkv, w_out, w_up, w_down, temporal_weight_first, temporal_weight_second)
    )
    working = lax.all_to_all(frames, "cell", split_axis=0, concat_axis=1, tiled=True)
    frame_count, cells_here = (working.shape[0], working.shape[1])
    residual = working.astype(jnp.float32)
    normed = normalize(residual).astype(jnp.bfloat16).reshape(-1, features)
    projected = jnp.dot(normed, whole_qkv, preferred_element_type=jnp.float32).astype(jnp.bfloat16)
    projected = projected.reshape(frame_count, cells_here, 3 * features)
    attended = attend(
        projected[..., :features],
        projected[..., features : 2 * features],
        projected[..., 2 * features :],
    )
    out_part = jnp.dot(
        attended.reshape(-1, features), whole_out, preferred_element_type=jnp.float32
    )
    mid_state = (residual + out_part.reshape(frame_count, cells_here, features)).astype(
        jnp.bfloat16
    )
    mid_float = lax.optimization_barrier(mid_state).astype(jnp.float32)
    normed_two = normalize(mid_float).astype(jnp.bfloat16).reshape(-1, features)
    hidden = jax.nn.gelu(jnp.dot(normed_two, whole_up, preferred_element_type=jnp.float32)).astype(
        jnp.bfloat16
    )
    down_part = jnp.dot(hidden, whole_down, preferred_element_type=jnp.float32).reshape(
        frame_count, cells_here, features
    )
    sectioned_frames = (mid_float + down_part).astype(jnp.bfloat16)
    sectioned_frames = lax.all_to_all(
        sectioned_frames, "cell", split_axis=1, concat_axis=0, tiled=True
    )
    padded_frames = with_halo(sectioned_frames, ((("tm", "sub"), 0),), DILATION_FIRST)
    earlier = padded_frames[:frames_local]
    later_frames = padded_frames[2 * DILATION_FIRST : 2 * DILATION_FIRST + frames_local]
    opening_layer = gated_step(sectioned_frames, earlier, later_frames, whole_tcn_a)
    shard_step_count = DILATION_SECOND // frames_local
    far_earlier = shifted(opening_layer, ("tm", "sub"), shard_step_count)
    far_later = shifted(opening_layer, ("tm", "sub"), -shard_step_count)
    return gated_step(opening_layer, far_earlier, far_later, whole_tcn_b)


ANYWHERE = pl.BlockSpec(memory_space=pl.ANY)
RESIDENT = pl.BlockSpec(memory_space=pltpu.VMEM)
SCALARS = pl.BlockSpec(memory_space=pltpu.SMEM)


TOKEN = jax.ShapeDtypeStruct((8, 128), jnp.float32)
TOKEN_SPEC = pl.BlockSpec((8, 128), lambda *at: (0, 0))


def params(mib):
    return pltpu.CompilerParams(vmem_limit_bytes=mib * MIB)


def moved(count):
    return pl.CostEstimate(flops=0, bytes_accessed=count, transcendentals=0)


def pack_weights_kernel(before, *refs):
    *sources, packed = refs
    width = packed.shape[1]
    at = 0
    for source in sources:
        rows = source.shape[0]
        for column in range(0, source.shape[1], width):
            packed[at : at + rows] = source[:, column : column + width]
            at += rows


def pack_weights(before, weights, width):
    rows = sum(w.size for w in weights) // width
    return pl.pallas_call(
        pack_weights_kernel,
        out_shape=jax.ShapeDtypeStruct((rows, width), weights[0].dtype),
        in_specs=[ANYWHERE] + [RESIDENT] * len(weights),
        out_specs=RESIDENT,
        compiler_params=params(8),
        cost_estimate=moved(rows * width),
        name="pack_weights",
    )(before, *weights)


def join_weights_kernel(place, before, mine, other, *wholes):
    width = mine.shape[1]
    for source, core in ((mine, place[0]), (other, 1 - place[0])):
        at = 0
        for whole in wholes:
            rows = whole.shape[0] // 2
            spot = pl.ds(pl.multiple_of(core * rows, 16), rows)
            for column in range(0, whole.shape[1], width):
                whole[spot, column : column + width] = source[at : at + rows]
                at += rows


def join_weights(place, before, mine, other, halves):
    return pl.pallas_call(
        join_weights_kernel,
        out_shape=[jax.ShapeDtypeStruct((2 * w.shape[0], w.shape[1]), w.dtype) for w in halves],
        in_specs=[SCALARS, ANYWHERE, RESIDENT, RESIDENT],
        out_specs=[RESIDENT] * len(halves),
        compiler_params=params(8),
        cost_estimate=moved(mine.size),
        name="join_weights",
    )(place, before, mine, other)


def pack_kernel(chunks, place, *refs):
    sources, (both, *cuts) = refs[: 3 * chunks], refs[3 * chunks :]
    units = sources[0].shape[1]
    for chunk in range(chunks):
        both[:, chunk * units : (chunk + 1) * units] = sources[chunk][...]
    for source, packed in zip(sources[chunks:], cuts):
        packed[...] = source[...]


def run_pack(place, grouped, units, chunks):
    slots, _, cells, features = grouped.shape
    shape = (slots, units, cells, features)
    wanted = [(delta, chunk) for chunk in range(chunks) for delta in (2, 3)]
    beside = [(1, chunk) for chunk in range(chunks)]

    def source(delta, chunk):
        return pl.BlockSpec(shape, lambda i, at: (0, 4 * chunk + (at[4] ^ delta), 0, 0))

    whole = (slots, chunks * units, cells, features)
    both, *cuts = pl.pallas_call(
        functools.partial(pack_kernel, chunks),
        grid_spec=pltpu.PrefetchScalarGridSpec(
            num_scalar_prefetch=1,
            grid=(1,),
            in_specs=[source(*piece) for piece in beside + wanted],
            out_specs=[RESIDENT] * (1 + len(wanted)),
        ),
        out_shape=[jax.ShapeDtypeStruct(whole, grouped.dtype)]
        + [jax.ShapeDtypeStruct(shape, grouped.dtype)] * len(wanted),
        compiler_params=params(8),
        cost_estimate=moved(grouped.size),
        name="pack",
    )(place, *[grouped] * len(beside + wanted))
    return both, [cuts[2 * chunk : 2 * chunk + 2] for chunk in range(chunks)]


def section_kernel(
    place,
    before,
    mine,
    other,
    w_qkv,
    w_out,
    w_up,
    w_down,
    even_ref,
    odd_ref,
    token,
):
    token[...] = jnp.zeros_like(token)
    slots, units, half, features = mine.shape
    cells = 2 * half
    parts = []
    for slot in range(slots):
        for unit in range(units):
            parts += [mine[slot, unit], other[slot, unit]]
    residual = jnp.concatenate(parts, axis=0).astype(jnp.float32)
    frame_count = slots * units
    normed = normalize(residual).astype(jnp.bfloat16)
    projected = jnp.dot(normed, w_qkv[...], preferred_element_type=jnp.float32).astype(jnp.bfloat16)
    pair_width = 2 * HEAD_DIM
    low = lax.broadcasted_iota(jnp.int32, (cells, pair_width), 1) < HEAD_DIM
    low_one = low.astype(jnp.bfloat16)
    high_one = 1 - low_one
    scale = HEAD_DIM ** (-0.5) * math.log2(math.e)
    rows = []
    for frame in range(frame_count):
        block = projected[frame * cells : (frame + 1) * cells]
        columns = []
        for pair in range(features // pair_width):
            at = pair * pair_width
            queries = block[:, at : at + pair_width]
            keys = block[:, features + at : features + at + pair_width]
            values = block[:, 2 * features + at : 2 * features + at + pair_width]
            split_keys = jnp.concatenate([keys * low_one, keys * high_one], axis=0)
            scores = lax.dot_general(
                queries, split_keys, (((1,), (1,)), ((), ())), preferred_element_type=jnp.float32
            )
            terms = []
            for head in range(2):
                own_scores = scores[:, head * cells : (head + 1) * cells]
                row_max = jnp.max(own_scores, axis=-1, keepdims=True)
                terms.append(jnp.exp2((own_scores - row_max) * scale).astype(jnp.bfloat16))
            split_values = jnp.concatenate(
                [
                    jnp.concatenate([values * low_one, low_one], axis=1),
                    jnp.concatenate([values * high_one, high_one], axis=1),
                ],
                axis=0,
            )
            mixed = jnp.dot(
                jnp.concatenate(terms, axis=1), split_values, preferred_element_type=jnp.float32
            )
            inverse = pl.reciprocal(mixed[:, pair_width:], approx=True)
            columns.append((mixed[:, :pair_width] * inverse).astype(jnp.bfloat16))
        rows.append(jnp.concatenate(columns, axis=1))
    attended = jnp.concatenate(rows, axis=0)

    mid_state = (
        residual + jnp.dot(attended, w_out[...], preferred_element_type=jnp.float32)
    ).astype(jnp.bfloat16)
    mid_float = mid_state.astype(jnp.float32)
    normed_two = normalize(mid_float).astype(jnp.bfloat16)
    total = mid_float
    width = math.gcd(w_up.shape[1], 512)
    for at in range(0, w_up.shape[1], width):
        lifted = jnp.dot(normed_two, w_up[:, at : at + width], preferred_element_type=jnp.float32)
        lifted = lifted.astype(jnp.bfloat16)
        inner = lifted * (
            math.sqrt(2 / math.pi) + (math.sqrt(2 / math.pi) * 0.044715) * (lifted * lifted)
        )
        halved = 0.5 * lifted
        hidden = halved + halved * jnp.tanh(inner)
        total = total + jnp.dot(hidden, w_down[at : at + width], preferred_element_type=jnp.float32)
    sectioned = total.astype(jnp.bfloat16)
    for unit in range(units):
        even_ref[unit] = sectioned[unit * cells : (unit + 1) * cells]
        odd_ref[unit] = sectioned[(units + unit) * cells : (units + unit + 1) * cells]


def gate(center, preact):
    features = center.shape[-1]
    preact = preact.astype(jnp.bfloat16)
    opened = 0.5 + 0.5 * jnp.tanh(0.5 * preact[:, features:])
    return center + jnp.tanh(preact[:, :features]) * opened


def temporal_kernel(chunk, place, before, *refs):
    *fields, w_first, w_second, out0, out1, out2, out3, token = refs
    token[...] = jnp.zeros_like(token)
    near, is_first, is_last = place[1], place[2], place[3]
    units, cells, features = fields[4].shape
    spans = [slice(chunk * units, (chunk + 1) * units)] * 4 + [slice(0, units)] * 4
    flat = [field[at].reshape(units * cells, features) for field, at in zip(fields, spans)]
    zero = jnp.zeros_like(flat[0])
    pairs = [(flat[i], flat[i + 4]) for i in range(4)]
    even_n, odd_n, left_a, right_a = [jnp.where(near == 0, a, b) for a, b in pairs]
    even_f, odd_f, left_b, right_b = [jnp.where(near == 0, b, a) for a, b in pairs]
    left_n = jnp.where(is_first == 1, zero, left_a)
    left_f = jnp.where(is_first == 1, left_a, left_b)
    right_n = jnp.where(is_last == 1, right_b, right_a)
    right_f = jnp.where(is_last == 1, zero, right_b)
    center = jnp.concatenate([even_n, odd_n, even_f, odd_f], axis=0)
    stacked = jnp.concatenate(
        [
            jnp.concatenate([left_n, even_n, left_f, even_f], axis=0),
            center,
            jnp.concatenate([odd_n, right_n, odd_f, right_f], axis=0),
        ],
        axis=1,
    )
    opening = gate(center, jnp.dot(stacked, w_first[...], preferred_element_type=jnp.float32))
    rows = 2 * units * cells
    near_part, far_part = opening[:rows], opening[rows:]
    both = jnp.concatenate([near_part, far_part], axis=1)
    result_n = gate(
        near_part, jnp.dot(both, w_second[features:], preferred_element_type=jnp.float32)
    )
    result_f = gate(
        far_part, jnp.dot(both, w_second[: 2 * features], preferred_element_type=jnp.float32)
    )
    same = jnp.where(near == 0, result_n, result_f)
    other = jnp.where(near == 0, result_f, result_n)
    half = cells // 2
    for slot in range(2):
        for unit in range(units):
            at = (slot * units + unit) * cells
            out0[slot, unit] = same[at : at + half]
            out1[slot, unit] = same[at + half : at + cells]
            out2[slot, unit] = other[at : at + half]
            out3[slot, unit] = other[at + half : at + cells]


def run_section(place, before, mine, other, weights, units, chunks, from_frames):
    slots, _, half, features = mine.shape
    shape_in = (slots, units, half, features)
    piece = pl.BlockSpec(shape_in, lambda i, at: (0, i, 0, 0))
    own = pl.BlockSpec(shape_in, lambda i, at: (0, 4 * i + at[4], 0, 0))
    block_out = pl.BlockSpec((units, 2 * half, features), lambda i, at: (i, 0, 0))
    held = jax.ShapeDtypeStruct if from_frames else pltpu.VMEM
    shape = held((chunks * units, 2 * half, features), jnp.bfloat16)
    return pl.pallas_call(
        section_kernel,
        grid_spec=pltpu.PrefetchScalarGridSpec(
            num_scalar_prefetch=1,
            grid=(chunks,),
            in_specs=([ANYWHERE, own, piece] if from_frames else [ANYWHERE, RESIDENT, RESIDENT])
            + [RESIDENT] * 4,
            out_specs=([block_out] * 2 if from_frames else [RESIDENT] * 2) + [TOKEN_SPEC],
        ),
        out_shape=[shape, shape, TOKEN],
        compiler_params=params(16),
        cost_estimate=moved(chunks * units * half * features),
        name="section",
    )(place, before, mine, other, *weights)


def run_temporal(place, before, own, far, weights, chunk, count, last):
    _, cells, features = own[0].shape
    shape = (2, count, cells // 2, features)
    block_out = pl.BlockSpec(shape, lambda i, at: (0, 0, 0, 0))
    block_own = pl.BlockSpec((count, cells, features), lambda i, at: (chunk, 0, 0))
    kept = (jax.ShapeDtypeStruct if last else pltpu.HBM)(shape, jnp.bfloat16)
    return pl.pallas_call(
        functools.partial(temporal_kernel, 0 if last else chunk),
        grid_spec=pltpu.PrefetchScalarGridSpec(
            num_scalar_prefetch=1,
            grid=(1,),
            in_specs=[ANYWHERE] + [block_own if last else RESIDENT] * 4 + [RESIDENT] * 6,
            out_specs=[RESIDENT if last else block_out] * 4 + [TOKEN_SPEC],
        ),
        out_shape=[kept] * 4 + [TOKEN],
        compiler_params=params(24),
        cost_estimate=moved(count * cells * features),
        name="temporal",
    )(place, before, *own, *far, *weights)


GROUP = ("far", "cell")
RING = ("near", "sub")


def paired(frames, w_qkv, w_out, w_up, w_down, temporal_weight_first, temporal_weight_second):
    frames_local, cells, features = frames.shape
    near_size, subs = lax.axis_size("near"), lax.axis_size("sub")
    sub, side = lax.axis_index("sub"), lax.axis_index("far")
    quarter = 2 * side + lax.axis_index("cell")
    ring = near_size * subs
    position = lax.axis_index("near") * subs + sub
    place = jnp.stack([sub, side, position == 0, position == ring - 1, quarter]).astype(jnp.int32)
    rightward = [(i, (i + 1) % ring) for i in range(ring)]
    leftward = [(target, source) for source, target in rightward]
    slots = frames_local // DILATION_FIRST
    grouped = frames.reshape(slots, DILATION_FIRST, cells, features)
    pinned = pltpu.with_memory_space_constraint(grouped, pltpu.HBM)
    units = DILATION_FIRST // 4 // CHUNKS

    def exchange(piece, delta):
        return lax.ppermute(piece, GROUP, [(i, i ^ delta) for i in range(4)])

    def halo(even, odd):
        return [even, odd, lax.ppermute(odd, RING, rightward), lax.ppermute(even, RING, leftward)]

    halves = (w_qkv, w_out, w_up, w_down, temporal_weight_first, temporal_weight_second)
    beside, cuts = run_pack(place, pinned, units, CHUNKS)
    mine = pack_weights(cuts[0][0], halves, features)
    beside = exchange(beside, 1)
    crossed = [[exchange(piece, delta) for delta, piece in zip((2, 3), cut)] for cut in cuts]
    other = lax.ppermute(mine, "sub", [(0, 1), (1, 0)])
    weights = join_weights(place, mine, mine, other, halves)
    section_weights, temporal_weights = weights[:4], weights[4:]

    even, odd, before = run_section(
        place, place, pinned, beside, section_weights, units, CHUNKS, True
    )
    own = halo(even, odd)
    far, outs = [], []
    for kind, index in ORDER:
        if kind == "s":
            even, odd, before = run_section(
                place, before, *crossed[index], section_weights, units, 1, False
            )
            far.append(halo(even, odd))
        else:
            last = index == CHUNKS - 1
            if last:
                own = [pltpu.with_memory_space_constraint(field, pltpu.HBM) for field in own]
            *sent, before = run_temporal(
                place, before, own, far[index], temporal_weights, index, units, last
            )
            outs.append([sent[0]] + [exchange(sent[delta], delta) for delta in (1, 2, 3)])
    result = jnp.zeros_like(grouped)
    for index, received in enumerate(outs):
        for delta in range(4):
            at = (4 * index + (quarter ^ delta)) * units
            result = lax.dynamic_update_slice_in_dim(result, received[delta], at, axis=1)
    return result.reshape(frames.shape)


def solution(mesh):
    groups, tm, cell, sub = (mesh.shape[axis] for axis in ("groups", "tm", "cell", "sub"))

    def run(frames, *weights):
        frame_total, cells, _ = frames.shape
        video = frame_total // groups
        frames_local = video // (tm * sub)
        fits = (
            video == 2 * DILATION_SECOND
            and frames_local == 2 * DILATION_FIRST
            and tm % 2 == 0
            and cell == 2
            and sub == 2
            and (cells // cell) % 16 == 0
            and DILATION_FIRST % (4 * CHUNKS) == 0
        )
        if fits:
            devices = mesh.devices.reshape(groups, 2, tm // 2, cell, sub)
            axes = ("groups", "far", "near", "cell", "sub")
            used, split, body = jax.sharding.Mesh(devices, axes), ("groups", "far", "near", "sub"), paired
        else:
            used, split, body = mesh, ("groups", "tm", "sub"), general
        return jax.shard_map(
            body,
            mesh=used,
            in_specs=(P(split, "cell", None),) + (P("sub", None),) * 6,
            out_specs=P(split, "cell", None),
            check_vma=False,
        )(frames, *weights)

    return run
```

```python
import functools
import math

import jax
import jax.numpy as jnp
from jax import lax
from jax.experimental import pallas as pl
from jax.experimental.pallas import tpu as pltpu
from jax.sharding import PartitionSpec as P

HEAD_DIM = 64
DILATION_FIRST = 16
DILATION_SECOND = 256
CHUNKS = 2
ORDER = (("s", 0), ("s", 1), ("t", 0), ("t", 1))
MIB = 1024 * 1024


def with_halo(block, sides, width):
    for axis, dim in sides:
        count = lax.axis_size(axis)
        forward = [(i, i + 1) for i in range(count - 1)]
        backward = [(target, source) for source, target in forward]
        low = lax.ppermute(
            lax.slice_in_dim(block, block.shape[dim] - width, None, axis=dim), axis, forward
        )
        high = lax.ppermute(lax.slice_in_dim(block, 0, width, axis=dim), axis, backward)
        block = jnp.concatenate([low, block, high], axis=dim)
    return block


def shifted(shard, axis, by):
    size = lax.axis_size(axis)
    pairs = [(i, i + by) for i in range(size) if 0 <= i + by < size]
    return lax.ppermute(shard, axis, pairs)


def normalize(values):
    row_mean = jnp.mean(values, axis=-1, keepdims=True)
    centred = values - row_mean
    row_var = jnp.mean(centred * centred, axis=-1, keepdims=True)
    return centred * lax.rsqrt(row_var + 1e-05)


def attend(queries, key_part, value_part):
    frame_count, q_cells, features = queries.shape
    head_count = features // HEAD_DIM
    q_heads = queries.reshape(frame_count, q_cells, head_count, HEAD_DIM)
    k_heads = key_part.reshape(frame_count, -1, head_count, HEAD_DIM)
    v_heads = value_part.reshape(frame_count, -1, head_count, HEAD_DIM)
    scores = jnp.einsum(
        "fqhd,fkhd->fhqk", q_heads, k_heads, preferred_element_type=jnp.float32
    ) * HEAD_DIM ** (-0.5)
    row_max = jnp.max(scores, axis=-1, keepdims=True)
    exp_terms = jnp.exp(scores - row_max)
    attn_probs = (exp_terms / jnp.sum(exp_terms, axis=-1, keepdims=True)).astype(jnp.bfloat16)
    mixed = jnp.einsum("fhqk,fkhd->fqhd", attn_probs, v_heads, preferred_element_type=jnp.float32)
    return mixed.astype(jnp.bfloat16).reshape(frame_count, q_cells, features)


def gated_step(center, earlier, later_frames, weight):
    features = center.shape[-1]
    stacked = jnp.concatenate([earlier, center, later_frames], axis=-1).reshape(-1, 3 * features)
    preact = jnp.dot(stacked, weight, preferred_element_type=jnp.float32)
    gated_part = jnp.tanh(preact[:, :features]) * jax.nn.sigmoid(preact[:, features:])
    return (center.astype(jnp.float32) + gated_part.reshape(center.shape)).astype(jnp.bfloat16)


def general(frames, w_qkv, w_out, w_up, w_down, temporal_weight_first, temporal_weight_second):
    frames_local, cell_rows, features = frames.shape
    whole_qkv, whole_out, whole_up, whole_down, whole_tcn_a, whole_tcn_b = (
        lax.all_gather(w, "sub", axis=0, tiled=True)
        for w in (w_qkv, w_out, w_up, w_down, temporal_weight_first, temporal_weight_second)
    )
    working = lax.all_to_all(frames, "cell", split_axis=0, concat_axis=1, tiled=True)
    frame_count, cells_here = (working.shape[0], working.shape[1])
    residual = working.astype(jnp.float32)
    normed = normalize(residual).astype(jnp.bfloat16).reshape(-1, features)
    projected = jnp.dot(normed, whole_qkv, preferred_element_type=jnp.float32).astype(jnp.bfloat16)
    projected = projected.reshape(frame_count, cells_here, 3 * features)
    attended = attend(
        projected[..., :features],
        projected[..., features : 2 * features],
        projected[..., 2 * features :],
    )
    out_part = jnp.dot(
        attended.reshape(-1, features), whole_out, preferred_element_type=jnp.float32
    )
    mid_state = (residual + out_part.reshape(frame_count, cells_here, features)).astype(
        jnp.bfloat16
    )
    mid_float = lax.optimization_barrier(mid_state).astype(jnp.float32)
    normed_two = normalize(mid_float).astype(jnp.bfloat16).reshape(-1, features)
    hidden = jax.nn.gelu(jnp.dot(normed_two, whole_up, preferred_element_type=jnp.float32)).astype(
        jnp.bfloat16
    )
    down_part = jnp.dot(hidden, whole_down, preferred_element_type=jnp.float32).reshape(
        frame_count, cells_here, features
    )
    sectioned_frames = (mid_float + down_part).astype(jnp.bfloat16)
    sectioned_frames = lax.all_to_all(
        sectioned_frames, "cell", split_axis=1, concat_axis=0, tiled=True
    )
    padded_frames = with_halo(sectioned_frames, ((("tm", "sub"), 0),), DILATION_FIRST)
    earlier = padded_frames[:frames_local]
    later_frames = padded_frames[2 * DILATION_FIRST : 2 * DILATION_FIRST + frames_local]
    opening_layer = gated_step(sectioned_frames, earlier, later_frames, whole_tcn_a)
    shard_step_count = DILATION_SECOND // frames_local
    far_earlier = shifted(opening_layer, ("tm", "sub"), shard_step_count)
    far_later = shifted(opening_layer, ("tm", "sub"), -shard_step_count)
    return gated_step(opening_layer, far_earlier, far_later, whole_tcn_b)


ANYWHERE = pl.BlockSpec(memory_space=pl.ANY)
RESIDENT = pl.BlockSpec(memory_space=pltpu.VMEM)
SCALARS = pl.BlockSpec(memory_space=pltpu.SMEM)


TOKEN = jax.ShapeDtypeStruct((8, 128), jnp.float32)
TOKEN_SPEC = pl.BlockSpec((8, 128), lambda *at: (0, 0))


def params(mib):
    return pltpu.CompilerParams(vmem_limit_bytes=mib * MIB)


def moved(count):
    return pl.CostEstimate(flops=0, bytes_accessed=count, transcendentals=0)


def pack_weights_kernel(before, *refs):
    *sources, packed = refs
    width = packed.shape[1]
    at = 0
    for source in sources:
        rows = source.shape[0]
        for column in range(0, source.shape[1], width):
            packed[at : at + rows] = source[:, column : column + width]
            at += rows


def pack_weights(before, weights, width):
    rows = sum(w.size for w in weights) // width
    return pl.pallas_call(
        pack_weights_kernel,
        out_shape=jax.ShapeDtypeStruct((rows, width), weights[0].dtype),
        in_specs=[ANYWHERE] + [RESIDENT] * len(weights),
        out_specs=RESIDENT,
        compiler_params=params(8),
        cost_estimate=moved(rows * width),
        name="pack_weights",
    )(before, *weights)


def join_weights_kernel(place, before, mine, other, *wholes):
    width = mine.shape[1]
    for source, core in ((mine, place[0]), (other, 1 - place[0])):
        at = 0
        for whole in wholes:
            rows = whole.shape[0] // 2
            spot = pl.ds(pl.multiple_of(core * rows, 16), rows)
            for column in range(0, whole.shape[1], width):
                whole[spot, column : column + width] = source[at : at + rows]
                at += rows


def join_weights(place, before, mine, other, halves):
    return pl.pallas_call(
        join_weights_kernel,
        out_shape=[jax.ShapeDtypeStruct((2 * w.shape[0], w.shape[1]), w.dtype) for w in halves],
        in_specs=[SCALARS, ANYWHERE, RESIDENT, RESIDENT],
        out_specs=[RESIDENT] * len(halves),
        compiler_params=params(8),
        cost_estimate=moved(mine.size),
        name="join_weights",
    )(place, before, mine, other)


def pack_kernel(chunks, place, *refs):
    sources, (both, *cuts) = refs[: 3 * chunks], refs[3 * chunks :]
    units = sources[0].shape[1]
    for chunk in range(chunks):
        both[:, chunk * units : (chunk + 1) * units] = sources[chunk][...]
    for source, packed in zip(sources[chunks:], cuts):
        packed[...] = source[...]


def run_pack(place, grouped, units, chunks):
    slots, _, cells, features = grouped.shape
    shape = (slots, units, cells, features)
    wanted = [(delta, chunk) for chunk in range(chunks) for delta in (2, 3)]
    beside = [(1, chunk) for chunk in range(chunks)]

    def source(delta, chunk):
        return pl.BlockSpec(shape, lambda i, at: (0, 4 * chunk + (at[4] ^ delta), 0, 0))

    whole = (slots, chunks * units, cells, features)
    both, *cuts = pl.pallas_call(
        functools.partial(pack_kernel, chunks),
        grid_spec=pltpu.PrefetchScalarGridSpec(
            num_scalar_prefetch=1,
            grid=(1,),
            in_specs=[source(*piece) for piece in beside + wanted],
            out_specs=[RESIDENT] * (1 + len(wanted)),
        ),
        out_shape=[jax.ShapeDtypeStruct(whole, grouped.dtype)]
        + [jax.ShapeDtypeStruct(shape, grouped.dtype)] * len(wanted),
        compiler_params=params(8),
        cost_estimate=moved(grouped.size),
        name="pack",
    )(place, *[grouped] * len(beside + wanted))
    return both, [cuts[2 * chunk : 2 * chunk + 2] for chunk in range(chunks)]


def section_rows(parts, cells, w_qkv, w_out, w_up, w_down):
    features = parts[0].shape[-1]
    residual = jnp.concatenate(parts, axis=0).astype(jnp.float32)
    frame_count = residual.shape[0] // cells
    normed = normalize(residual).astype(jnp.bfloat16)
    projected = jnp.dot(normed, w_qkv[...], preferred_element_type=jnp.float32).astype(jnp.bfloat16)
    pair_width = 2 * HEAD_DIM
    low = lax.broadcasted_iota(jnp.int32, (cells, pair_width), 1) < HEAD_DIM
    low_one = low.astype(jnp.bfloat16)
    high_one = 1 - low_one
    scale = HEAD_DIM ** (-0.5) * math.log2(math.e)
    rows = []
    for frame in range(frame_count):
        block = projected[frame * cells : (frame + 1) * cells]
        columns = []
        for pair in range(features // pair_width):
            at = pair * pair_width
            queries = block[:, at : at + pair_width]
            keys = block[:, features + at : features + at + pair_width]
            values = block[:, 2 * features + at : 2 * features + at + pair_width]
            split_keys = jnp.concatenate([keys * low_one, keys * high_one], axis=0)
            scores = lax.dot_general(
                queries, split_keys, (((1,), (1,)), ((), ())), preferred_element_type=jnp.float32
            )
            terms = []
            for head in range(2):
                own_scores = scores[:, head * cells : (head + 1) * cells]
                row_max = jnp.max(own_scores, axis=-1, keepdims=True)
                terms.append(jnp.exp2((own_scores - row_max) * scale).astype(jnp.bfloat16))
            split_values = jnp.concatenate(
                [
                    jnp.concatenate([values * low_one, low_one], axis=1),
                    jnp.concatenate([values * high_one, high_one], axis=1),
                ],
                axis=0,
            )
            mixed = jnp.dot(
                jnp.concatenate(terms, axis=1), split_values, preferred_element_type=jnp.float32
            )
            inverse = pl.reciprocal(mixed[:, pair_width:], approx=True)
            columns.append((mixed[:, :pair_width] * inverse).astype(jnp.bfloat16))
        rows.append(jnp.concatenate(columns, axis=1))
    attended = jnp.concatenate(rows, axis=0)

    mid_state = (
        residual + jnp.dot(attended, w_out[...], preferred_element_type=jnp.float32)
    ).astype(jnp.bfloat16)
    mid_float = mid_state.astype(jnp.float32)
    normed_two = normalize(mid_float).astype(jnp.bfloat16)
    total = mid_float
    width = math.gcd(w_up.shape[1], 512)
    for at in range(0, w_up.shape[1], width):
        lifted = jnp.dot(normed_two, w_up[:, at : at + width], preferred_element_type=jnp.float32)
        lifted = lifted.astype(jnp.bfloat16)
        inner = lifted * (
            math.sqrt(2 / math.pi) + (math.sqrt(2 / math.pi) * 0.044715) * (lifted * lifted)
        )
        halved = 0.5 * lifted
        hidden = halved + halved * jnp.tanh(inner)
        total = total + jnp.dot(hidden, w_down[at : at + width], preferred_element_type=jnp.float32)
    return total.astype(jnp.bfloat16)


def section_kernel(
    place,
    before,
    mine,
    other,
    w_qkv,
    w_out,
    w_up,
    w_down,
    even_ref,
    odd_ref,
    token,
):
    token[...] = jnp.zeros_like(token)
    slots, units, half, features = mine.shape
    cells = 2 * half
    parts = []
    for slot in range(slots):
        for unit in range(units):
            parts += [mine[slot, unit], other[slot, unit]]
    frames = slots * units
    per = max(frames // 2, 1)
    done = []
    for at in range(0, frames, per):
        done.append(section_rows(parts[2 * at : 2 * (at + per)], cells, w_qkv, w_out, w_up, w_down))
    sectioned = jnp.concatenate(done, axis=0)
    for unit in range(units):
        even_ref[unit] = sectioned[unit * cells : (unit + 1) * cells]
        odd_ref[unit] = sectioned[(units + unit) * cells : (units + unit + 1) * cells]


def gate(center, preact):
    features = center.shape[-1]
    preact = preact.astype(jnp.bfloat16)
    opened = 0.5 + 0.5 * jnp.tanh(0.5 * preact[:, features:])
    return center + jnp.tanh(preact[:, :features]) * opened


def temporal_unit(place, fields, w_first, w_second, outs, own_unit, far_unit):
    near, is_first, is_last = place[1], place[2], place[3]
    cells, features = fields[0].shape[1:]
    spans = [slice(own_unit, own_unit + 1)] * 4 + [slice(far_unit, far_unit + 1)] * 4
    units = 1
    flat = [field[at].reshape(units * cells, features) for field, at in zip(fields, spans)]
    zero = jnp.zeros_like(flat[0])
    pairs = [(flat[i], flat[i + 4]) for i in range(4)]
    even_n, odd_n, left_a, right_a = [jnp.where(near == 0, a, b) for a, b in pairs]
    even_f, odd_f, left_b, right_b = [jnp.where(near == 0, b, a) for a, b in pairs]
    left_n = jnp.where(is_first == 1, zero, left_a)
    left_f = jnp.where(is_first == 1, left_a, left_b)
    right_n = jnp.where(is_last == 1, right_b, right_a)
    right_f = jnp.where(is_last == 1, zero, right_b)
    center = jnp.concatenate([even_n, odd_n, even_f, odd_f], axis=0)
    stacked = jnp.concatenate(
        [
            jnp.concatenate([left_n, even_n, left_f, even_f], axis=0),
            center,
            jnp.concatenate([odd_n, right_n, odd_f, right_f], axis=0),
        ],
        axis=1,
    )
    opening = gate(center, jnp.dot(stacked, w_first[...], preferred_element_type=jnp.float32))
    rows = 2 * units * cells
    near_part, far_part = opening[:rows], opening[rows:]
    both = jnp.concatenate([near_part, far_part], axis=1)
    result_n = gate(
        near_part, jnp.dot(both, w_second[features:], preferred_element_type=jnp.float32)
    )
    result_f = gate(
        far_part, jnp.dot(both, w_second[: 2 * features], preferred_element_type=jnp.float32)
    )
    same = jnp.where(near == 0, result_n, result_f)
    other = jnp.where(near == 0, result_f, result_n)
    half = cells // 2
    for slot in range(2):
        at = slot * cells
        outs[0][slot, far_unit] = same[at : at + half]
        outs[1][slot, far_unit] = same[at + half : at + cells]
        outs[2][slot, far_unit] = other[at : at + half]
        outs[3][slot, far_unit] = other[at + half : at + cells]


def temporal_kernel(chunk, place, before, *refs):
    fields, (w_first, w_second, *outs, token) = refs[:8], refs[8:]
    token[...] = jnp.zeros_like(token)
    count = fields[4].shape[0]
    for unit in range(count):
        temporal_unit(place, fields, w_first, w_second, outs, chunk * count + unit, unit)


def run_section(place, before, mine, other, weights, units, chunks, from_frames):
    slots, _, half, features = mine.shape
    shape_in = (slots, units, half, features)
    piece = pl.BlockSpec(shape_in, lambda i, at: (0, i, 0, 0))
    own = pl.BlockSpec(shape_in, lambda i, at: (0, 4 * i + at[4], 0, 0))
    block_out = pl.BlockSpec((units, 2 * half, features), lambda i, at: (i, 0, 0))
    held = jax.ShapeDtypeStruct if from_frames else pltpu.VMEM
    shape = held((chunks * units, 2 * half, features), jnp.bfloat16)
    return pl.pallas_call(
        section_kernel,
        grid_spec=pltpu.PrefetchScalarGridSpec(
            num_scalar_prefetch=1,
            grid=(chunks,),
            in_specs=([ANYWHERE, own, piece] if from_frames else [ANYWHERE, RESIDENT, RESIDENT])
            + [RESIDENT] * 4,
            out_specs=([block_out] * 2 if from_frames else [RESIDENT] * 2) + [TOKEN_SPEC],
        ),
        out_shape=[shape, shape, TOKEN],
        compiler_params=params(16),
        cost_estimate=moved(chunks * units * half * features),
        name="section",
    )(place, before, mine, other, *weights)


def run_temporal(place, before, own, far, weights, chunk, count, last):
    _, cells, features = own[0].shape
    shape = (2, count, cells // 2, features)
    block_out = pl.BlockSpec(shape, lambda i, at: (0, 0, 0, 0))
    block_own = pl.BlockSpec((count, cells, features), lambda i, at: (chunk, 0, 0))
    kept = (jax.ShapeDtypeStruct if last else pltpu.HBM)(shape, jnp.bfloat16)
    return pl.pallas_call(
        functools.partial(temporal_kernel, 0 if last else chunk),
        grid_spec=pltpu.PrefetchScalarGridSpec(
            num_scalar_prefetch=1,
            grid=(1,),
            in_specs=[ANYWHERE] + [block_own if last else RESIDENT] * 4 + [RESIDENT] * 6,
            out_specs=[RESIDENT if last else block_out] * 4 + [TOKEN_SPEC],
        ),
        out_shape=[kept] * 4 + [TOKEN],
        compiler_params=params(24),
        cost_estimate=moved(count * cells * features),
        name="temporal",
    )(place, before, *own, *far, *weights)


GROUP = ("far", "cell")
RING = ("near", "sub")


def paired(frames, w_qkv, w_out, w_up, w_down, temporal_weight_first, temporal_weight_second):
    frames_local, cells, features = frames.shape
    near_size, subs = lax.axis_size("near"), lax.axis_size("sub")
    sub, side = lax.axis_index("sub"), lax.axis_index("far")
    quarter = 2 * side + lax.axis_index("cell")
    ring = near_size * subs
    position = lax.axis_index("near") * subs + sub
    place = jnp.stack([sub, side, position == 0, position == ring - 1, quarter]).astype(jnp.int32)
    rightward = [(i, (i + 1) % ring) for i in range(ring)]
    leftward = [(target, source) for source, target in rightward]
    slots = frames_local // DILATION_FIRST
    grouped = frames.reshape(slots, DILATION_FIRST, cells, features)
    pinned = pltpu.with_memory_space_constraint(grouped, pltpu.HBM)
    units = DILATION_FIRST // 4 // CHUNKS

    def exchange(piece, delta):
        return lax.ppermute(piece, GROUP, [(i, i ^ delta) for i in range(4)])

    def halo(even, odd):
        return [even, odd, lax.ppermute(odd, RING, rightward), lax.ppermute(even, RING, leftward)]

    halves = (w_qkv, w_out, w_up, w_down, temporal_weight_first, temporal_weight_second)
    beside, cuts = run_pack(place, pinned, units, CHUNKS)
    mine = pack_weights(cuts[0][0], halves, features)
    beside = exchange(beside, 1)
    crossed = [[exchange(piece, delta) for delta, piece in zip((2, 3), cut)] for cut in cuts]
    other = lax.ppermute(mine, "sub", [(0, 1), (1, 0)])
    weights = join_weights(place, mine, mine, other, halves)
    section_weights, temporal_weights = weights[:4], weights[4:]

    even, odd, before = run_section(
        place, place, pinned, beside, section_weights, units, CHUNKS, True
    )
    own = halo(even, odd)
    far, outs = [], []
    for kind, index in ORDER:
        if kind == "s":
            even, odd, before = run_section(
                place, before, *crossed[index], section_weights, units, 1, False
            )
            far.append(halo(even, odd))
        else:
            last = index == CHUNKS - 1
            if last:
                own = [pltpu.with_memory_space_constraint(field, pltpu.HBM) for field in own]
            *sent, before = run_temporal(
                place, before, own, far[index], temporal_weights, index, units, last
            )
            outs.append([sent[0]] + [exchange(sent[delta], delta) for delta in (1, 2, 3)])
    result = jnp.zeros_like(grouped)
    for index, received in enumerate(outs):
        for delta in range(4):
            at = (4 * index + (quarter ^ delta)) * units
            result = lax.dynamic_update_slice_in_dim(result, received[delta], at, axis=1)
    return result.reshape(frames.shape)


def solution(mesh):
    groups, tm, cell, sub = (mesh.shape[axis] for axis in ("groups", "tm", "cell", "sub"))

    def run(frames, *weights):
        frame_total, cells, _ = frames.shape
        video = frame_total // groups
        frames_local = video // (tm * sub)
        fits = (
            video == 2 * DILATION_SECOND
            and frames_local == 2 * DILATION_FIRST
            and tm % 2 == 0
            and cell == 2
            and sub == 2
            and (cells // cell) % 16 == 0
            and DILATION_FIRST % (4 * CHUNKS) == 0
        )
        if fits:
            devices = mesh.devices.reshape(groups, 2, tm // 2, cell, sub)
            axes = ("groups", "far", "near", "cell", "sub")
            used, split, body = jax.sharding.Mesh(devices, axes), ("groups", "far", "near", "sub"), paired
        else:
            used, split, body = mesh, ("groups", "tm", "sub"), general
        return jax.shard_map(
            body,
            mesh=used,
            in_specs=(P(split, "cell", None),) + (P("sub", None),) * 6,
            out_specs=P(split, "cell", None),
            check_vma=False,
        )(frames, *weights)

    return run
```

```python
import functools
import math

import jax
import jax.numpy as jnp
from jax import lax
from jax.experimental import pallas as pl
from jax.experimental.pallas import tpu as pltpu
from jax.sharding import PartitionSpec as P

HEAD_DIM = 64
DILATION_FIRST = 16
DILATION_SECOND = 256
CHUNKS = 2
ORDER = (("s", 0), ("s", 1), ("t", 0), ("t", 1))
MIB = 1024 * 1024


def with_halo(block, sides, width):
    for axis, dim in sides:
        count = lax.axis_size(axis)
        forward = [(i, i + 1) for i in range(count - 1)]
        backward = [(target, source) for source, target in forward]
        low = lax.ppermute(
            lax.slice_in_dim(block, block.shape[dim] - width, None, axis=dim), axis, forward
        )
        high = lax.ppermute(lax.slice_in_dim(block, 0, width, axis=dim), axis, backward)
        block = jnp.concatenate([low, block, high], axis=dim)
    return block


def shifted(shard, axis, by):
    size = lax.axis_size(axis)
    pairs = [(i, i + by) for i in range(size) if 0 <= i + by < size]
    return lax.ppermute(shard, axis, pairs)


def normalize(values):
    row_mean = jnp.mean(values, axis=-1, keepdims=True)
    centred = values - row_mean
    row_var = jnp.mean(centred * centred, axis=-1, keepdims=True)
    return centred * lax.rsqrt(row_var + 1e-05)


def attend(queries, key_part, value_part):
    frame_count, q_cells, features = queries.shape
    head_count = features // HEAD_DIM
    q_heads = queries.reshape(frame_count, q_cells, head_count, HEAD_DIM)
    k_heads = key_part.reshape(frame_count, -1, head_count, HEAD_DIM)
    v_heads = value_part.reshape(frame_count, -1, head_count, HEAD_DIM)
    scores = jnp.einsum(
        "fqhd,fkhd->fhqk", q_heads, k_heads, preferred_element_type=jnp.float32
    ) * HEAD_DIM ** (-0.5)
    row_max = jnp.max(scores, axis=-1, keepdims=True)
    exp_terms = jnp.exp(scores - row_max)
    attn_probs = (exp_terms / jnp.sum(exp_terms, axis=-1, keepdims=True)).astype(jnp.bfloat16)
    mixed = jnp.einsum("fhqk,fkhd->fqhd", attn_probs, v_heads, preferred_element_type=jnp.float32)
    return mixed.astype(jnp.bfloat16).reshape(frame_count, q_cells, features)


def gated_step(center, earlier, later_frames, weight):
    features = center.shape[-1]
    stacked = jnp.concatenate([earlier, center, later_frames], axis=-1).reshape(-1, 3 * features)
    preact = jnp.dot(stacked, weight, preferred_element_type=jnp.float32)
    gated_part = jnp.tanh(preact[:, :features]) * jax.nn.sigmoid(preact[:, features:])
    return (center.astype(jnp.float32) + gated_part.reshape(center.shape)).astype(jnp.bfloat16)


def general(frames, w_qkv, w_out, w_up, w_down, temporal_weight_first, temporal_weight_second):
    frames_local, cell_rows, features = frames.shape
    whole_qkv, whole_out, whole_up, whole_down, whole_tcn_a, whole_tcn_b = (
        lax.all_gather(w, "sub", axis=0, tiled=True)
        for w in (w_qkv, w_out, w_up, w_down, temporal_weight_first, temporal_weight_second)
    )
    working = lax.all_to_all(frames, "cell", split_axis=0, concat_axis=1, tiled=True)
    frame_count, cells_here = (working.shape[0], working.shape[1])
    residual = working.astype(jnp.float32)
    normed = normalize(residual).astype(jnp.bfloat16).reshape(-1, features)
    projected = jnp.dot(normed, whole_qkv, preferred_element_type=jnp.float32).astype(jnp.bfloat16)
    projected = projected.reshape(frame_count, cells_here, 3 * features)
    attended = attend(
        projected[..., :features],
        projected[..., features : 2 * features],
        projected[..., 2 * features :],
    )
    out_part = jnp.dot(
        attended.reshape(-1, features), whole_out, preferred_element_type=jnp.float32
    )
    mid_state = (residual + out_part.reshape(frame_count, cells_here, features)).astype(
        jnp.bfloat16
    )
    mid_float = lax.optimization_barrier(mid_state).astype(jnp.float32)
    normed_two = normalize(mid_float).astype(jnp.bfloat16).reshape(-1, features)
    hidden = jax.nn.gelu(jnp.dot(normed_two, whole_up, preferred_element_type=jnp.float32)).astype(
        jnp.bfloat16
    )
    down_part = jnp.dot(hidden, whole_down, preferred_element_type=jnp.float32).reshape(
        frame_count, cells_here, features
    )
    sectioned_frames = (mid_float + down_part).astype(jnp.bfloat16)
    sectioned_frames = lax.all_to_all(
        sectioned_frames, "cell", split_axis=1, concat_axis=0, tiled=True
    )
    padded_frames = with_halo(sectioned_frames, ((("tm", "sub"), 0),), DILATION_FIRST)
    earlier = padded_frames[:frames_local]
    later_frames = padded_frames[2 * DILATION_FIRST : 2 * DILATION_FIRST + frames_local]
    opening_layer = gated_step(sectioned_frames, earlier, later_frames, whole_tcn_a)
    shard_step_count = DILATION_SECOND // frames_local
    far_earlier = shifted(opening_layer, ("tm", "sub"), shard_step_count)
    far_later = shifted(opening_layer, ("tm", "sub"), -shard_step_count)
    return gated_step(opening_layer, far_earlier, far_later, whole_tcn_b)


ANYWHERE = pl.BlockSpec(memory_space=pl.ANY)
RESIDENT = pl.BlockSpec(memory_space=pltpu.VMEM)
SCALARS = pl.BlockSpec(memory_space=pltpu.SMEM)


TOKEN = jax.ShapeDtypeStruct((8, 128), jnp.float32)
TOKEN_SPEC = pl.BlockSpec((8, 128), lambda *at: (0, 0))


def params(mib):
    return pltpu.CompilerParams(vmem_limit_bytes=mib * MIB)


def moved(count):
    return pl.CostEstimate(flops=0, bytes_accessed=count, transcendentals=0)


def pack_weights_kernel(before, *refs):
    *sources, packed = refs
    width = packed.shape[1]
    at = 0
    for source in sources:
        rows = source.shape[0]
        for column in range(0, source.shape[1], width):
            packed[at : at + rows] = source[:, column : column + width]
            at += rows


def pack_weights(before, weights, width):
    rows = sum(w.size for w in weights) // width
    return pl.pallas_call(
        pack_weights_kernel,
        out_shape=jax.ShapeDtypeStruct((rows, width), weights[0].dtype),
        in_specs=[ANYWHERE] + [RESIDENT] * len(weights),
        out_specs=RESIDENT,
        compiler_params=params(8),
        cost_estimate=moved(rows * width),
        name="pack_weights",
    )(before, *weights)


def join_weights_kernel(place, before, mine, other, *wholes):
    width = mine.shape[1]
    for source, core in ((mine, place[0]), (other, 1 - place[0])):
        at = 0
        for whole in wholes:
            rows = whole.shape[0] // 2
            spot = pl.ds(pl.multiple_of(core * rows, 16), rows)
            for column in range(0, whole.shape[1], width):
                whole[spot, column : column + width] = source[at : at + rows]
                at += rows


def join_weights(place, before, mine, other, halves):
    return pl.pallas_call(
        join_weights_kernel,
        out_shape=[jax.ShapeDtypeStruct((2 * w.shape[0], w.shape[1]), w.dtype) for w in halves],
        in_specs=[SCALARS, ANYWHERE, RESIDENT, RESIDENT],
        out_specs=[RESIDENT] * len(halves),
        compiler_params=params(8),
        cost_estimate=moved(mine.size),
        name="join_weights",
    )(place, before, mine, other)


def pack_kernel(chunks, place, *refs):
    sources, (both, *cuts) = refs[: 3 * chunks], refs[3 * chunks :]
    units = sources[0].shape[1]
    for chunk in range(chunks):
        both[:, chunk * units : (chunk + 1) * units] = sources[chunk][...]
    for source, packed in zip(sources[chunks:], cuts):
        packed[...] = source[...]


def run_pack(place, grouped, units, chunks):
    slots, _, cells, features = grouped.shape
    shape = (slots, units, cells, features)
    wanted = [(delta, chunk) for chunk in range(chunks) for delta in (2, 3)]
    beside = [(1, chunk) for chunk in range(chunks)]

    def source(delta, chunk):
        return pl.BlockSpec(shape, lambda i, at: (0, 4 * chunk + (at[4] ^ delta), 0, 0))

    whole = (slots, chunks * units, cells, features)
    both, *cuts = pl.pallas_call(
        functools.partial(pack_kernel, chunks),
        grid_spec=pltpu.PrefetchScalarGridSpec(
            num_scalar_prefetch=1,
            grid=(1,),
            in_specs=[source(*piece) for piece in beside + wanted],
            out_specs=[RESIDENT] * (1 + len(wanted)),
        ),
        out_shape=[jax.ShapeDtypeStruct(whole, grouped.dtype)]
        + [jax.ShapeDtypeStruct(shape, grouped.dtype)] * len(wanted),
        compiler_params=params(8),
        cost_estimate=moved(grouped.size),
        name="pack",
    )(place, *[grouped] * len(beside + wanted))
    return both, [cuts[2 * chunk : 2 * chunk + 2] for chunk in range(chunks)]


def section_kernel(
    place,
    before,
    mine,
    other,
    w_qkv,
    w_out,
    w_up,
    w_down,
    even_ref,
    odd_ref,
    token,
):
    token[...] = jnp.zeros_like(token)
    slots, units, half, features = mine.shape
    cells = 2 * half
    parts = []
    for slot in range(slots):
        for unit in range(units):
            parts += [mine[slot, unit], other[slot, unit]]
    residual = jnp.concatenate(parts, axis=0).astype(jnp.float32)
    frame_count = slots * units
    normed = normalize(residual).astype(jnp.bfloat16)
    projected = jnp.dot(normed, w_qkv[...], preferred_element_type=jnp.float32).astype(jnp.bfloat16)
    pair_width = 2 * HEAD_DIM
    low = lax.broadcasted_iota(jnp.int32, (cells, pair_width), 1) < HEAD_DIM
    low_one = low.astype(jnp.bfloat16)
    high_one = 1 - low_one
    scale = HEAD_DIM ** (-0.5) * math.log2(math.e)
    rows = []
    for frame in range(frame_count):
        block = projected[frame * cells : (frame + 1) * cells]
        columns = []
        for pair in range(features // pair_width):
            at = pair * pair_width
            queries = block[:, at : at + pair_width]
            keys = block[:, features + at : features + at + pair_width]
            values = block[:, 2 * features + at : 2 * features + at + pair_width]
            split_keys = jnp.concatenate([keys * low_one, keys * high_one], axis=0)
            scores = lax.dot_general(
                queries, split_keys, (((1,), (1,)), ((), ())), preferred_element_type=jnp.float32
            )
            terms = []
            for head in range(2):
                own_scores = scores[:, head * cells : (head + 1) * cells]
                row_max = jnp.max(own_scores, axis=-1, keepdims=True)
                terms.append(jnp.exp2((own_scores - row_max) * scale).astype(jnp.bfloat16))
            split_values = jnp.concatenate(
                [
                    jnp.concatenate([values * low_one, low_one], axis=1),
                    jnp.concatenate([values * high_one, high_one], axis=1),
                ],
                axis=0,
            )
            mixed = jnp.dot(
                jnp.concatenate(terms, axis=1), split_values, preferred_element_type=jnp.float32
            )
            inverse = pl.reciprocal(mixed[:, pair_width:], approx=True)
            columns.append((mixed[:, :pair_width] * inverse).astype(jnp.bfloat16))
        rows.append(jnp.concatenate(columns, axis=1))
    attended = jnp.concatenate(rows, axis=0)

    mid_state = (
        residual + jnp.dot(attended, w_out[...], preferred_element_type=jnp.float32)
    ).astype(jnp.bfloat16)
    mid_float = mid_state.astype(jnp.float32)
    normed_two = normalize(mid_float).astype(jnp.bfloat16)
    total = mid_float
    width = math.gcd(w_up.shape[1], 512)
    for at in range(0, w_up.shape[1], width):
        lifted = jnp.dot(normed_two, w_up[:, at : at + width], preferred_element_type=jnp.float32)
        lifted = lifted.astype(jnp.bfloat16)
        inner = lifted * (
            math.sqrt(2 / math.pi) + (math.sqrt(2 / math.pi) * 0.044715) * (lifted * lifted)
        )
        halved = 0.5 * lifted
        hidden = halved + halved * jnp.tanh(inner)
        total = total + jnp.dot(hidden, w_down[at : at + width], preferred_element_type=jnp.float32)
    sectioned = total.astype(jnp.bfloat16)
    for unit in range(units):
        even_ref[unit] = sectioned[unit * cells : (unit + 1) * cells]
        odd_ref[unit] = sectioned[(units + unit) * cells : (units + unit + 1) * cells]


def gate(center, preact):
    features = center.shape[-1]
    preact = preact.astype(jnp.bfloat16)
    opened = 0.5 + 0.5 * jnp.tanh(0.5 * preact[:, features:])
    return center + jnp.tanh(preact[:, :features]) * opened


def temporal_unit(place, fields, w_first, w_second, outs, own_unit, far_unit):
    near, is_first, is_last = place[1], place[2], place[3]
    cells, features = fields[0].shape[1:]
    spans = [slice(own_unit, own_unit + 1)] * 4 + [slice(far_unit, far_unit + 1)] * 4
    units = 1
    flat = [field[at].reshape(units * cells, features) for field, at in zip(fields, spans)]
    zero = jnp.zeros_like(flat[0])
    pairs = [(flat[i], flat[i + 4]) for i in range(4)]
    even_n, odd_n, left_a, right_a = [jnp.where(near == 0, a, b) for a, b in pairs]
    even_f, odd_f, left_b, right_b = [jnp.where(near == 0, b, a) for a, b in pairs]
    left_n = jnp.where(is_first == 1, zero, left_a)
    left_f = jnp.where(is_first == 1, left_a, left_b)
    right_n = jnp.where(is_last == 1, right_b, right_a)
    right_f = jnp.where(is_last == 1, zero, right_b)
    center = jnp.concatenate([even_n, odd_n, even_f, odd_f], axis=0)
    stacked = jnp.concatenate(
        [
            jnp.concatenate([left_n, even_n, left_f, even_f], axis=0),
            center,
            jnp.concatenate([odd_n, right_n, odd_f, right_f], axis=0),
        ],
        axis=1,
    )
    opening = gate(center, jnp.dot(stacked, w_first[...], preferred_element_type=jnp.float32))
    rows = 2 * units * cells
    near_part, far_part = opening[:rows], opening[rows:]
    both = jnp.concatenate([near_part, far_part], axis=1)
    result_n = gate(
        near_part, jnp.dot(both, w_second[features:], preferred_element_type=jnp.float32)
    )
    result_f = gate(
        far_part, jnp.dot(both, w_second[: 2 * features], preferred_element_type=jnp.float32)
    )
    same = jnp.where(near == 0, result_n, result_f)
    other = jnp.where(near == 0, result_f, result_n)
    half = cells // 2
    for slot in range(2):
        at = slot * cells
        outs[0][slot, far_unit] = same[at : at + half]
        outs[1][slot, far_unit] = same[at + half : at + cells]
        outs[2][slot, far_unit] = other[at : at + half]
        outs[3][slot, far_unit] = other[at + half : at + cells]


def temporal_kernel(chunk, place, before, *refs):
    fields, (w_first, w_second, *outs, token) = refs[:8], refs[8:]
    token[...] = jnp.zeros_like(token)
    count = fields[4].shape[0]
    for unit in range(count):
        temporal_unit(place, fields, w_first, w_second, outs, chunk * count + unit, unit)


def run_section(place, before, mine, other, weights, units, chunks, from_frames):
    slots, _, half, features = mine.shape
    shape_in = (slots, units, half, features)
    piece = pl.BlockSpec(shape_in, lambda i, at: (0, i, 0, 0))
    own = pl.BlockSpec(shape_in, lambda i, at: (0, 4 * i + at[4], 0, 0))
    block_out = pl.BlockSpec((units, 2 * half, features), lambda i, at: (i, 0, 0))
    held = jax.ShapeDtypeStruct if from_frames else pltpu.VMEM
    shape = held((chunks * units, 2 * half, features), jnp.bfloat16)
    return pl.pallas_call(
        section_kernel,
        grid_spec=pltpu.PrefetchScalarGridSpec(
            num_scalar_prefetch=1,
            grid=(chunks,),
            in_specs=([ANYWHERE, own, piece] if from_frames else [ANYWHERE, RESIDENT, RESIDENT])
            + [RESIDENT] * 4,
            out_specs=([block_out] * 2 if from_frames else [RESIDENT] * 2) + [TOKEN_SPEC],
        ),
        out_shape=[shape, shape, TOKEN],
        compiler_params=params(16),
        cost_estimate=moved(chunks * units * half * features),
        name="section",
    )(place, before, mine, other, *weights)


def run_temporal(place, before, own, far, weights, chunk, count, last):
    _, cells, features = own[0].shape
    shape = (2, count, cells // 2, features)
    block_out = pl.BlockSpec(shape, lambda i, at: (0, 0, 0, 0))
    block_own = pl.BlockSpec((count, cells, features), lambda i, at: (chunk, 0, 0))
    kept = (jax.ShapeDtypeStruct if last else pltpu.HBM)(shape, jnp.bfloat16)
    return pl.pallas_call(
        functools.partial(temporal_kernel, 0 if last else chunk),
        grid_spec=pltpu.PrefetchScalarGridSpec(
            num_scalar_prefetch=1,
            grid=(1,),
            in_specs=[ANYWHERE] + [block_own if last else RESIDENT] * 4 + [RESIDENT] * 6,
            out_specs=[RESIDENT if last else block_out] * 4 + [TOKEN_SPEC],
        ),
        out_shape=[kept] * 4 + [TOKEN],
        compiler_params=params(24),
        cost_estimate=moved(count * cells * features),
        name="temporal",
    )(place, before, *own, *far, *weights)


GROUP = ("far", "cell")
RING = ("near", "sub")


def paired(frames, w_qkv, w_out, w_up, w_down, temporal_weight_first, temporal_weight_second):
    frames_local, cells, features = frames.shape
    near_size, subs = lax.axis_size("near"), lax.axis_size("sub")
    sub, side = lax.axis_index("sub"), lax.axis_index("far")
    quarter = 2 * side + lax.axis_index("cell")
    ring = near_size * subs
    position = lax.axis_index("near") * subs + sub
    place = jnp.stack([sub, side, position == 0, position == ring - 1, quarter]).astype(jnp.int32)
    rightward = [(i, (i + 1) % ring) for i in range(ring)]
    leftward = [(target, source) for source, target in rightward]
    slots = frames_local // DILATION_FIRST
    grouped = frames.reshape(slots, DILATION_FIRST, cells, features)
    pinned = pltpu.with_memory_space_constraint(grouped, pltpu.HBM)
    units = DILATION_FIRST // 4 // CHUNKS

    def exchange(piece, delta):
        return lax.ppermute(piece, GROUP, [(i, i ^ delta) for i in range(4)])

    def halo(even, odd):
        return [even, odd, lax.ppermute(odd, RING, rightward), lax.ppermute(even, RING, leftward)]

    halves = (w_qkv, w_out, w_up, w_down, temporal_weight_first, temporal_weight_second)
    beside, cuts = run_pack(place, pinned, units, CHUNKS)
    mine = pack_weights(cuts[0][0], halves, features)
    beside = exchange(beside, 1)
    crossed = [[exchange(piece, delta) for delta, piece in zip((2, 3), cut)] for cut in cuts]
    other = lax.ppermute(mine, "sub", [(0, 1), (1, 0)])
    weights = join_weights(place, mine, mine, other, halves)
    section_weights, temporal_weights = weights[:4], weights[4:]

    even, odd, before = run_section(
        place, place, pinned, beside, section_weights, units, CHUNKS, True
    )
    own = halo(even, odd)
    far, outs = [], []
    for kind, index in ORDER:
        if kind == "s":
            even, odd, before = run_section(
                place, before, *crossed[index], section_weights, units, 1, False
            )
            far.append(halo(even, odd))
        else:
            last = index == CHUNKS - 1
            if last:
                own = [pltpu.with_memory_space_constraint(field, pltpu.HBM) for field in own]
            *sent, before = run_temporal(
                place, before, own, far[index], temporal_weights, index, units, last
            )
            outs.append([sent[0]] + [exchange(sent[delta], delta) for delta in (1, 2, 3)])
    result = jnp.zeros_like(grouped)
    for index, received in enumerate(outs):
        for delta in range(4):
            at = (4 * index + (quarter ^ delta)) * units
            result = lax.dynamic_update_slice_in_dim(result, received[delta], at, axis=1)
    return result.reshape(frames.shape)


def solution(mesh):
    groups, tm, cell, sub = (mesh.shape[axis] for axis in ("groups", "tm", "cell", "sub"))

    def run(frames, *weights):
        frame_total, cells, _ = frames.shape
        video = frame_total // groups
        frames_local = video // (tm * sub)
        fits = (
            video == 2 * DILATION_SECOND
            and frames_local == 2 * DILATION_FIRST
            and tm % 2 == 0
            and cell == 2
            and sub == 2
            and (cells // cell) % 16 == 0
            and DILATION_FIRST % (4 * CHUNKS) == 0
        )
        if fits:
            devices = mesh.devices.reshape(groups, 2, tm // 2, cell, sub)
            axes = ("groups", "far", "near", "cell", "sub")
            used, split, body = jax.sharding.Mesh(devices, axes), ("groups", "far", "near", "sub"), paired
        else:
            used, split, body = mesh, ("groups", "tm", "sub"), general
        return jax.shard_map(
            body,
            mesh=used,
            in_specs=(P(split, "cell", None),) + (P("sub", None),) * 6,
            out_specs=P(split, "cell", None),
            check_vma=False,
        )(frames, *weights)

    return run
```

```python
import functools
import math

import jax
import jax.numpy as jnp
from jax import lax
from jax.experimental import pallas as pl
from jax.experimental.pallas import tpu as pltpu
from jax.sharding import PartitionSpec as P

HEAD_DIM = 64
DILATION_FIRST = 16
DILATION_SECOND = 256
CHUNKS = 2
ORDER = (("s", 0), ("s", 1), ("t", 0), ("t", 1))
MIB = 1024 * 1024


def with_halo(block, sides, width):
    for axis, dim in sides:
        count = lax.axis_size(axis)
        forward = [(i, i + 1) for i in range(count - 1)]
        backward = [(target, source) for source, target in forward]
        low = lax.ppermute(
            lax.slice_in_dim(block, block.shape[dim] - width, None, axis=dim), axis, forward
        )
        high = lax.ppermute(lax.slice_in_dim(block, 0, width, axis=dim), axis, backward)
        block = jnp.concatenate([low, block, high], axis=dim)
    return block


def shifted(shard, axis, by):
    size = lax.axis_size(axis)
    pairs = [(i, i + by) for i in range(size) if 0 <= i + by < size]
    return lax.ppermute(shard, axis, pairs)


def normalize(values):
    row_mean = jnp.mean(values, axis=-1, keepdims=True)
    centred = values - row_mean
    row_var = jnp.mean(centred * centred, axis=-1, keepdims=True)
    return centred * lax.rsqrt(row_var + 1e-05)


def attend(queries, key_part, value_part):
    frame_count, q_cells, features = queries.shape
    head_count = features // HEAD_DIM
    q_heads = queries.reshape(frame_count, q_cells, head_count, HEAD_DIM)
    k_heads = key_part.reshape(frame_count, -1, head_count, HEAD_DIM)
    v_heads = value_part.reshape(frame_count, -1, head_count, HEAD_DIM)
    scores = jnp.einsum(
        "fqhd,fkhd->fhqk", q_heads, k_heads, preferred_element_type=jnp.float32
    ) * HEAD_DIM ** (-0.5)
    row_max = jnp.max(scores, axis=-1, keepdims=True)
    exp_terms = jnp.exp(scores - row_max)
    attn_probs = (exp_terms / jnp.sum(exp_terms, axis=-1, keepdims=True)).astype(jnp.bfloat16)
    mixed = jnp.einsum("fhqk,fkhd->fqhd", attn_probs, v_heads, preferred_element_type=jnp.float32)
    return mixed.astype(jnp.bfloat16).reshape(frame_count, q_cells, features)


def gated_step(center, earlier, later_frames, weight):
    features = center.shape[-1]
    stacked = jnp.concatenate([earlier, center, later_frames], axis=-1).reshape(-1, 3 * features)
    preact = jnp.dot(stacked, weight, preferred_element_type=jnp.float32)
    gated_part = jnp.tanh(preact[:, :features]) * jax.nn.sigmoid(preact[:, features:])
    return (center.astype(jnp.float32) + gated_part.reshape(center.shape)).astype(jnp.bfloat16)


def general(frames, w_qkv, w_out, w_up, w_down, temporal_weight_first, temporal_weight_second):
    frames_local, cell_rows, features = frames.shape
    whole_qkv, whole_out, whole_up, whole_down, whole_tcn_a, whole_tcn_b = (
        lax.all_gather(w, "sub", axis=0, tiled=True)
        for w in (w_qkv, w_out, w_up, w_down, temporal_weight_first, temporal_weight_second)
    )
    working = lax.all_to_all(frames, "cell", split_axis=0, concat_axis=1, tiled=True)
    frame_count, cells_here = (working.shape[0], working.shape[1])
    residual = working.astype(jnp.float32)
    normed = normalize(residual).astype(jnp.bfloat16).reshape(-1, features)
    projected = jnp.dot(normed, whole_qkv, preferred_element_type=jnp.float32).astype(jnp.bfloat16)
    projected = projected.reshape(frame_count, cells_here, 3 * features)
    attended = attend(
        projected[..., :features],
        projected[..., features : 2 * features],
        projected[..., 2 * features :],
    )
    out_part = jnp.dot(
        attended.reshape(-1, features), whole_out, preferred_element_type=jnp.float32
    )
    mid_state = (residual + out_part.reshape(frame_count, cells_here, features)).astype(
        jnp.bfloat16
    )
    mid_float = lax.optimization_barrier(mid_state).astype(jnp.float32)
    normed_two = normalize(mid_float).astype(jnp.bfloat16).reshape(-1, features)
    hidden = jax.nn.gelu(jnp.dot(normed_two, whole_up, preferred_element_type=jnp.float32)).astype(
        jnp.bfloat16
    )
    down_part = jnp.dot(hidden, whole_down, preferred_element_type=jnp.float32).reshape(
        frame_count, cells_here, features
    )
    sectioned_frames = (mid_float + down_part).astype(jnp.bfloat16)
    sectioned_frames = lax.all_to_all(
        sectioned_frames, "cell", split_axis=1, concat_axis=0, tiled=True
    )
    padded_frames = with_halo(sectioned_frames, ((("tm", "sub"), 0),), DILATION_FIRST)
    earlier = padded_frames[:frames_local]
    later_frames = padded_frames[2 * DILATION_FIRST : 2 * DILATION_FIRST + frames_local]
    opening_layer = gated_step(sectioned_frames, earlier, later_frames, whole_tcn_a)
    shard_step_count = DILATION_SECOND // frames_local
    far_earlier = shifted(opening_layer, ("tm", "sub"), shard_step_count)
    far_later = shifted(opening_layer, ("tm", "sub"), -shard_step_count)
    return gated_step(opening_layer, far_earlier, far_later, whole_tcn_b)


ANYWHERE = pl.BlockSpec(memory_space=pl.ANY)
RESIDENT = pl.BlockSpec(memory_space=pltpu.VMEM)
SCALARS = pl.BlockSpec(memory_space=pltpu.SMEM)


TOKEN = jax.ShapeDtypeStruct((8, 128), jnp.float32)
TOKEN_SPEC = pl.BlockSpec((8, 128), lambda *at: (0, 0))


def params(mib):
    return pltpu.CompilerParams(vmem_limit_bytes=mib * MIB)


def moved(count):
    return pl.CostEstimate(flops=0, bytes_accessed=count, transcendentals=0)


def pack_weights_kernel(before, *refs):
    *sources, packed = refs
    width = packed.shape[1]
    at = 0
    for source in sources:
        rows = source.shape[0]
        for column in range(0, source.shape[1], width):
            packed[at : at + rows] = source[:, column : column + width]
            at += rows


def pack_weights(before, weights, width):
    rows = sum(w.size for w in weights) // width
    return pl.pallas_call(
        pack_weights_kernel,
        out_shape=jax.ShapeDtypeStruct((rows, width), weights[0].dtype),
        in_specs=[ANYWHERE] + [RESIDENT] * len(weights),
        out_specs=RESIDENT,
        compiler_params=params(8),
        cost_estimate=moved(rows * width),
        name="pack_weights",
    )(before, *weights)


def join_weights_kernel(place, before, mine, other, *wholes):
    width = mine.shape[1]
    for source, core in ((mine, place[0]), (other, 1 - place[0])):
        at = 0
        for whole in wholes:
            rows = whole.shape[0] // 2
            spot = pl.ds(pl.multiple_of(core * rows, 16), rows)
            for column in range(0, whole.shape[1], width):
                whole[spot, column : column + width] = source[at : at + rows]
                at += rows


def join_weights(place, before, mine, other, halves):
    return pl.pallas_call(
        join_weights_kernel,
        out_shape=[jax.ShapeDtypeStruct((2 * w.shape[0], w.shape[1]), w.dtype) for w in halves],
        in_specs=[SCALARS, ANYWHERE, RESIDENT, RESIDENT],
        out_specs=[RESIDENT] * len(halves),
        compiler_params=params(8),
        cost_estimate=moved(mine.size),
        name="join_weights",
    )(place, before, mine, other)


def pack_kernel(chunks, place, *refs):
    sources, (both, *cuts) = refs[: 3 * chunks], refs[3 * chunks :]
    units = sources[0].shape[1]
    for chunk in range(chunks):
        both[:, chunk * units : (chunk + 1) * units] = sources[chunk][...]
    for source, packed in zip(sources[chunks:], cuts):
        packed[...] = source[...]


def run_pack(place, grouped, units, chunks):
    slots, _, cells, features = grouped.shape
    shape = (slots, units, cells, features)
    wanted = [(delta, chunk) for chunk in range(chunks) for delta in (2, 3)]
    beside = [(1, chunk) for chunk in range(chunks)]

    def source(delta, chunk):
        return pl.BlockSpec(shape, lambda i, at: (0, 4 * chunk + (at[4] ^ delta), 0, 0))

    whole = (slots, chunks * units, cells, features)
    both, *cuts = pl.pallas_call(
        functools.partial(pack_kernel, chunks),
        grid_spec=pltpu.PrefetchScalarGridSpec(
            num_scalar_prefetch=1,
            grid=(1,),
            in_specs=[source(*piece) for piece in beside + wanted],
            out_specs=[RESIDENT] * (1 + len(wanted)),
        ),
        out_shape=[jax.ShapeDtypeStruct(whole, grouped.dtype)]
        + [jax.ShapeDtypeStruct(shape, grouped.dtype)] * len(wanted),
        compiler_params=params(8),
        cost_estimate=moved(grouped.size),
        name="pack",
    )(place, *[grouped] * len(beside + wanted))
    return both, [cuts[2 * chunk : 2 * chunk + 2] for chunk in range(chunks)]


def section_kernel(
    place,
    before,
    mine,
    other,
    w_qkv,
    w_out,
    w_up,
    w_down,
    even_ref,
    odd_ref,
    token,
):
    token[...] = jnp.zeros_like(token)
    slots, units, half, features = mine.shape
    cells = 2 * half
    parts = []
    for slot in range(slots):
        for unit in range(units):
            parts += [mine[slot, unit], other[slot, unit]]
    residual = jnp.concatenate(parts, axis=0).astype(jnp.float32)
    frame_count = slots * units
    normed = normalize(residual).astype(jnp.bfloat16)
    projected = jnp.dot(normed, w_qkv[...], preferred_element_type=jnp.float32).astype(jnp.bfloat16)
    pair_width = 2 * HEAD_DIM
    low = lax.broadcasted_iota(jnp.int32, (cells, pair_width), 1) < HEAD_DIM
    low_one = low.astype(jnp.bfloat16)
    high_one = 1 - low_one
    scale = HEAD_DIM ** (-0.5) * math.log2(math.e)
    rows = []
    for frame in range(frame_count):
        block = projected[frame * cells : (frame + 1) * cells]
        columns = []
        for pair in range(features // pair_width):
            at = pair * pair_width
            queries = block[:, at : at + pair_width]
            keys = block[:, features + at : features + at + pair_width]
            values = block[:, 2 * features + at : 2 * features + at + pair_width]
            split_keys = jnp.concatenate([keys * low_one, keys * high_one], axis=0)
            scores = lax.dot_general(
                queries, split_keys, (((1,), (1,)), ((), ())), preferred_element_type=jnp.float32
            )
            terms = []
            for head in range(2):
                own_scores = scores[:, head * cells : (head + 1) * cells]
                row_max = jnp.max(own_scores, axis=-1, keepdims=True)
                terms.append(jnp.exp2((own_scores - row_max) * scale).astype(jnp.bfloat16))
            split_values = jnp.concatenate(
                [
                    jnp.concatenate([values * low_one, low_one], axis=1),
                    jnp.concatenate([values * high_one, high_one], axis=1),
                ],
                axis=0,
            )
            mixed = jnp.dot(
                jnp.concatenate(terms, axis=1), split_values, preferred_element_type=jnp.float32
            )
            inverse = pl.reciprocal(mixed[:, pair_width:], approx=True)
            columns.append((mixed[:, :pair_width] * inverse).astype(jnp.bfloat16))
        rows.append(jnp.concatenate(columns, axis=1))
    attended = jnp.concatenate(rows, axis=0)

    mid_state = (
        residual + jnp.dot(attended, w_out[...], preferred_element_type=jnp.float32)
    ).astype(jnp.bfloat16)
    mid_float = mid_state.astype(jnp.float32)
    normed_two = normalize(mid_float).astype(jnp.bfloat16)
    total = mid_float
    width = math.gcd(w_up.shape[1], 768)
    for at in range(0, w_up.shape[1], width):
        lifted = jnp.dot(normed_two, w_up[:, at : at + width], preferred_element_type=jnp.float32)
        lifted = lifted.astype(jnp.bfloat16)
        inner = lifted * (
            math.sqrt(2 / math.pi) + (math.sqrt(2 / math.pi) * 0.044715) * (lifted * lifted)
        )
        halved = 0.5 * lifted
        hidden = halved + halved * jnp.tanh(inner)
        total = total + jnp.dot(hidden, w_down[at : at + width], preferred_element_type=jnp.float32)
    sectioned = total.astype(jnp.bfloat16)
    for unit in range(units):
        even_ref[unit] = sectioned[unit * cells : (unit + 1) * cells]
        odd_ref[unit] = sectioned[(units + unit) * cells : (units + unit + 1) * cells]


def gate(center, preact):
    features = center.shape[-1]
    preact = preact.astype(jnp.bfloat16)
    opened = 0.5 + 0.5 * jnp.tanh(0.5 * preact[:, features:])
    return center + jnp.tanh(preact[:, :features]) * opened


def temporal_unit(place, fields, w_first, w_second, outs, own_unit, far_unit):
    near, is_first, is_last = place[1], place[2], place[3]
    cells, features = fields[0].shape[1:]
    spans = [slice(own_unit, own_unit + 1)] * 4 + [slice(far_unit, far_unit + 1)] * 4
    units = 1
    flat = [field[at].reshape(units * cells, features) for field, at in zip(fields, spans)]
    zero = jnp.zeros_like(flat[0])
    pairs = [(flat[i], flat[i + 4]) for i in range(4)]
    even_n, odd_n, left_a, right_a = [jnp.where(near == 0, a, b) for a, b in pairs]
    even_f, odd_f, left_b, right_b = [jnp.where(near == 0, b, a) for a, b in pairs]
    left_n = jnp.where(is_first == 1, zero, left_a)
    left_f = jnp.where(is_first == 1, left_a, left_b)
    right_n = jnp.where(is_last == 1, right_b, right_a)
    right_f = jnp.where(is_last == 1, zero, right_b)
    center = jnp.concatenate([even_n, odd_n, even_f, odd_f], axis=0)
    stacked = jnp.concatenate(
        [
            jnp.concatenate([left_n, even_n, left_f, even_f], axis=0),
            center,
            jnp.concatenate([odd_n, right_n, odd_f, right_f], axis=0),
        ],
        axis=1,
    )
    opening = gate(center, jnp.dot(stacked, w_first[...], preferred_element_type=jnp.float32))
    rows = 2 * units * cells
    near_part, far_part = opening[:rows], opening[rows:]
    both = jnp.concatenate([near_part, far_part], axis=1)
    result_n = gate(
        near_part, jnp.dot(both, w_second[features:], preferred_element_type=jnp.float32)
    )
    result_f = gate(
        far_part, jnp.dot(both, w_second[: 2 * features], preferred_element_type=jnp.float32)
    )
    same = jnp.where(near == 0, result_n, result_f)
    other = jnp.where(near == 0, result_f, result_n)
    half = cells // 2
    for slot in range(2):
        at = slot * cells
        outs[0][slot, far_unit] = same[at : at + half]
        outs[1][slot, far_unit] = same[at + half : at + cells]
        outs[2][slot, far_unit] = other[at : at + half]
        outs[3][slot, far_unit] = other[at + half : at + cells]


def temporal_kernel(chunk, place, before, *refs):
    fields, (w_first, w_second, *outs, token) = refs[:8], refs[8:]
    token[...] = jnp.zeros_like(token)
    count = fields[4].shape[0]
    for unit in range(count):
        temporal_unit(place, fields, w_first, w_second, outs, chunk * count + unit, unit)


def run_section(place, before, mine, other, weights, units, chunks, from_frames):
    slots, _, half, features = mine.shape
    shape_in = (slots, units, half, features)
    piece = pl.BlockSpec(shape_in, lambda i, at: (0, i, 0, 0))
    own = pl.BlockSpec(shape_in, lambda i, at: (0, 4 * i + at[4], 0, 0))
    block_out = pl.BlockSpec((units, 2 * half, features), lambda i, at: (i, 0, 0))
    held = jax.ShapeDtypeStruct if from_frames else pltpu.VMEM
    shape = held((chunks * units, 2 * half, features), jnp.bfloat16)
    return pl.pallas_call(
        section_kernel,
        grid_spec=pltpu.PrefetchScalarGridSpec(
            num_scalar_prefetch=1,
            grid=(chunks,),
            in_specs=([ANYWHERE, own, piece] if from_frames else [ANYWHERE, RESIDENT, RESIDENT])
            + [RESIDENT] * 4,
            out_specs=([block_out] * 2 if from_frames else [RESIDENT] * 2) + [TOKEN_SPEC],
        ),
        out_shape=[shape, shape, TOKEN],
        compiler_params=params(16),
        cost_estimate=moved(chunks * units * half * features),
        name="section",
    )(place, before, mine, other, *weights)


def run_temporal(place, before, own, far, weights, chunk, count, last):
    _, cells, features = own[0].shape
    shape = (2, count, cells // 2, features)
    block_out = pl.BlockSpec(shape, lambda i, at: (0, 0, 0, 0))
    block_own = pl.BlockSpec((count, cells, features), lambda i, at: (chunk, 0, 0))
    kept = (jax.ShapeDtypeStruct if last else pltpu.HBM)(shape, jnp.bfloat16)
    return pl.pallas_call(
        functools.partial(temporal_kernel, 0 if last else chunk),
        grid_spec=pltpu.PrefetchScalarGridSpec(
            num_scalar_prefetch=1,
            grid=(1,),
            in_specs=[ANYWHERE] + [block_own if last else RESIDENT] * 4 + [RESIDENT] * 6,
            out_specs=[RESIDENT if last else block_out] * 4 + [TOKEN_SPEC],
        ),
        out_shape=[kept] * 4 + [TOKEN],
        compiler_params=params(24),
        cost_estimate=moved(count * cells * features),
        name="temporal",
    )(place, before, *own, *far, *weights)


GROUP = ("far", "cell")
RING = ("near", "sub")


def paired(frames, w_qkv, w_out, w_up, w_down, temporal_weight_first, temporal_weight_second):
    frames_local, cells, features = frames.shape
    near_size, subs = lax.axis_size("near"), lax.axis_size("sub")
    sub, side = lax.axis_index("sub"), lax.axis_index("far")
    quarter = 2 * side + lax.axis_index("cell")
    ring = near_size * subs
    position = lax.axis_index("near") * subs + sub
    place = jnp.stack([sub, side, position == 0, position == ring - 1, quarter]).astype(jnp.int32)
    rightward = [(i, (i + 1) % ring) for i in range(ring)]
    leftward = [(target, source) for source, target in rightward]
    slots = frames_local // DILATION_FIRST
    grouped = frames.reshape(slots, DILATION_FIRST, cells, features)
    pinned = pltpu.with_memory_space_constraint(grouped, pltpu.HBM)
    units = DILATION_FIRST // 4 // CHUNKS

    def exchange(piece, delta):
        return lax.ppermute(piece, GROUP, [(i, i ^ delta) for i in range(4)])

    def halo(even, odd):
        return [even, odd, lax.ppermute(odd, RING, rightward), lax.ppermute(even, RING, leftward)]

    halves = (w_qkv, w_out, w_up, w_down, temporal_weight_first, temporal_weight_second)
    beside, cuts = run_pack(place, pinned, units, CHUNKS)
    mine = pack_weights(cuts[0][0], halves, features)
    beside = exchange(beside, 1)
    crossed = [[exchange(piece, delta) for delta, piece in zip((2, 3), cut)] for cut in cuts]
    other = lax.ppermute(mine, "sub", [(0, 1), (1, 0)])
    weights = join_weights(place, mine, mine, other, halves)
    section_weights, temporal_weights = weights[:4], weights[4:]

    even, odd, before = run_section(
        place, place, pinned, beside, section_weights, units, CHUNKS, True
    )
    own = halo(even, odd)
    far, outs = [], []
    for kind, index in ORDER:
        if kind == "s":
            even, odd, before = run_section(
                place, before, *crossed[index], section_weights, units, 1, False
            )
            far.append(halo(even, odd))
        else:
            last = index == CHUNKS - 1
            if last:
                own = [pltpu.with_memory_space_constraint(field, pltpu.HBM) for field in own]
            *sent, before = run_temporal(
                place, before, own, far[index], temporal_weights, index, units, last
            )
            outs.append([sent[0]] + [exchange(sent[delta], delta) for delta in (1, 2, 3)])
    result = jnp.zeros_like(grouped)
    for index, received in enumerate(outs):
        for delta in range(4):
            at = (4 * index + (quarter ^ delta)) * units
            result = lax.dynamic_update_slice_in_dim(result, received[delta], at, axis=1)
    return result.reshape(frames.shape)


def solution(mesh):
    groups, tm, cell, sub = (mesh.shape[axis] for axis in ("groups", "tm", "cell", "sub"))

    def run(frames, *weights):
        frame_total, cells, _ = frames.shape
        video = frame_total // groups
        frames_local = video // (tm * sub)
        fits = (
            video == 2 * DILATION_SECOND
            and frames_local == 2 * DILATION_FIRST
            and tm % 2 == 0
            and cell == 2
            and sub == 2
            and (cells // cell) % 16 == 0
            and DILATION_FIRST % (4 * CHUNKS) == 0
        )
        if fits:
            devices = mesh.devices.reshape(groups, 2, tm // 2, cell, sub)
            axes = ("groups", "far", "near", "cell", "sub")
            used, split, body = jax.sharding.Mesh(devices, axes), ("groups", "far", "near", "sub"), paired
        else:
            used, split, body = mesh, ("groups", "tm", "sub"), general
        return jax.shard_map(
            body,
            mesh=used,
            in_specs=(P(split, "cell", None),) + (P("sub", None),) * 6,
            out_specs=P(split, "cell", None),
            check_vma=False,
        )(frames, *weights)

    return run
```
